32 devices in a mesh: section: 2 (over x), fsdp: 16 (over z, y, core).
Axes of the slice: x: 2, y: 2, z: 4, core: 2. Of those that a mesh axis runs over, the one named last changes fastest.
Arguments:
- section_input: bfloat16 [2, 4096, 4096], P('section', 'fsdp'), may hold values from -6 to 6
- segment_ids: int32 [2, 4096], P('section', 'fsdp'), may hold values from 0 to 2, never falling along the last dimension, each value on 1 to 3072 neighbouring positions
- query_weight: bfloat16 [2, 4096, 2048], P('section', 'fsdp'), as said below
- keyval_weight: bfloat16 [2, 4096, 512], P('section', 'fsdp'), as said below
- out_weight: bfloat16 [2, 2048, 4096], P('section', None, 'fsdp'), may hold values from -0.125 to 0.125
Outputs:
- passed: bfloat16 [2, 4096, 4096], P('section', 'fsdp')
The draws below stay inside these ranges and needn't reach their ends.
Inputs may be any that keep to these rules, and one draw needn't show every extreme that they name: `query_weight`: query projection weights. `keyval_weight`: key and value projection weights.
All inputs are finite; a program needn't handle non-finite values.
Results may differ from the reference program's by a relative error of at most 0.012.
The reference program's roundings to bfloat16 on the way count: a program that leaves them out, or rounds other values in their place, can miss the bound.
Values may be sent and summed in bfloat16 or wider, within the bound.
No kernel may reach another device: no remote copies, remote signals or barrier semaphores. Data moves between devices by JAX's collectives and lax.ppermute only.
A program may use at most 192 MiB of HBM per device.

```python
import math
import jax
import jax.numpy as jnp
import numpy as np
from jax import lax

MODEL_WIDTH = 4096
QUERY_HEADS = 32
KEY_HEADS = 4
HEAD_SIZE = 64
LOOKBACK_SPAN = 2048
SEQUENCE_TOKENS = 4096
N_SECTION = 2


def joint_weights(key):
    base_key = jax.random.fold_in(key, 11)
    first_key, following_key = jax.random.split(base_key)
    query_raw = jnp.clip(jax.random.normal(first_key, (N_SECTION, MODEL_WIDTH, QUERY_HEADS * HEAD_SIZE), jnp.float32), -6.0, 6.0)
    unprojected_key_value = jnp.clip(jax.random.normal(following_key, (N_SECTION, MODEL_WIDTH, 2 * KEY_HEADS * HEAD_SIZE), jnp.float32), -6.0, 6.0)
    query_slice = query_raw * (2.8 / math.sqrt(MODEL_WIDTH))
    key_value_slice = unprojected_key_value * (1.0 / math.sqrt(MODEL_WIDTH))
    return (query_slice, key_value_slice)


def draw_query_weight(key, part):
    return joint_weights(key)[0].astype(jnp.bfloat16)


def draw_keyval_weight(key, part):
    return joint_weights(key)[1].astype(jnp.bfloat16)


def steps_of(own_key, shape, shards, low, largest):
    level = 1.0
    for axis_at, parts in shards:
        heights = jax.random.uniform(jax.random.fold_in(jax.random.fold_in(own_key, 6), axis_at), (parts,), jnp.float32, low / len(shards), largest / len(shards))
        level = level * jnp.repeat(jnp.exp(heights), shape[axis_at] // parts).reshape((-1,) + (1,) * (len(shape) - 1 - axis_at))
    return level


def length_profile(amount, total, reach, skew):
    portions = [(1 << 20) // math.isqrt(standing ** skew) + 1 for standing in range(2, amount + 1)]
    spare, given = total - reach - (amount - 1), [1] * (amount - 1)
    while spare > 0:
        free = [i for i in range(amount - 1) if given[i] < reach]
        pool, left = sum([portions[i] for i in free]), spare
        for i in free:
            extra = min(reach - given[i], max(1, left * portions[i] // pool), spare)
            given[i] = given[i] + extra
            spare = spare - extra
    return np.array([reach] + given)


def uneven(own_key, count, total, reach, lean):
    if count == 2:
        one = jax.random.randint(own_key, (), max(1, total - reach), min(reach, total - 1) + 1)
        return jnp.stack([one, total - one])
    tallies = jnp.asarray(length_profile(count, total, reach, lean), jnp.int32)
    couples = (count - 1) // 2
    giver, receiver = tallies[1:1 + 2 * couples:2], tallies[2:2 + 2 * couples:2]
    slack = jnp.minimum(giver - 1, reach - receiver)
    passed = jax.random.randint(jax.random.fold_in(own_key, 1), (couples,), 0, 1 << 20) % (slack + 1)
    tallies = tallies.at[1:1 + 2 * couples:2].set(giver - passed).at[2:2 + 2 * couples:2].set(receiver + passed)
    return tallies[jax.random.permutation(jax.random.fold_in(own_key, 2), count)]


def centred(key, dims, width, limit, cuts=(), held_as=jnp.bfloat16):
    drawn = width * jax.random.normal(key, dims, jnp.float32)
    if cuts:
        drawn = drawn * steps_of(key, dims, cuts, -0.22, 0.18)
    return jnp.clip(drawn, -limit, limit).astype(held_as)


def setup_inputs(seed: int = 0) -> dict:
    keys = jax.random.split(jax.random.key(seed), 6)
    return {
        "section_input": centred(keys[0], (N_SECTION, SEQUENCE_TOKENS, MODEL_WIDTH), 1.0, 6.0, ((0, 2), (1, 16))),
        "segment_ids": jax.vmap(lambda own: jnp.searchsorted(jnp.cumsum(uneven(own, 3, SEQUENCE_TOKENS, 3 * SEQUENCE_TOKENS // 4, 0)), jnp.arange(SEQUENCE_TOKENS), side="right"))(jax.random.split(keys[1], N_SECTION)).reshape((N_SECTION, SEQUENCE_TOKENS)).astype(jnp.int32),
        "query_weight": draw_query_weight(jax.random.fold_in(keys[5], 71), 0),
        "keyval_weight": draw_keyval_weight(jax.random.fold_in(keys[5], 71), 0),
        "out_weight": centred(keys[4], (N_SECTION, QUERY_HEADS * HEAD_SIZE, MODEL_WIDTH), (QUERY_HEADS * HEAD_SIZE) ** -0.5, 0.125, ((0, 2), (2, 16))),
    }


def normed(values):
    widened = values.astype(jnp.float32)
    scaled = widened * lax.rsqrt(lax.optimization_barrier(jnp.mean(widened * widened, axis=-1, keepdims=True)) + 1e-05)
    return scaled.astype(jnp.bfloat16)

def apply_layer(hidden, segments, query_weight, keyval_weight, out_weight):
    queries_per_group = QUERY_HEADS // KEY_HEADS
    normal_rows = normed(hidden)
    query_rows = jnp.dot(normal_rows, query_weight, preferred_element_type=jnp.float32).astype(jnp.bfloat16)
    key_value_rows = jnp.dot(normal_rows, keyval_weight, preferred_element_type=jnp.float32).astype(jnp.bfloat16)
    key_lines = key_value_rows[:, :KEY_HEADS * HEAD_SIZE].reshape(SEQUENCE_TOKENS, KEY_HEADS, HEAD_SIZE)
    value_lines = key_value_rows[:, KEY_HEADS * HEAD_SIZE:].reshape(SEQUENCE_TOKENS, KEY_HEADS, HEAD_SIZE)
    padded_keys = jnp.concatenate([jnp.zeros((LOOKBACK_SPAN, KEY_HEADS, HEAD_SIZE), jnp.bfloat16), key_lines], axis=0)
    padded_values = jnp.concatenate([jnp.zeros((LOOKBACK_SPAN, KEY_HEADS, HEAD_SIZE), jnp.bfloat16), value_lines], axis=0)
    seg_int = segments.astype(jnp.int32)
    seg_padded = jnp.concatenate([jnp.full((LOOKBACK_SPAN,), -1, jnp.int32), seg_int], axis=0)
    rows_per_block = math.gcd(SEQUENCE_TOKENS, 512)
    key_span = LOOKBACK_SPAN + rows_per_block

    def attend(block_index):
        first_row = (block_index * rows_per_block).astype(jnp.int32)
        query_tile = lax.dynamic_slice_in_dim(query_rows, first_row, rows_per_block, 0)
        query_tile = query_tile.reshape(rows_per_block, KEY_HEADS, queries_per_group, HEAD_SIZE).astype(jnp.float32)
        key_block = lax.dynamic_slice_in_dim(padded_keys, first_row, key_span, 0).astype(jnp.float32)
        value_block = lax.dynamic_slice_in_dim(padded_values, first_row, key_span, 0).astype(jnp.float32)
        key_segs = lax.dynamic_slice_in_dim(seg_padded, first_row, key_span, 0)
        query_segs = lax.dynamic_slice_in_dim(seg_int, first_row, rows_per_block, 0)
        query_pos = first_row + jnp.arange(rows_per_block, dtype=jnp.int32)
        key_pos = first_row - LOOKBACK_SPAN + jnp.arange(key_span, dtype=jnp.int32)
        scores = jnp.einsum('qhgd,khd->hgqk', query_tile, key_block) * HEAD_SIZE ** (-0.5)
        visible = (query_segs[:, None] == key_segs[None, :]) & (key_pos[None, :] <= query_pos[:, None])
        visible = visible & (key_pos[None, :] > query_pos[:, None] - LOOKBACK_SPAN) & (key_pos[None, :] >= 0)
        scores = jnp.where(visible, scores, -1e+30)
        row_peak = lax.optimization_barrier(jnp.max(scores, axis=-1, keepdims=True))
        weights = jnp.where(visible, jnp.exp(scores - row_peak), 0.0)
        weight_sum = lax.optimization_barrier(jnp.sum(weights, axis=-1))
        rounded = lax.optimization_barrier(weights.astype(jnp.bfloat16)).astype(jnp.float32)
        mixed_heads = jnp.einsum('hgqk,khd->hgqd', rounded, value_block) / weight_sum[..., None]
        return jnp.transpose(mixed_heads, (2, 0, 1, 3)).reshape(rows_per_block, QUERY_HEADS * HEAD_SIZE).astype(jnp.bfloat16)
    attended = lax.map(attend, jnp.arange(SEQUENCE_TOKENS // rows_per_block, dtype=jnp.int32)).reshape(SEQUENCE_TOKENS, QUERY_HEADS * HEAD_SIZE)
    projected = jnp.dot(attended, out_weight, preferred_element_type=jnp.float32)
    return (hidden.astype(jnp.float32) + projected).astype(jnp.bfloat16)

def reference(section_input, segment_ids, query_weight, keyval_weight, out_weight):
    results = []
    for section_index in range(N_SECTION):
        results.append(apply_layer(section_input[section_index], segment_ids[section_index], query_weight[section_index], keyval_weight[section_index], out_weight[section_index]))
    stacked = jnp.stack(results)
    return jnp.roll(stacked, 1, axis=0)
```

```python
import functools

import jax
import jax.numpy as jnp
from jax import lax
from jax.experimental import pallas as pl
from jax.experimental.pallas import tpu as pltpu
from jax.sharding import PartitionSpec as P

QUERY_HEADS = 32
KEY_HEADS = 4
HEAD_SIZE = 64
LOOKBACK_SPAN = 2048
GROUP = QUERY_HEADS // KEY_HEADS
GROUP_WIDTH = GROUP * HEAD_SIZE
TILE = 256
MASKED = -1e30


def normed(values):
    widened = values.astype(jnp.float32)
    scaled = widened * lax.rsqrt(jnp.mean(widened * widened, axis=-1, keepdims=True) + 1e-05)
    return scaled.astype(jnp.bfloat16)


def ring_order(chips):
    return list(range(0, chips, 2)) + list(range(chips - 1, 0, -2))


def swap_cores(value):
    count = lax.axis_size("fsdp")
    return lax.ppermute(value, "fsdp", [(i, i ^ 1) for i in range(count)])


def along_ring(value, step):
    chips = lax.axis_size("fsdp") // 2
    order = ring_order(chips)
    pairs = []
    for place in range(chips):
        target = order[(place + step) % chips]
        pairs += [(2 * order[place] + core, 2 * target + core) for core in range(2)]
    return lax.ppermute(value, "fsdp", pairs)


def to_later_chip(value, steps):
    count = lax.axis_size("fsdp")
    return lax.ppermute(value, "fsdp", [(i, i + 2 * steps) for i in range(count - 2 * steps)])


def to_next_section(value, cross=False):
    sections, count = lax.axis_size("section"), lax.axis_size("fsdp")
    pairs = []
    for section in range(sections):
        for i in range(count):
            target = ((section + 1) % sections) * count + (i ^ 1 if cross else i)
            pairs.append((section * count + i, target))
    return lax.ppermute(value, ("section", "fsdp"), pairs)


def around(shard):
    chips = lax.axis_size("fsdp") // 2
    rows = shard.shape[0]
    ahead = behind = shard
    for step in range(1, (chips - 1) // 2 + 1):
        ahead, behind = along_ring(ahead, 1), along_ring(behind, -1)
        yield -step, 0, ahead
        yield step, 0, behind
    if chips % 2 == 0:
        half = rows // 2
        yield chips // 2, 0, along_ring(ahead[:half], 1)
        yield chips // 2, half, along_ring(behind[half:], -1)


def attention_kernel(lo_ref, q_ref, kt_ref, v_ref, out_ref, score_ref):
    tile = pl.program_id(0)
    start = pl.multiple_of(tile * TILE, TILE)
    span = LOOKBACK_SPAN + TILE
    lo = lo_ref[...] - start
    lane = lax.broadcasted_iota(jnp.int32, (TILE, 128), 1)
    row = lax.broadcasted_iota(jnp.int32, (TILE, 128), 0)
    blocks = span // TILE

    def scores_of(pair, parity):
        q = q_ref[:, pair * 128:(pair + 1) * 128]
        peak = jnp.full((TILE, 128), MASKED, jnp.float32)
        for block in range(blocks):
            first = pl.multiple_of(start + block * TILE, TILE)
            found = jnp.dot(q, kt_ref[parity, :, pl.ds(first, TILE)], preferred_element_type=jnp.float32)
            for part in range(TILE // 128):
                at = block * TILE + part * 128
                visible = lane + at >= lo
                if at >= LOOKBACK_SPAN:
                    visible = visible & (lane + (at - LOOKBACK_SPAN) <= row)
                kept = jnp.where(visible, found[:, part * 128:(part + 1) * 128], MASKED)
                peak = jnp.maximum(peak, kept)
                score_ref[parity, :, at:at + 128] = kept
        return jnp.max(peak, axis=1, keepdims=True)

    def mixed_of(parity, peak):
        total = jnp.zeros((TILE, 128), jnp.float32)
        mixed = jnp.zeros((TILE, 128), jnp.float32)
        for block in range(blocks):
            first = pl.multiple_of(start + block * TILE, TILE)
            weights = jnp.exp(score_ref[parity, :, block * TILE:(block + 1) * TILE] - peak)
            for part in range(TILE // 128):
                total = total + weights[:, part * 128:(part + 1) * 128]
            mixed = mixed + jnp.dot(
                weights.astype(jnp.bfloat16), v_ref[parity, pl.ds(first, TILE), :],
                preferred_element_type=jnp.float32,
            )
        return mixed * (1.0 / jnp.sum(total, axis=1, keepdims=True))

    pairs = q_ref.shape[1] // 128
    for pair in range(pairs):
        peaks = [scores_of(pair, parity) for parity in range(2)]
        parts = [mixed_of(parity, peaks[parity]) for parity in range(2)]
        out_ref[:, pair * 128:(pair + 1) * 128] = (parts[0] + parts[1]).astype(out_ref.dtype)


def attention(lo, queries, keys_t, values):
    rows = queries.shape[0]
    window = keys_t.shape[2]
    span = LOOKBACK_SPAN + TILE
    flops = 4 * rows * span * GROUP * 128
    return pl.pallas_call(
        attention_kernel,
        grid=(rows // TILE,),
        in_specs=[
            pl.BlockSpec((TILE, 128), lambda t: (t, 0)),
            pl.BlockSpec((TILE, GROUP_WIDTH), lambda t: (t, 0)),
            pl.BlockSpec((2, 128, window), lambda t: (0, 0, 0)),
            pl.BlockSpec((2, window, 128), lambda t: (0, 0, 0)),
        ],
        out_specs=pl.BlockSpec((TILE, GROUP_WIDTH), lambda t: (t, 0)),
        out_shape=jax.ShapeDtypeStruct((rows, GROUP_WIDTH), jnp.bfloat16),
        scratch_shapes=[pltpu.VMEM((2, TILE, span), jnp.float32)],
        compiler_params=pltpu.CompilerParams(vmem_limit_bytes=40 * 1024 * 1024),
        cost_estimate=pl.CostEstimate(flops=flops, bytes_accessed=4 * 1024 * 1024, transcendentals=rows * span * GROUP),
    )(lo, queries, keys_t, values)


def body(section_input, segment_ids, query_weight, keyval_weight, out_weight):
    hidden, segments = section_input[0], segment_ids[0]
    rows, width = hidden.shape
    device = lax.axis_index("fsdp")
    chips = lax.axis_size("fsdp") // 2
    chip, core = device // 2, device % 2
    order = ring_order(chips)
    place = jnp.array([order.index(i) for i in range(chips)], jnp.int32)[chip]

    def source(distance):
        return jnp.array(order, jnp.int32)[(place + distance) % chips]

    def in_order(own, other):
        first = jnp.where(core == 0, own, other)
        return jnp.concatenate([first, jnp.where(core == 0, other, own)], axis=0)

    def half(weight, keep):
        parts = weight.reshape(rows, -1, 2, weight.shape[1] // KEY_HEADS if weight.shape[1] > 512 else HEAD_SIZE)
        return lax.dynamic_index_in_dim(parts, core if keep else 1 - core, 2, keepdims=False)

    key_own, key_sent = half(keyval_weight[0], True), half(keyval_weight[0], False)
    query_own, query_sent = half(query_weight[0], True), half(query_weight[0], False)
    key_shard = in_order(key_own.reshape(rows, -1), swap_cores(key_sent.reshape(rows, -1)))
    query_shards = [in_order(query_own[:, g], swap_cores(query_sent[:, g])) for g in range(2)]

    normal_rows = normed(hidden)
    chip_rows = in_order(normal_rows, swap_cores(normal_rows))
    chip_segments = in_order(segments, swap_cores(segments))

    out_shard = to_next_section(out_weight[0])
    hidden_before = to_next_section(hidden)

    def projected(shard):
        depth = shard.shape[0]
        total = jnp.zeros((2 * rows, shard.shape[1]), jnp.float32)
        for distance, first, part in [(0, 0, shard)] + list(around(shard)):
            columns = lax.dynamic_slice(
                chip_rows, (0, source(distance) * depth + first), (2 * rows, part.shape[0])
            )
            total = total + jnp.dot(columns, part, preferred_element_type=jnp.float32)
        return total.astype(jnp.bfloat16)

    keyvals = projected(key_shard)
    marks = jnp.zeros((16, keyvals.shape[1]), jnp.bfloat16)
    marks = marks.at[: 2 * rows // keyvals.shape[1]].set(
        (chip_segments + 1).astype(jnp.bfloat16).reshape(-1, keyvals.shape[1])
    )
    parcel = jnp.concatenate([keyvals, marks], axis=0)
    lookback = -(-LOOKBACK_SPAN // (2 * rows))
    parcels = [to_later_chip(parcel, steps) for steps in range(lookback, 0, -1)] + [parcel]
    window = jnp.concatenate([item[: 2 * rows] for item in parcels], axis=0)
    window_marks = jnp.concatenate(
        [item[2 * rows:].reshape(-1)[: 2 * rows].astype(jnp.int32) for item in parcels]
    )
    own_marks = window_marks[-2 * rows:]
    earlier = jnp.sum((window_marks[None, :] < own_marks[:, None]).astype(jnp.int32), axis=1)
    lowest = jnp.maximum(earlier, jnp.arange(1, 2 * rows + 1, dtype=jnp.int32))
    lowest = jnp.broadcast_to(lowest[:, None], (2 * rows, 128))

    queries = [
        projected(shard) * jnp.bfloat16(HEAD_SIZE ** -0.5) for shard in query_shards
    ]

    arrived = [[], []]
    out_halves = [out_shard[: out_shard.shape[0] // 2], out_shard[out_shard.shape[0] // 2:]]
    out_full = []
    for g in range(2):
        depth, columns = out_halves[g].shape
        full = jnp.zeros((depth, width), jnp.bfloat16)
        for distance, first, part in [(0, 0, out_halves[g])] + list(around(out_halves[g])):
            other = swap_cores(part)
            at = source(distance) * 2
            full = lax.dynamic_update_slice(full, part, (first, (at + core) * columns))
            full = lax.dynamic_update_slice(full, other, (first, (at + 1 - core) * columns))
        out_full.append(full)

    total = hidden_before.astype(jnp.float32)
    for g in range(2):
        keys = window[:, g * HEAD_SIZE:(g + 1) * HEAD_SIZE]
        values = window[:, (2 + g) * HEAD_SIZE:(3 + g) * HEAD_SIZE]
        blank = jnp.zeros_like(keys)
        keys_t = jnp.stack(
            [jnp.concatenate([keys, blank], axis=1).T, jnp.concatenate([blank, keys], axis=1).T]
        )
        wide = jnp.stack(
            [jnp.concatenate([values, blank], axis=1), jnp.concatenate([blank, values], axis=1)]
        )
        attended = attention(lowest, queries[g], keys_t, wide)
        attended = attended.reshape(2, rows, GROUP_WIDTH)
        same = to_next_section(lax.dynamic_index_in_dim(attended, core, 0, keepdims=False))
        cross = to_next_section(lax.dynamic_index_in_dim(attended, 1 - core, 0, keepdims=False), cross=True)
        mine = jnp.concatenate(
            [jnp.where(core == 0, same, cross), jnp.where(core == 0, cross, same)], axis=1
        )
        total = total + jnp.dot(mine, out_full[g], preferred_element_type=jnp.float32)
    return total.astype(jnp.bfloat16)[None]


def solution(mesh):
    return jax.shard_map(
        body,
        mesh=mesh,
        in_specs=(
            P("section", "fsdp", None),
            P("section", "fsdp"),
            P("section", "fsdp", None),
            P("section", "fsdp", None),
            P("section", None, "fsdp"),
        ),
        out_specs=P("section", "fsdp", None),
        check_vma=False,
    )
```

```python
import functools

import jax
import jax.numpy as jnp
from jax import lax
from jax.experimental import pallas as pl
from jax.experimental.pallas import tpu as pltpu
from jax.sharding import PartitionSpec as P

QUERY_HEADS = 32
KEY_HEADS = 4
HEAD_SIZE = 64
LOOKBACK_SPAN = 2048
GROUP = QUERY_HEADS // KEY_HEADS
GROUP_WIDTH = GROUP * HEAD_SIZE
TILE = 256
MASKED = -1e30


def normed(values):
    widened = values.astype(jnp.float32)
    scaled = widened * lax.rsqrt(jnp.mean(widened * widened, axis=-1, keepdims=True) + 1e-05)
    return scaled.astype(jnp.bfloat16)


def ring_order(chips):
    return list(range(0, chips, 2)) + list(range(chips - 1, 0, -2))


def swap_cores(value):
    count = lax.axis_size("fsdp")
    return lax.ppermute(value, "fsdp", [(i, i ^ 1) for i in range(count)])


def along_ring(value, step):
    chips = lax.axis_size("fsdp") // 2
    order = ring_order(chips)
    pairs = []
    for place in range(chips):
        target = order[(place + step) % chips]
        pairs += [(2 * order[place] + core, 2 * target + core) for core in range(2)]
    return lax.ppermute(value, "fsdp", pairs)


def swap_chips(value):
    count = lax.axis_size("fsdp")
    return lax.ppermute(value, "fsdp", [(i, i ^ 2) for i in range(count)])


def two_chips_on(value):
    count = lax.axis_size("fsdp")
    return lax.ppermute(value, "fsdp", [(i, i + 4) for i in range(count - 4)])


def to_next_section(value):
    count = lax.axis_size("section")
    return lax.ppermute(value, "section", [(i, (i + 1) % count) for i in range(count)])


def around(shard, longer):
    chips = lax.axis_size("fsdp") // 2
    found, moving = {0: shard}, {1: shard, -1: shard}
    for step in range(1, chips // 2 + 1):
        for way in (1, -1):
            if 2 * step < chips or way == longer:
                moving[way] = along_ring(moving[way], way)
                found[-way * step % chips] = moving[way]
    return found


def tied_kernel(value_ref, other_ref, out_ref):
    pass


def after(value, other):
    anywhere = pl.BlockSpec(memory_space=pl.ANY)
    return pl.pallas_call(
        tied_kernel,
        in_specs=[anywhere, anywhere],
        out_specs=anywhere,
        out_shape=jax.ShapeDtypeStruct(value.shape, value.dtype),
        input_output_aliases={0: 0},
    )(value, other)


def out_kernel(count, at_ref, rows_ref, add_ref, *refs):
    weights, out_ref = refs[: 2 * count], refs[-1]
    depth = weights[0].shape[0]
    out_ref[...] = refs[2 * count][...]
    for i in range(count):
        columns = weights[i].shape[1]
        at = pl.ds(pl.multiple_of(at_ref[i] * columns, columns), columns)
        total = add_ref[:, at].astype(jnp.float32)
        for part in range(2):
            total = total + jnp.dot(
                rows_ref[:, part * depth:(part + 1) * depth], weights[part * count + i][...],
                preferred_element_type=jnp.float32,
            )
        out_ref[:, at] = total.astype(out_ref.dtype)


def out_columns(rows, add, before, first, second, at):
    count = len(first)
    whole = pl.BlockSpec(memory_space=pltpu.VMEM)
    flops = 2 * rows.shape[0] * rows.shape[1] * count * first[0].shape[1]
    return pl.pallas_call(
        functools.partial(out_kernel, count),
        in_specs=[pl.BlockSpec(memory_space=pltpu.SMEM)] + [whole] * (3 + 2 * count),
        out_specs=whole,
        out_shape=jax.ShapeDtypeStruct(before.shape, before.dtype),
        input_output_aliases={3 + 2 * count: 0},
        compiler_params=pltpu.CompilerParams(vmem_limit_bytes=40 * 1024 * 1024),
        cost_estimate=pl.CostEstimate(flops=flops, bytes_accessed=8 * 1024 * 1024, transcendentals=0),
    )(at, rows, add, *first, *second, before)


def attention_kernel(lo_ref, q_ref, kt_ref, v_ref, out_ref, score_ref):
    tile = pl.program_id(0)
    start = pl.multiple_of(tile * TILE, TILE)
    span = LOOKBACK_SPAN + TILE
    lo = lo_ref[...] - start
    lane = lax.broadcasted_iota(jnp.int32, (TILE, 128), 1)
    row = lax.broadcasted_iota(jnp.int32, (TILE, 128), 0)
    blocks = span // TILE

    def scores_of(pair, parity):
        q = q_ref[:, pair * 128:(pair + 1) * 128]
        peak = jnp.full((TILE, 128), MASKED, jnp.float32)
        for block in range(blocks):
            first = pl.multiple_of(start + block * TILE, TILE)
            found = jnp.dot(q, kt_ref[parity, :, pl.ds(first, TILE)], preferred_element_type=jnp.float32)
            for part in range(TILE // 128):
                at = block * TILE + part * 128
                visible = lane + at >= lo
                if at >= LOOKBACK_SPAN:
                    visible = visible & (lane + (at - LOOKBACK_SPAN) <= row)
                kept = jnp.where(visible, found[:, part * 128:(part + 1) * 128], MASKED)
                peak = jnp.maximum(peak, kept)
                score_ref[parity, :, at:at + 128] = kept
        return jnp.max(peak, axis=1, keepdims=True)

    def mixed_of(parity, peak):
        total = jnp.zeros((TILE, 128), jnp.float32)
        mixed = jnp.zeros((TILE, 128), jnp.float32)
        for block in range(blocks):
            first = pl.multiple_of(start + block * TILE, TILE)
            weights = jnp.exp(score_ref[parity, :, block * TILE:(block + 1) * TILE] - peak)
            for part in range(TILE // 128):
                total = total + weights[:, part * 128:(part + 1) * 128]
            mixed = mixed + jnp.dot(
                weights.astype(jnp.bfloat16), v_ref[parity, pl.ds(first, TILE), :],
                preferred_element_type=jnp.float32,
            )
        return mixed * (1.0 / jnp.sum(total, axis=1, keepdims=True))

    pairs = q_ref.shape[1] // 128
    for pair in range(pairs):
        peaks = [scores_of(pair, parity) for parity in range(2)]
        parts = [mixed_of(parity, peaks[parity]) for parity in range(2)]
        out_ref[:, pair * 128:(pair + 1) * 128] = (parts[0] + parts[1]).astype(out_ref.dtype)


def attention(lo, queries, keys_t, values):
    rows = queries.shape[0]
    window = keys_t.shape[2]
    span = LOOKBACK_SPAN + TILE
    flops = 4 * rows * span * GROUP * 128
    return pl.pallas_call(
        attention_kernel,
        grid=(rows // TILE,),
        in_specs=[
            pl.BlockSpec((TILE, 128), lambda t: (t, 0)),
            pl.BlockSpec((TILE, GROUP_WIDTH), lambda t: (t, 0)),
            pl.BlockSpec((2, 128, window), lambda t: (0, 0, 0)),
            pl.BlockSpec((2, window, 128), lambda t: (0, 0, 0)),
        ],
        out_specs=pl.BlockSpec((TILE, GROUP_WIDTH), lambda t: (t, 0)),
        out_shape=jax.ShapeDtypeStruct((rows, GROUP_WIDTH), jnp.bfloat16),
        scratch_shapes=[pltpu.VMEM((2, TILE, span), jnp.float32)],
        compiler_params=pltpu.CompilerParams(vmem_limit_bytes=40 * 1024 * 1024),
        cost_estimate=pl.CostEstimate(flops=flops, bytes_accessed=4 * 1024 * 1024, transcendentals=rows * span * GROUP),
    )(lo, queries, keys_t, values)


def body(section_input, segment_ids, query_weight, keyval_weight, out_weight):
    hidden, segments = section_input[0], segment_ids[0]
    rows, width = hidden.shape
    device = lax.axis_index("fsdp")
    chips = lax.axis_size("fsdp") // 2
    chip, core = device // 2, device % 2
    order = jnp.array(ring_order(chips), jnp.int32)
    place = jnp.argmax(order == chip)

    def source(distance):
        return order[(place + distance) % chips]

    def in_order(own, other, axis=0):
        first = jnp.where(core == 0, own, other)
        return jnp.concatenate([first, jnp.where(core == 0, other, own)], axis=axis)

    def own_features(value):
        parts = value.reshape(rows, chips, 2, -1)
        kept = lax.dynamic_index_in_dim(parts, core, 2, keepdims=False).reshape(rows, -1)
        sent = lax.dynamic_index_in_dim(parts, 1 - core, 2, keepdims=False).reshape(rows, -1)
        return in_order(kept, swap_cores(sent))

    keyval_shards = around(keyval_weight[0], 1)
    per_half = query_weight.shape[2] // 2
    query_shards = [
        around(query_weight[0][:, g * per_half:(g + 1) * per_half], 1 - 2 * g) for g in range(2)
    ]
    out_shard = to_next_section(out_weight[0])
    chip_rows = own_features(normed(hidden))
    hidden_before = own_features(to_next_section(hidden))

    def projected(shards):
        total = None
        for distance, shard in shards.items():
            depth = shard.shape[0]
            columns = lax.dynamic_slice(chip_rows, (0, source(distance) * depth), (2 * rows, depth))
            found = jnp.dot(columns, shard, preferred_element_type=jnp.float32)
            total = found if total is None else total + found
        return total

    def of_core(value, which):
        parts = value.reshape(2 * rows, -1, 2, HEAD_SIZE)
        return lax.dynamic_index_in_dim(parts, which, 2, keepdims=False).reshape(2 * rows, -1)

    partial = projected(keyval_shards)
    marks = jnp.zeros((8, rows), jnp.float32).at[0].set((segments + 1).astype(jnp.float32))
    received = swap_cores(jnp.concatenate([of_core(partial, 1 - core), marks], axis=0))
    keyvals = (of_core(partial, core) + received[: 2 * rows]).astype(jnp.bfloat16)
    chip_marks = in_order(marks[:1], received[2 * rows:2 * rows + 1]).astype(jnp.bfloat16)
    chip_marks = jnp.concatenate([chip_marks, jnp.zeros((14, rows), jnp.bfloat16)], axis=0)
    parcel = jnp.concatenate([keyvals, chip_marks], axis=0)
    back_two = two_chips_on(parcel)
    back_four = two_chips_on(back_two)
    even = chip % 2 == 0
    swapped = swap_chips(jnp.concatenate([jnp.where(even, parcel, back_four), back_two], axis=0))
    length = parcel.shape[0]
    crossed = [swapped[:length], swapped[length:]]
    parcels = [
        back_four, jnp.where(even, crossed[0], crossed[1]), back_two, jnp.where(even, crossed[1], crossed[0]), parcel
    ]
    window = jnp.concatenate([item[: 2 * rows] for item in parcels], axis=0)
    window_marks = jnp.concatenate([item[2 * rows:2 * rows + 2].reshape(-1) for item in parcels]).astype(jnp.int32)
    own_marks = window_marks[-2 * rows:]
    earlier = jnp.sum((window_marks[None, :] < own_marks[:, None]).astype(jnp.int32), axis=1)
    lowest = jnp.maximum(earlier, jnp.arange(1, 2 * rows + 1, dtype=jnp.int32))
    lowest = jnp.broadcast_to(lowest[:, None], (2 * rows, 128))

    half = out_shard.shape[0] // 2
    out_shards = [
        around(after(out_shard[g * half:(g + 1) * half], query_shards[g][(1 - 2 * g) * 3 % chips]), 1 - 2 * g)
        for g in range(2)
    ]

    attended_rows = []
    for g in range(2):
        partial = projected(query_shards[g])
        kept = lax.dynamic_slice(partial, (0, core * GROUP_WIDTH), (2 * rows, GROUP_WIDTH))
        sent = lax.dynamic_slice(partial, (0, (1 - core) * GROUP_WIDTH), (2 * rows, GROUP_WIDTH))
        queries = (kept + swap_cores(sent)).astype(jnp.bfloat16) * jnp.bfloat16(HEAD_SIZE ** -0.5)
        keys = window[:, g * HEAD_SIZE:(g + 1) * HEAD_SIZE]
        values = window[:, (2 + g) * HEAD_SIZE:(3 + g) * HEAD_SIZE]
        blank = jnp.zeros_like(keys)
        keys_t = jnp.stack(
            [jnp.concatenate([keys, blank], axis=1).T, jnp.concatenate([blank, keys], axis=1).T]
        )
        wide = jnp.stack(
            [jnp.concatenate([values, blank], axis=1), jnp.concatenate([blank, values], axis=1)]
        )
        attended = to_next_section(attention(lowest, queries, keys_t, wide))
        attended_rows.append(in_order(attended, swap_cores(attended), axis=1))
    attended_rows = jnp.concatenate(attended_rows, axis=1)

    made = jnp.zeros((2 * rows, width // 2), jnp.bfloat16)
    distances = sorted(out_shards[0], key=lambda d: min(d, chips - d))
    for some in (distances[:5], distances[5:7], distances[7:]):
        at = jnp.stack([source(distance) for distance in some])
        made = out_columns(
            attended_rows, hidden_before, made,
            [out_shards[0][d] for d in some], [out_shards[1][d] for d in some], at,
        )
    kept = lax.dynamic_slice(made, (core * rows, 0), (rows, width // 2)).reshape(rows, chips, 1, -1)
    sent = lax.dynamic_slice(made, ((1 - core) * rows, 0), (rows, width // 2))
    other = swap_cores(sent).reshape(rows, chips, 1, -1)
    return in_order(kept, other, axis=2).reshape(1, rows, width)


def solution(mesh):
    return jax.shard_map(
        body,
        mesh=mesh,
        in_specs=(
            P("section", "fsdp", None),
            P("section", "fsdp"),
            P("section", "fsdp", None),
            P("section", "fsdp", None),
            P("section", None, "fsdp"),
        ),
        out_specs=P("section", "fsdp", None),
        check_vma=False,
    )
```

```python
import jax
import jax.numpy as jnp
from jax import lax
from jax.experimental import pallas as pl
from jax.experimental.pallas import tpu as pltpu
from jax.sharding import PartitionSpec as P

QUERY_HEADS = 32
KEY_HEADS = 4
HEAD_SIZE = 64
LOOKBACK_SPAN = 2048
GROUP = QUERY_HEADS // KEY_HEADS
GROUP_WIDTH = GROUP * HEAD_SIZE
TILE = 256
MASKED = -1e30


def normed(values):
    widened = values.astype(jnp.float32)
    scaled = widened * lax.rsqrt(jnp.mean(widened * widened, axis=-1, keepdims=True) + 1e-05)
    return scaled.astype(jnp.bfloat16)


def swap_cores(value):
    count = lax.axis_size("fsdp")
    return lax.ppermute(value, "fsdp", [(i, i ^ 1) for i in range(count)])


def gathered(value):
    count = lax.axis_size("fsdp")
    groups = [list(range(core, count, 2)) for core in range(2)]
    return lax.all_gather(value, "fsdp", axis=0, tiled=False, axis_index_groups=groups)


def swap_chips(value):
    count = lax.axis_size("fsdp")
    return lax.ppermute(value, "fsdp", [(i, i ^ 2) for i in range(count)])


def two_chips_on(value):
    count = lax.axis_size("fsdp")
    return lax.ppermute(value, "fsdp", [(i, i + 4) for i in range(count - 4)])


def to_next_section(value):
    count = lax.axis_size("section")
    return lax.ppermute(value, "section", [(i, (i + 1) % count) for i in range(count)])


def out_kernel(rows_ref, weight_ref, add_ref, out_ref):
    total = add_ref[...].astype(jnp.float32) + jnp.dot(
        rows_ref[...], weight_ref[0], preferred_element_type=jnp.float32
    )
    out_ref[...] = total.astype(out_ref.dtype)


def out_columns(rows, weights, add):
    chips, depth, columns = weights.shape
    count = rows.shape[0]
    return pl.pallas_call(
        out_kernel,
        grid=(chips,),
        in_specs=[
            pl.BlockSpec((count, depth), lambda i: (0, 0)),
            pl.BlockSpec((1, depth, columns), lambda i: (i, 0, 0)),
            pl.BlockSpec((count, columns), lambda i: (0, i)),
        ],
        out_specs=pl.BlockSpec((count, columns), lambda i: (0, i)),
        out_shape=jax.ShapeDtypeStruct(add.shape, add.dtype),
        compiler_params=pltpu.CompilerParams(vmem_limit_bytes=40 * 1024 * 1024),
        cost_estimate=pl.CostEstimate(
            flops=2 * count * depth * chips * columns, bytes_accessed=12 * 1024 * 1024, transcendentals=0
        ),
    )(rows, weights, add)


def attention_kernel(lo_ref, q_ref, kt_ref, v_ref, out_ref, score_ref):
    tile = pl.program_id(0)
    start = pl.multiple_of(tile * TILE, TILE)
    span = LOOKBACK_SPAN + TILE
    lo = lo_ref[...] - start
    lane = lax.broadcasted_iota(jnp.int32, (TILE, 128), 1)
    row = lax.broadcasted_iota(jnp.int32, (TILE, 128), 0)
    blocks = span // TILE

    def scores_of(pair, parity):
        q = q_ref[:, pair * 128:(pair + 1) * 128]
        peak = jnp.full((TILE, 128), MASKED, jnp.float32)
        for block in range(blocks):
            first = pl.multiple_of(start + block * TILE, TILE)
            found = jnp.dot(q, kt_ref[parity, :, pl.ds(first, TILE)], preferred_element_type=jnp.float32)
            for part in range(TILE // 128):
                at = block * TILE + part * 128
                visible = lane + at >= lo
                if at >= LOOKBACK_SPAN:
                    visible = visible & (lane + (at - LOOKBACK_SPAN) <= row)
                kept = jnp.where(visible, found[:, part * 128:(part + 1) * 128], MASKED)
                peak = jnp.maximum(peak, kept)
                score_ref[parity, :, at:at + 128] = kept
        return jnp.max(peak, axis=1, keepdims=True)

    def mixed_of(parity, peak):
        total = jnp.zeros((TILE, 128), jnp.float32)
        mixed = jnp.zeros((TILE, 128), jnp.float32)
        for block in range(blocks):
            first = pl.multiple_of(start + block * TILE, TILE)
            weights = jnp.exp(score_ref[parity, :, block * TILE:(block + 1) * TILE] - peak)
            for part in range(TILE // 128):
                total = total + weights[:, part * 128:(part + 1) * 128]
            mixed = mixed + jnp.dot(
                weights.astype(jnp.bfloat16), v_ref[parity, pl.ds(first, TILE), :],
                preferred_element_type=jnp.float32,
            )
        return mixed * (1.0 / jnp.sum(total, axis=1, keepdims=True))

    pairs = q_ref.shape[1] // 128
    for pair in range(pairs):
        peaks = [scores_of(pair, parity) for parity in range(2)]
        parts = [mixed_of(parity, peaks[parity]) for parity in range(2)]
        out_ref[:, pair * 128:(pair + 1) * 128] = (parts[0] + parts[1]).astype(out_ref.dtype)


def attention(lo, queries, keys_t, values):
    rows = queries.shape[0]
    window = keys_t.shape[2]
    span = LOOKBACK_SPAN + TILE
    flops = 4 * rows * span * GROUP * 128
    return pl.pallas_call(
        attention_kernel,
        grid=(rows // TILE,),
        in_specs=[
            pl.BlockSpec((TILE, 128), lambda t: (t, 0)),
            pl.BlockSpec((TILE, GROUP_WIDTH), lambda t: (t, 0)),
            pl.BlockSpec((2, 128, window), lambda t: (0, 0, 0)),
            pl.BlockSpec((2, window, 128), lambda t: (0, 0, 0)),
        ],
        out_specs=pl.BlockSpec((TILE, GROUP_WIDTH), lambda t: (t, 0)),
        out_shape=jax.ShapeDtypeStruct((rows, GROUP_WIDTH), jnp.bfloat16),
        scratch_shapes=[pltpu.VMEM((2, TILE, span), jnp.float32)],
        compiler_params=pltpu.CompilerParams(vmem_limit_bytes=40 * 1024 * 1024),
        cost_estimate=pl.CostEstimate(flops=flops, bytes_accessed=4 * 1024 * 1024, transcendentals=rows * span * GROUP),
    )(lo, queries, keys_t, values)


def body(section_input, segment_ids, query_weight, keyval_weight, out_weight):
    hidden, segments = section_input[0], segment_ids[0]
    rows, width = hidden.shape
    device = lax.axis_index("fsdp")
    chips = lax.axis_size("fsdp") // 2
    chip, core = device // 2, device % 2

    def in_order(own, other, axis=0):
        first = jnp.where(core == 0, own, other)
        return jnp.concatenate([first, jnp.where(core == 0, other, own)], axis=axis)

    def own_features(value):
        parts = value.reshape(rows, chips, 2, -1)
        kept = lax.dynamic_index_in_dim(parts, core, 2, keepdims=False).reshape(rows, -1)
        sent = lax.dynamic_index_in_dim(parts, 1 - core, 2, keepdims=False).reshape(rows, -1)
        return in_order(kept, swap_cores(sent))

    weights = gathered(jnp.concatenate([keyval_weight[0], query_weight[0]], axis=1))
    weights = weights.reshape(chips * rows, -1)
    out_shard = to_next_section(out_weight[0])
    chip_rows = own_features(normed(hidden))
    hidden_before = own_features(to_next_section(hidden))
    key_width = keyval_weight.shape[2]

    def projected(first, count):
        return jnp.dot(chip_rows, weights[:, first:first + count], preferred_element_type=jnp.float32)

    def of_core(value, which):
        parts = value.reshape(2 * rows, -1, 2, HEAD_SIZE)
        return lax.dynamic_index_in_dim(parts, which, 2, keepdims=False).reshape(2 * rows, -1)

    partial = projected(0, key_width)
    marks = jnp.zeros((8, rows), jnp.float32).at[0].set((segments + 1).astype(jnp.float32))
    received = swap_cores(jnp.concatenate([of_core(partial, 1 - core), marks], axis=0))
    keyvals = (of_core(partial, core) + received[: 2 * rows]).astype(jnp.bfloat16)
    chip_marks = in_order(marks[:1], received[2 * rows:2 * rows + 1]).astype(jnp.bfloat16)
    chip_marks = jnp.concatenate([chip_marks, jnp.zeros((14, rows), jnp.bfloat16)], axis=0)
    parcel = jnp.concatenate([keyvals, chip_marks], axis=0)
    back_two = two_chips_on(parcel)
    back_four = two_chips_on(back_two)
    even = chip % 2 == 0
    swapped = swap_chips(jnp.concatenate([jnp.where(even, parcel, back_four), back_two], axis=0))
    length = parcel.shape[0]
    crossed = [swapped[:length], swapped[length:]]
    parcels = [
        back_four, jnp.where(even, crossed[0], crossed[1]), back_two, jnp.where(even, crossed[1], crossed[0]), parcel
    ]
    window = jnp.concatenate([item[: 2 * rows] for item in parcels], axis=0)
    window_marks = jnp.concatenate([item[2 * rows:2 * rows + 2].reshape(-1) for item in parcels]).astype(jnp.int32)
    own_marks = window_marks[-2 * rows:]
    earlier = jnp.sum((window_marks[None, :] < own_marks[:, None]).astype(jnp.int32), axis=1)
    lowest = jnp.maximum(earlier, jnp.arange(1, 2 * rows + 1, dtype=jnp.int32))
    lowest = jnp.broadcast_to(lowest[:, None], (2 * rows, 128))

    out_weights = gathered(out_shard)
    attended_rows = []
    for g in range(2):
        partial = projected(key_width + 2 * g * GROUP_WIDTH, 2 * GROUP_WIDTH)
        kept = lax.dynamic_slice(partial, (0, core * GROUP_WIDTH), (2 * rows, GROUP_WIDTH))
        sent = lax.dynamic_slice(partial, (0, (1 - core) * GROUP_WIDTH), (2 * rows, GROUP_WIDTH))
        queries = (kept + swap_cores(sent)).astype(jnp.bfloat16) * jnp.bfloat16(HEAD_SIZE ** -0.5)
        keys = window[:, g * HEAD_SIZE:(g + 1) * HEAD_SIZE]
        values = window[:, (2 + g) * HEAD_SIZE:(3 + g) * HEAD_SIZE]
        blank = jnp.zeros_like(keys)
        keys_t = jnp.stack(
            [jnp.concatenate([keys, blank], axis=1).T, jnp.concatenate([blank, keys], axis=1).T]
        )
        wide = jnp.stack(
            [jnp.concatenate([values, blank], axis=1), jnp.concatenate([blank, values], axis=1)]
        )
        attended = to_next_section(attention(lowest, queries, keys_t, wide))
        attended_rows.append(in_order(attended, swap_cores(attended), axis=1))
    attended_rows = jnp.concatenate(attended_rows, axis=1)

    made = out_columns(attended_rows, out_weights, hidden_before)
    kept = lax.dynamic_slice(made, (core * rows, 0), (rows, width // 2)).reshape(rows, chips, 1, -1)
    sent = lax.dynamic_slice(made, ((1 - core) * rows, 0), (rows, width // 2))
    other = swap_cores(sent).reshape(rows, chips, 1, -1)
    return in_order(kept, other, axis=2).reshape(1, rows, width)


def solution(mesh):
    return jax.shard_map(
        body,
        mesh=mesh,
        in_specs=(
            P("section", "fsdp", None),
            P("section", "fsdp"),
            P("section", "fsdp", None),
            P("section", "fsdp", None),
            P("section", None, "fsdp"),
        ),
        out_specs=P("section", "fsdp", None),
        check_vma=False,
    )
```

```python
import functools

import jax
import jax.numpy as jnp
from jax import lax
from jax.experimental import pallas as pl
from jax.experimental.pallas import tpu as pltpu
from jax.sharding import PartitionSpec as P

QUERY_HEADS = 32
KEY_HEADS = 4
HEAD_SIZE = 64
LOOKBACK_SPAN = 2048
GROUP = QUERY_HEADS // KEY_HEADS
GROUP_WIDTH = GROUP * HEAD_SIZE
TILE = 256
MASKED = -1e30
MARK_ROWS = 16


def ring_order(chips):
    return list(range(0, chips, 2)) + list(range(chips - 1, 0, -2))


def swap_cores(value):
    count = lax.axis_size("fsdp")
    return lax.ppermute(value, "fsdp", [(i, i ^ 1) for i in range(count)])


def swap_chips(value):
    count = lax.axis_size("fsdp")
    return lax.ppermute(value, "fsdp", [(i, i ^ 2) for i in range(count)])


def two_chips_on(value):
    count = lax.axis_size("fsdp")
    return lax.ppermute(value, "fsdp", [(i, i + 4) for i in range(count - 4)])


def to_next_section(value):
    count = lax.axis_size("section")
    return lax.ppermute(value, "section", [(i, (i + 1) % count) for i in range(count)])


def along_ring(value, step):
    chips = lax.axis_size("fsdp") // 2
    order = ring_order(chips)
    pairs = []
    for place in range(chips):
        target = order[(place + step) % chips]
        pairs += [(2 * order[place] + core, 2 * target + core) for core in range(2)]
    return lax.ppermute(value, "fsdp", pairs)


def run(kernel, outs, scalars, arrays, waits=(), aliases=None, scratch=()):
    whole = pl.BlockSpec(memory_space=pltpu.VMEM)
    taken = 1 + len(arrays)

    def only(*refs):
        kernel(*refs[:taken], *refs[taken + len(waits):])

    return pl.pallas_call(
        only,
        in_specs=[pl.BlockSpec(memory_space=pltpu.SMEM)] + [whole] * len(arrays)
        + [pl.BlockSpec(memory_space=pl.ANY)] * len(waits),
        out_specs=[whole] * len(outs),
        out_shape=[jax.ShapeDtypeStruct(shape, dtype) for shape, dtype in outs],
        scratch_shapes=list(scratch),
        input_output_aliases=aliases or {},
        compiler_params=pltpu.CompilerParams(vmem_limit_bytes=40 * 1024 * 1024),
        cost_estimate=pl.CostEstimate(flops=1000000, bytes_accessed=100000, transcendentals=0),
    )(scalars, *arrays, *waits)


def tied_kernel(*refs):
    pass


def after(value, *others):
    anywhere = pl.BlockSpec(memory_space=pl.ANY)
    return pl.pallas_call(
        tied_kernel,
        in_specs=[anywhere] * (1 + len(others)),
        out_specs=anywhere,
        out_shape=jax.ShapeDtypeStruct(value.shape, value.dtype),
        input_output_aliases={0: 0},
        cost_estimate=pl.CostEstimate(flops=0, bytes_accessed=0, transcendentals=0),
    )(value, *others)


class Ring:
    def __init__(self, shard, longer):
        self.chips, self.longer, self.step = lax.axis_size("fsdp") // 2, longer, 0
        self.moving, self.found = {1: shard, -1: shard}, {0: shard}
        self.last = shard

    def advance(self, *waits):
        self.step += 1
        for way in (1, -1):
            if 2 * self.step < self.chips or way == self.longer:
                value = after(self.moving[way], *waits) if waits else self.moving[way]
                self.moving[way] = self.last = along_ring(value, way)
                self.found[-way * self.step % self.chips] = self.last


def block(index, size):
    return pl.ds(pl.multiple_of(index * size, size), size)


def split_kernel(norm, scal_ref, rows_ref, kept_ref, sent_ref):
    core = scal_ref[0]
    count, width = rows_ref.shape
    size, some = 256, 64
    for first in range(0, count, some):
        at = slice(first, first + some)
        if norm:
            values = rows_ref[at, :].astype(jnp.float32)
            scale = lax.rsqrt(jnp.mean(values * values, axis=1, keepdims=True) + 1e-05)
        for j in range(width // (2 * size)):
            for out_ref, which in ((kept_ref, core), (sent_ref, 1 - core)):
                part = rows_ref[at, block(2 * j + which, size)]
                if norm:
                    part = (part.astype(jnp.float32) * scale).astype(jnp.bfloat16)
                out_ref[at, j * size:(j + 1) * size] = part


def keyval_kernel(distances, scal_ref, segs_ref, own_ref, other_ref, *refs):
    weights, (kept_ref, sent_ref) = refs[: len(distances)], refs[len(distances):]
    core = scal_ref[0]
    rows = own_ref.shape[0]
    lane = lax.broadcasted_iota(jnp.int32, (rows, 128), 1)
    for rows_ref, which in ((own_ref, core), (other_ref, 1 - core)):
        total = None
        for distance, weight_ref in zip(distances, weights):
            found = jnp.dot(
                rows_ref[:, block(scal_ref[2 + distance], weight_ref.shape[0])], weight_ref[...],
                preferred_element_type=jnp.float32,
            )
            total = found if total is None else total + found
        for part in range(2):
            low = total[:, part * 256:part * 256 + 128]
            high = total[:, part * 256 + 128:part * 256 + 256]
            zero = jnp.where(lane < HEAD_SIZE, low, pltpu.roll(high, HEAD_SIZE, 1))
            one = jnp.where(lane < HEAD_SIZE, pltpu.roll(low, HEAD_SIZE, 1), high)
            at = slice(part * 128, part * 128 + 128)
            kept_ref[block(which, rows), at] = jnp.where(core == 0, zero, one)
            sent_ref[block(which, rows), at] = jnp.where(core == 0, one, zero)
    marks = (segs_ref[...] + 1).astype(jnp.float32)
    sent_ref[2 * rows:, :] = jnp.broadcast_to(marks, (8, marks.shape[1]))


def parcel_kernel(scal_ref, segs_ref, kept_ref, received_ref, out_ref):
    core = scal_ref[0]
    count = kept_ref.shape[0]
    out_ref[:count, :] = (kept_ref[...] + received_ref[:count, :]).astype(out_ref.dtype)
    own = (segs_ref[...] + 1).astype(jnp.float32)
    other = received_ref[count:count + 1, :]
    first, second = jnp.where(core == 0, own, other), jnp.where(core == 0, other, own)
    row = lax.broadcasted_iota(jnp.int32, (MARK_ROWS, own.shape[1]), 0)
    marks = jnp.where(row == 0, first, jnp.where(row == 1, second, 0.0))
    out_ref[count:, :] = marks.astype(out_ref.dtype)


def window_kernel(scal_ref, four_ref, two_ref, own_ref, crossed_ref, kt_ref, v_ref, lo_ref):
    odd = scal_ref[1]
    length = own_ref.shape[0]
    count = length - MARK_ROWS
    half = count // 2
    second = pl.multiple_of(odd * length, MARK_ROWS)
    fourth = pl.multiple_of((1 - odd) * length, MARK_ROWS)
    places = [(four_ref, 0), (crossed_ref, second), (two_ref, 0), (crossed_ref, fourth), (own_ref, 0)]
    lane = lax.broadcasted_iota(jnp.int32, (count, 128), 1)
    blank = jnp.zeros((HEAD_SIZE, count), jnp.bfloat16)
    marks = []
    for i, (ref, first) in enumerate(places):
        at = slice(i * count, (i + 1) * count)
        keys = ref[pl.ds(first, count), 0:128].astype(jnp.float32).T.astype(jnp.bfloat16)
        values = ref[pl.ds(first, count), 128:256].astype(jnp.float32)
        turned = pltpu.roll(values, HEAD_SIZE, 1)
        for g in range(2):
            head = keys[g * HEAD_SIZE:(g + 1) * HEAD_SIZE]
            kt_ref[g, 0, :HEAD_SIZE, at] = head
            kt_ref[g, 0, HEAD_SIZE:, at] = blank
            kt_ref[g, 1, :HEAD_SIZE, at] = blank
            kt_ref[g, 1, HEAD_SIZE:, at] = head
            low, high = (values, turned) if g == 0 else (turned, values)
            v_ref[g, 0, at, :] = jnp.where(lane < HEAD_SIZE, low, 0.0).astype(jnp.bfloat16)
            v_ref[g, 1, at, :] = jnp.where(lane < HEAD_SIZE, 0.0, high).astype(jnp.bfloat16)
        found = ref[pl.ds(first + count, MARK_ROWS), :].astype(jnp.float32)
        marks += [found[0:1, :], found[1:2, :]]
    across = lax.broadcasted_iota(jnp.int32, (half, half), 1)
    down = lax.broadcasted_iota(jnp.int32, (half, half), 0)
    for part in range(2):
        mine = jnp.sum(jnp.where(across == down, marks[-2 + part], 0.0), axis=1, keepdims=True)
        earlier = jnp.zeros((half, half), jnp.float32)
        for row in marks:
            earlier = earlier + jnp.where(row < mine, 1.0, 0.0)
        earlier = jnp.sum(earlier, axis=1, keepdims=True).astype(jnp.int32)
        place = lax.broadcasted_iota(jnp.int32, (half, 128), 0) + (part * half + 1)
        lo_ref[part * half:(part + 1) * half, :] = jnp.maximum(earlier, place)


def query_kernel(distances, more, scal_ref, own_ref, other_ref, *refs):
    weights, refs = refs[: len(distances)], refs[len(distances):]
    core = scal_ref[0]
    rows = own_ref.shape[0]
    outs = refs[-2:]
    for rows_ref, which in ((own_ref, core), (other_ref, 1 - core)):
        at = block(which, rows)
        for i, column in enumerate((core, 1 - core)):
            total = refs[i][at, :] if more else None
            for distance, weight_ref in zip(distances, weights):
                found = jnp.dot(
                    rows_ref[:, block(scal_ref[2 + distance], weight_ref.shape[0])],
                    weight_ref[:, block(column, GROUP_WIDTH)],
                    preferred_element_type=jnp.float32,
                )
                total = found if total is None else total + found
            outs[i][at, :] = total


def attention_kernel(lo_ref, kept_ref, received_ref, kt_ref, v_ref, out_ref, query_ref, score_ref):
    tile = pl.program_id(0)
    start = pl.multiple_of(tile * TILE, TILE)
    span = LOOKBACK_SPAN + TILE
    lo = lo_ref[...] - start
    lane = lax.broadcasted_iota(jnp.int32, (TILE, 128), 1)
    row = lax.broadcasted_iota(jnp.int32, (TILE, 128), 0)
    blocks = span // TILE
    queries = (kept_ref[...] + received_ref[...]).astype(jnp.bfloat16)
    query_ref[...] = queries * jnp.bfloat16(HEAD_SIZE ** -0.5)

    def scores_of(pair, parity):
        q = query_ref[:, pair * 128:(pair + 1) * 128]
        peak = jnp.full((TILE, 128), MASKED, jnp.float32)
        for i in range(blocks):
            first = pl.multiple_of(start + i * TILE, TILE)
            found = jnp.dot(q, kt_ref[parity, :, pl.ds(first, TILE)], preferred_element_type=jnp.float32)
            for part in range(TILE // 128):
                at = i * TILE + part * 128
                visible = lane + at >= lo
                if at >= LOOKBACK_SPAN:
                    visible = visible & (lane + (at - LOOKBACK_SPAN) <= row)
                kept = jnp.where(visible, found[:, part * 128:(part + 1) * 128], MASKED)
                peak = jnp.maximum(peak, kept)
                score_ref[parity, :, at:at + 128] = kept
        return jnp.max(peak, axis=1, keepdims=True)

    def mixed_of(parity, peak):
        total = jnp.zeros((TILE, 128), jnp.float32)
        mixed = jnp.zeros((TILE, 128), jnp.float32)
        for i in range(blocks):
            first = pl.multiple_of(start + i * TILE, TILE)
            weights = jnp.exp(score_ref[parity, :, i * TILE:(i + 1) * TILE] - peak)
            for part in range(TILE // 128):
                total = total + weights[:, part * 128:(part + 1) * 128]
            mixed = mixed + jnp.dot(
                weights.astype(jnp.bfloat16), v_ref[parity, pl.ds(first, TILE), :],
                preferred_element_type=jnp.float32,
            )
        return mixed * (1.0 / jnp.sum(total, axis=1, keepdims=True))

    for pair in range(GROUP // 2):
        peaks = [scores_of(pair, parity) for parity in range(2)]
        parts = [mixed_of(parity, peaks[parity]) for parity in range(2)]
        out_ref[:, pair * 128:(pair + 1) * 128] = (parts[0] + parts[1]).astype(out_ref.dtype)


def attention(lo, kept, received, keys_t, values, waits):
    rows = kept.shape[0]
    window = keys_t.shape[2]
    span = LOOKBACK_SPAN + TILE

    def only(*refs):
        attention_kernel(*refs[:5], *refs[5 + len(waits):])

    return pl.pallas_call(
        only,
        grid=(rows // TILE,),
        in_specs=[
            pl.BlockSpec((TILE, 128), lambda t: (t, 0)),
            pl.BlockSpec((TILE, GROUP_WIDTH), lambda t: (t, 0)),
            pl.BlockSpec((TILE, GROUP_WIDTH), lambda t: (t, 0)),
            pl.BlockSpec((2, 128, window), lambda t: (0, 0, 0)),
            pl.BlockSpec((2, window, 128), lambda t: (0, 0, 0)),
        ] + [pl.BlockSpec(memory_space=pl.ANY)] * len(waits),
        out_specs=pl.BlockSpec((TILE, GROUP_WIDTH), lambda t: (t, 0)),
        out_shape=jax.ShapeDtypeStruct((rows, GROUP_WIDTH), jnp.bfloat16),
        scratch_shapes=[
            pltpu.VMEM((TILE, GROUP_WIDTH), jnp.bfloat16), pltpu.VMEM((2, TILE, span), jnp.float32)
        ],
        compiler_params=pltpu.CompilerParams(vmem_limit_bytes=40 * 1024 * 1024),
        cost_estimate=pl.CostEstimate(flops=1000000, bytes_accessed=100000, transcendentals=0),
    )(lo, kept, received, keys_t, values, *waits)


def out_kernel(distances, mode, scal_ref, *refs):
    attended, refs = refs[:4], refs[4:]
    adds, refs = refs[:2], refs[2:]
    weights, refs = refs[: 2 * len(distances)], refs[2 * len(distances):]
    outs = refs[-2:]
    core = scal_ref[0]
    rows = adds[0].shape[0]
    depth = attended[0].shape[1]
    if mode != "alone":
        for i in range(2):
            outs[i][...] = refs[i][...] if mode == "more" else jnp.zeros_like(outs[i])
    for i, which in enumerate((core, 1 - core)):
        for j, distance in enumerate(distances):
            columns = weights[2 * j].shape[1]
            at = block(scal_ref[2 + distance], columns)
            total = adds[i][:, at].astype(jnp.float32)
            for g in range(2):
                for side, column in enumerate((core, 1 - core)):
                    total = total + jnp.dot(
                        attended[2 * g + side][block(which, rows), :],
                        weights[2 * j + g][block(column, depth), :],
                        preferred_element_type=jnp.float32,
                    )
            if mode == "alone":
                outs[i][...] = total.astype(outs[i].dtype)
            else:
                outs[i][:, at] = total.astype(outs[i].dtype)


def join_kernel(last, scal_ref, own_ref, other_ref, own_last_ref, other_last_ref, out_ref):
    core = scal_ref[0]
    size = own_last_ref.shape[1]
    for j in range(own_ref.shape[1] // size):
        at = slice(j * size, (j + 1) * size)
        out_ref[:, block(2 * j + core, size)] = own_ref[:, at]
        out_ref[:, block(2 * j + 1 - core, size)] = other_ref[:, at]
    j = scal_ref[2 + last]
    out_ref[:, block(2 * j + core, size)] = own_last_ref[...]
    out_ref[:, block(2 * j + 1 - core, size)] = other_last_ref[...]


def body(section_input, segment_ids, query_weight, keyval_weight, out_weight):
    hidden = section_input[0]
    rows, width = hidden.shape
    device = lax.axis_index("fsdp")
    chips = lax.axis_size("fsdp") // 2
    chip, core = device // 2, device % 2
    order = jnp.array(ring_order(chips), jnp.int32)
    place = jnp.argmax(order == chip).astype(jnp.int32)
    sources = order[(place + jnp.arange(chips, dtype=jnp.int32)) % chips]
    scalars = jnp.concatenate([jnp.stack([core, chip % 2]).astype(jnp.int32), sources])

    per_half = query_weight.shape[2] // 2
    keyval = Ring(keyval_weight[0], 1)
    query = [Ring(query_weight[0][:, g * per_half:(g + 1) * per_half], 1 - 2 * g) for g in range(2)]
    keyval.advance()
    query[0].advance()
    query[1].advance()
    out_shard = to_next_section(out_weight[0])

    half = ((rows, width // 2), jnp.bfloat16)
    own_rows, sent = run(functools.partial(split_kernel, True), [half, half], scalars, [hidden])
    other_rows = swap_cores(sent)

    keyval.advance()
    keyval.advance()
    query[0].advance()
    query[1].advance(query[0].found[chips - 1])
    keyval.advance(query[1].found[1])
    distances = list(range(chips))
    kept, sent = run(
        functools.partial(keyval_kernel, distances),
        [((2 * rows, 256), jnp.float32), ((2 * rows + 8, 256), jnp.float32)],
        scalars, [segment_ids, own_rows, other_rows] + [keyval.found[d] for d in distances],
    )
    parcel, = run(
        parcel_kernel, [((2 * rows + MARK_ROWS, 256), jnp.bfloat16)], scalars,
        [segment_ids, kept, swap_cores(sent)],
    )
    back_two = two_chips_on(parcel)

    query[0].advance(keyval.last)
    query[1].advance(query[0].found[2])
    near = [0, 1, chips - 1, 2, chips - 2]
    far = [d for d in distances if d not in near]
    partial_sum = ((2 * rows, GROUP_WIDTH), jnp.float32)
    sums = [
        run(
            functools.partial(query_kernel, near, False), [partial_sum] * 2, scalars,
            [own_rows, other_rows] + [query[g].found[d] for d in near], waits=[parcel],
        )
        for g in range(2)
    ]
    back_four = two_chips_on(back_two)
    even = chip % 2 == 0
    crossed = swap_chips(jnp.concatenate([jnp.where(even, parcel, back_four), back_two], axis=0))
    window = 5 * 2 * rows
    keys_t, values, lowest = run(
        window_kernel,
        [((2, 2, 128, window), jnp.bfloat16), ((2, 2, window, 128), jnp.bfloat16), ((2 * rows, 128), jnp.int32)],
        scalars, [back_four, back_two, parcel, crossed], waits=sums[0][:1] + sums[1][:1],
    )

    middle = out_shard.shape[0] // 2
    out_ready = after(out_shard, query[0].found[3], query[1].found[3])
    query[0].advance()
    query[1].advance()
    out = [Ring(out_ready[g * middle:(g + 1) * middle], 1 - 2 * g) for g in range(2)]
    out[0].advance()
    out[1].advance()
    hidden_next = to_next_section(after(hidden, out_shard))

    sums = [
        run(
            functools.partial(query_kernel, far, True), [partial_sum] * 2, scalars,
            [own_rows, other_rows] + [query[g].found[d] for d in far] + list(sums[g]), waits=[keys_t],
        )
        for g in range(2)
    ]
    received = [swap_cores(sums[g][1]) for g in range(2)]
    out[0].advance(received[0])
    out[1].advance(received[1])
    attended = [None, None]
    attended[0] = attention(
        lowest, sums[0][0], received[0], keys_t[0], values[0], [out[0].found[1], out[1].found[1]]
    )
    out[0].advance(attended[0])
    out[1].advance(attended[0])
    attended[1] = attention(
        lowest, sums[1][0], received[1], keys_t[1], values[1], [out[0].found[2], out[1].found[2]]
    )
    kept, sent = run(functools.partial(split_kernel, False), [half, half], scalars, [hidden_next])
    adds = [kept, swap_cores(sent)]
    out[0].advance(attended[1])
    out[1].advance(attended[1])
    arrived = []
    for g in range(2):
        mine = to_next_section(attended[g])
        arrived += [mine, swap_cores(mine)]

    def made(some, mode, before=()):
        shards = [out[g].found[d] for d in some for g in range(2)]
        outs = [((rows, out_shard.shape[1]), jnp.bfloat16)] * 2 if mode == "alone" else [half, half]
        taken = arrived + adds + shards
        aliases = {1 + len(taken) + i: i for i in range(2)} if before else {}
        return run(
            functools.partial(out_kernel, some, mode), outs, scalars, taken + list(before), aliases=aliases
        )

    most = made([0, 1, chips - 1, 2, chips - 2], "first")
    most = made([3, chips - 3], "more", most)
    other_most = swap_cores(most[1])
    last = made([chips // 2], "alone")
    joined, = run(
        functools.partial(join_kernel, chips // 2), [((rows, width), jnp.bfloat16)], scalars,
        [most[0], other_most, last[0], swap_cores(last[1])],
    )
    return joined[None]


def solution(mesh):
    return jax.shard_map(
        body,
        mesh=mesh,
        in_specs=(
            P("section", "fsdp", None),
            P("section", "fsdp"),
            P("section", "fsdp", None),
            P("section", "fsdp", None),
            P("section", None, "fsdp"),
        ),
        out_specs=P("section", "fsdp", None),
        check_vma=False,
    )
```

```python
import functools

import jax
import jax.numpy as jnp
from jax import lax
from jax.experimental import pallas as pl
from jax.experimental.pallas import tpu as pltpu
from jax.sharding import PartitionSpec as P

QUERY_HEADS = 32
KEY_HEADS = 4
HEAD_SIZE = 64
LOOKBACK_SPAN = 2048
GROUP = QUERY_HEADS // KEY_HEADS
GROUP_WIDTH = GROUP * HEAD_SIZE
TILE = 256
MASKED = -1e30
MARK_ROWS = 16


def ring_order(chips):
    return list(range(0, chips, 2)) + list(range(chips - 1, 0, -2))


def swap_cores(value):
    count = lax.axis_size("fsdp")
    return lax.ppermute(value, "fsdp", [(i, i ^ 1) for i in range(count)])


def swap_chips(value):
    count = lax.axis_size("fsdp")
    return lax.ppermute(value, "fsdp", [(i, i ^ 2) for i in range(count)])


def two_chips_on(value):
    count = lax.axis_size("fsdp")
    return lax.ppermute(value, "fsdp", [(i, i + 4) for i in range(count - 4)])


def to_next_section(value, other_core=False):
    sections, count = lax.axis_size("section"), lax.axis_size("fsdp")
    pairs = []
    for section in range(sections):
        for i in range(count):
            target = i ^ 1 if other_core else i
            pairs.append((section * count + i, (section + 1) % sections * count + target))
    return lax.ppermute(value, ("section", "fsdp"), pairs)


def along_ring(value, step):
    chips = lax.axis_size("fsdp") // 2
    order = ring_order(chips)
    pairs = []
    for place in range(chips):
        target = order[(place + step) % chips]
        pairs += [(2 * order[place] + core, 2 * target + core) for core in range(2)]
    return lax.ppermute(value, "fsdp", pairs)


def run(kernel, outs, scalars, arrays, waits=(), aliases=None, scratch=()):
    whole = pl.BlockSpec(memory_space=pltpu.VMEM)
    taken = 1 + len(arrays)

    def only(*refs):
        kernel(*refs[:taken], *refs[taken + len(waits):])

    return pl.pallas_call(
        only,
        in_specs=[pl.BlockSpec(memory_space=pltpu.SMEM)] + [whole] * len(arrays)
        + [pl.BlockSpec(memory_space=pl.ANY)] * len(waits),
        out_specs=[whole] * len(outs),
        out_shape=[jax.ShapeDtypeStruct(shape, dtype) for shape, dtype in outs],
        scratch_shapes=list(scratch),
        input_output_aliases=aliases or {},
        compiler_params=pltpu.CompilerParams(vmem_limit_bytes=40 * 1024 * 1024),
        cost_estimate=pl.CostEstimate(flops=1000000, bytes_accessed=100000, transcendentals=0),
    )(scalars, *arrays, *waits)


def around(shard):
    chips = lax.axis_size("fsdp") // 2
    found, moving = {0: [(0, shard)]}, {1: shard, -1: shard}
    for step in range(1, (chips - 1) // 2 + 1):
        for way in (1, -1):
            moving[way] = along_ring(moving[way], way)
            found[-way * step % chips] = [(0, moving[way])]
    if chips % 2 == 0:
        half = shard.shape[0] // 2
        found[chips // 2] = [
            (0, along_ring(moving[1][:half], 1)), (half, along_ring(moving[-1][half:], -1))
        ]
    return found


def block(index, size):
    return pl.ds(pl.multiple_of(index * size, size), size)


def split_kernel(norm, scal_ref, rows_ref, kept_ref, sent_ref):
    core = scal_ref[0]
    count, width = rows_ref.shape
    size, some = 256, 64
    for first in range(0, count, some):
        at = slice(first, first + some)
        if norm:
            values = rows_ref[at, :].astype(jnp.float32)
            scale = lax.rsqrt(jnp.mean(values * values, axis=1, keepdims=True) + 1e-05)
        for j in range(width // (2 * size)):
            for out_ref, which in ((kept_ref, core), (sent_ref, 1 - core)):
                part = rows_ref[at, block(2 * j + which, size)]
                if norm:
                    part = (part.astype(jnp.float32) * scale).astype(jnp.bfloat16)
                out_ref[at, j * size:(j + 1) * size] = part


def keyval_kernel(scal_ref, segs_ref, own_ref, other_ref, weight_ref, kept_ref, sent_ref):
    core = scal_ref[0]
    rows = own_ref.shape[0]
    size = 256
    total = None
    for j in range(own_ref.shape[1] // size):
        for ref, which in ((own_ref, core), (other_ref, 1 - core)):
            found = jnp.dot(
                ref[:, j * size:(j + 1) * size], weight_ref[0, block(2 * j + which, size), :],
                preferred_element_type=jnp.float32,
            )
            total = found if total is None else total + found
    lane = lax.broadcasted_iota(jnp.int32, (rows, 128), 1)
    for part in range(2):
        low = total[:, part * 256:part * 256 + 128]
        high = total[:, part * 256 + 128:part * 256 + 256]
        zero = jnp.where(lane < HEAD_SIZE, low, pltpu.roll(high, HEAD_SIZE, 1))
        one = jnp.where(lane < HEAD_SIZE, pltpu.roll(low, HEAD_SIZE, 1), high)
        at = slice(part * 128, part * 128 + 128)
        kept_ref[:, at] = jnp.where(core == 0, zero, one).astype(kept_ref.dtype)
        sent_ref[:rows, at] = jnp.where(core == 0, one, zero).astype(sent_ref.dtype)
    marks = (segs_ref[...] + 1).astype(jnp.float32)
    sent_ref[rows:, :] = jnp.broadcast_to(marks, (MARK_ROWS, rows)).astype(sent_ref.dtype)


def parcel_kernel(scal_ref, segs_ref, kept_ref, received_ref, out_ref):
    core = scal_ref[0]
    rows = kept_ref.shape[0]
    out_ref[block(core, rows), :] = kept_ref[...]
    out_ref[block(1 - core, rows), :] = received_ref[:rows, :]
    own = (segs_ref[...] + 1).astype(jnp.float32)
    other = received_ref[rows:, :].astype(jnp.float32)[0:1, :]
    first, second = jnp.where(core == 0, own, other), jnp.where(core == 0, other, own)
    row = lax.broadcasted_iota(jnp.int32, (MARK_ROWS, rows), 0)
    marks = jnp.where(row == 0, first, jnp.where(row == 1, second, 0.0))
    out_ref[2 * rows:, :] = marks.astype(out_ref.dtype)


def window_kernel(scal_ref, four_ref, two_ref, own_ref, crossed_ref, kt_ref, v_ref, lo_ref):
    odd = scal_ref[1]
    length = own_ref.shape[0]
    count = length - MARK_ROWS
    half = count // 2
    second = pl.multiple_of(odd * length, MARK_ROWS)
    fourth = pl.multiple_of((1 - odd) * length, MARK_ROWS)
    places = [(four_ref, 0), (crossed_ref, second), (two_ref, 0), (crossed_ref, fourth), (own_ref, 0)]
    lane = lax.broadcasted_iota(jnp.int32, (count, 128), 1)
    blank = jnp.zeros((HEAD_SIZE, count), jnp.bfloat16)
    marks = []
    for i, (ref, first) in enumerate(places):
        at = slice(i * count, (i + 1) * count)
        keys = ref[pl.ds(first, count), 0:128].astype(jnp.float32).T.astype(jnp.bfloat16)
        values = ref[pl.ds(first, count), 128:256].astype(jnp.float32)
        turned = pltpu.roll(values, HEAD_SIZE, 1)
        for g in range(2):
            head = keys[g * HEAD_SIZE:(g + 1) * HEAD_SIZE]
            kt_ref[g, 0, :HEAD_SIZE, at] = head
            kt_ref[g, 0, HEAD_SIZE:, at] = blank
            kt_ref[g, 1, :HEAD_SIZE, at] = blank
            kt_ref[g, 1, HEAD_SIZE:, at] = head
            low, high = (values, turned) if g == 0 else (turned, values)
            v_ref[g, 0, at, :] = jnp.where(lane < HEAD_SIZE, low, 0.0).astype(jnp.bfloat16)
            v_ref[g, 1, at, :] = jnp.where(lane < HEAD_SIZE, 0.0, high).astype(jnp.bfloat16)
        found = ref[pl.ds(first + count, MARK_ROWS), :].astype(jnp.float32)
        marks += [found[0:1, :], found[1:2, :]]
    across = lax.broadcasted_iota(jnp.int32, (half, half), 1)
    down = lax.broadcasted_iota(jnp.int32, (half, half), 0)
    for part in range(2):
        mine = jnp.sum(jnp.where(across == down, marks[-2 + part], 0.0), axis=1, keepdims=True)
        earlier = jnp.zeros((half, half), jnp.float32)
        for row in marks:
            earlier = earlier + jnp.where(row < mine, 1.0, 0.0)
        earlier = jnp.sum(earlier, axis=1, keepdims=True).astype(jnp.int32)
        place = lax.broadcasted_iota(jnp.int32, (half, 128), 0) + (part * half + 1)
        lo_ref[part * half:(part + 1) * half, :] = jnp.maximum(earlier, place)


def query_kernel(pieces, g, more, scal_ref, own_ref, other_ref, *refs):
    weights, refs = refs[: len(pieces)], refs[len(pieces):]
    core = scal_ref[0]
    rows = own_ref.shape[0]
    outs = refs[-2:]
    for rows_ref, which in ((own_ref, core), (other_ref, 1 - core)):
        at = block(which, rows)
        for i, column in enumerate((core, 1 - core)):
            total = refs[i][at, :] if more else None
            for (distance, first), weight_ref in zip(pieces, weights):
                depth = weight_ref.shape[0]
                start = pl.multiple_of(scal_ref[2 + distance] * rows + first, depth)
                found = jnp.dot(
                    rows_ref[:, pl.ds(start, depth)], weight_ref[:, block(2 * g + column, GROUP_WIDTH)],
                    preferred_element_type=jnp.float32,
                )
                total = found if total is None else total + found
            outs[i][at, :] = total


def attention_kernel(
    scal_ref, lo_ref, kept_ref, received_ref, kt_ref, v_ref, same_ref, cross_ref, query_ref, score_ref, out_ref
):
    step = pl.program_id(0)
    tile = jnp.where(step == 0, scal_ref[0], 1 - scal_ref[0])
    start = pl.multiple_of(tile * TILE, TILE)
    span = LOOKBACK_SPAN + TILE
    lo = lo_ref[pl.ds(start, TILE), :] - start
    lane = lax.broadcasted_iota(jnp.int32, (TILE, 128), 1)
    row = lax.broadcasted_iota(jnp.int32, (TILE, 128), 0)
    blocks = span // TILE
    queries = (kept_ref[pl.ds(start, TILE), :] + received_ref[pl.ds(start, TILE), :]).astype(jnp.bfloat16)
    query_ref[...] = queries * jnp.bfloat16(HEAD_SIZE ** -0.5)

    def scores_of(pair, parity):
        q = query_ref[:, pair * 128:(pair + 1) * 128]
        peak = jnp.full((TILE, 128), MASKED, jnp.float32)
        for i in range(blocks):
            first = pl.multiple_of(start + i * TILE, TILE)
            found = jnp.dot(q, kt_ref[parity, :, pl.ds(first, TILE)], preferred_element_type=jnp.float32)
            for part in range(TILE // 128):
                at = i * TILE + part * 128
                visible = lane + at >= lo
                if at >= LOOKBACK_SPAN:
                    visible = visible & (lane + (at - LOOKBACK_SPAN) <= row)
                kept = jnp.where(visible, found[:, part * 128:(part + 1) * 128], MASKED)
                peak = jnp.maximum(peak, kept)
                score_ref[parity, :, at:at + 128] = kept
        return jnp.max(peak, axis=1, keepdims=True)

    def mixed_of(parity, peak):
        total = jnp.zeros((TILE, 128), jnp.float32)
        mixed = jnp.zeros((TILE, 128), jnp.float32)
        for i in range(blocks):
            first = pl.multiple_of(start + i * TILE, TILE)
            weights = jnp.exp(score_ref[parity, :, i * TILE:(i + 1) * TILE] - peak)
            for part in range(TILE // 128):
                total = total + weights[:, part * 128:(part + 1) * 128]
            mixed = mixed + jnp.dot(
                weights.astype(jnp.bfloat16), v_ref[parity, pl.ds(first, TILE), :],
                preferred_element_type=jnp.float32,
            )
        return mixed * (1.0 / jnp.sum(total, axis=1, keepdims=True))

    for pair in range(GROUP // 2):
        peaks = [scores_of(pair, parity) for parity in range(2)]
        parts = [mixed_of(parity, peaks[parity]) for parity in range(2)]
        out_ref[:, pair * 128:(pair + 1) * 128] = (parts[0] + parts[1]).astype(out_ref.dtype)

    @pl.when(step == 0)
    def _():
        same_ref[...] = out_ref[...]

    @pl.when(step == 1)
    def _():
        cross_ref[...] = out_ref[...]


def attention(scalars, lo, kept, received, keys_t, values):
    rows = kept.shape[0]
    span = LOOKBACK_SPAN + TILE
    arrays = [lo, kept, received, keys_t, values]
    part = (TILE, GROUP_WIDTH)
    return pl.pallas_call(
        attention_kernel,
        grid=(rows // TILE,),
        in_specs=[pl.BlockSpec(memory_space=pltpu.SMEM)]
        + [pl.BlockSpec(memory_space=pltpu.VMEM)] * len(arrays),
        out_specs=[pl.BlockSpec(memory_space=pltpu.VMEM)] * 2,
        out_shape=[jax.ShapeDtypeStruct(part, jnp.bfloat16)] * 2,
        scratch_shapes=[
            pltpu.VMEM(part, jnp.bfloat16), pltpu.VMEM((2, TILE, span), jnp.float32),
            pltpu.VMEM(part, jnp.bfloat16),
        ],
        compiler_params=pltpu.CompilerParams(vmem_limit_bytes=40 * 1024 * 1024),
        cost_estimate=pl.CostEstimate(flops=1000000, bytes_accessed=100000, transcendentals=0),
    )(scalars, *arrays)


def out_kernel(scal_ref, *refs):
    attended, (weight_ref, add_ref, out_ref) = refs[:4], refs[4:]
    core = scal_ref[0]
    total = add_ref[...].astype(jnp.float32)
    for g in range(2):
        for side, column in enumerate((core, 1 - core)):
            total = total + jnp.dot(
                attended[2 * g + side][...], weight_ref[0, block(2 * g + column, GROUP_WIDTH), :],
                preferred_element_type=jnp.float32,
            )
    out_ref[...] = total.astype(out_ref.dtype)


def projected_out(scalars, attended, weights, add):
    count, depth, columns = weights.shape
    rows = add.shape[0]
    return pl.pallas_call(
        out_kernel,
        grid=(count,),
        in_specs=[pl.BlockSpec(memory_space=pltpu.SMEM)]
        + [pl.BlockSpec(memory_space=pltpu.VMEM)] * len(attended)
        + [
            pl.BlockSpec((1, depth, columns), lambda i: (i, 0, 0)),
            pl.BlockSpec((rows, columns), lambda i: (0, i)),
        ],
        out_specs=pl.BlockSpec((rows, columns), lambda i: (0, i)),
        out_shape=jax.ShapeDtypeStruct(add.shape, add.dtype),
        compiler_params=pltpu.CompilerParams(vmem_limit_bytes=40 * 1024 * 1024),
        cost_estimate=pl.CostEstimate(
            flops=2 * rows * depth * count * columns, bytes_accessed=20 * 1024 * 1024, transcendentals=0
        ),
    )(scalars, *attended, weights, add)


def body(section_input, segment_ids, query_weight, keyval_weight, out_weight):
    hidden = section_input[0]
    rows, width = hidden.shape
    device = lax.axis_index("fsdp")
    chips = lax.axis_size("fsdp") // 2
    chip, core = device // 2, device % 2
    order = jnp.array(ring_order(chips), jnp.int32)
    place = jnp.argmax(order == chip).astype(jnp.int32)
    sources = order[(place + jnp.arange(chips, dtype=jnp.int32)) % chips]
    scalars = jnp.concatenate([jnp.stack([core, chip % 2]).astype(jnp.int32), sources])

    query_pieces = around(query_weight[0])
    keyval_full = lax.all_gather(keyval_weight, "fsdp", axis=1, tiled=True)
    out_full = lax.all_gather(to_next_section(out_weight[0]), "fsdp", axis=0, tiled=False)

    half = ((rows, width // 2), jnp.bfloat16)
    own_rows, sent_rows = run(functools.partial(split_kernel, True), [half, half], scalars, [hidden])
    other_rows = swap_cores(sent_rows)

    kept, sent = run(
        keyval_kernel, [((rows, 256), jnp.bfloat16), ((rows + MARK_ROWS, 256), jnp.bfloat16)],
        scalars, [segment_ids, own_rows, sent_rows, keyval_full],
    )
    parcel, = run(
        parcel_kernel, [((2 * rows + MARK_ROWS, 256), jnp.bfloat16)], scalars,
        [segment_ids, kept, swap_cores(sent)],
    )
    back_two = two_chips_on(parcel)
    back_four = two_chips_on(back_two)
    even = chip % 2 == 0
    crossed = swap_chips(jnp.concatenate([jnp.where(even, parcel, back_four), back_two], axis=0))
    window = 5 * 2 * rows
    keys_t, values, lowest = run(
        window_kernel,
        [((2, 2, 128, window), jnp.bfloat16), ((2, 2, window, 128), jnp.bfloat16), ((2 * rows, 128), jnp.int32)],
        scalars, [back_four, back_two, parcel, crossed],
    )

    def query_sums(distances, g, waits, before=()):
        pieces = [(d, first) for d in distances for first, _ in query_pieces[d]]
        shards = [shard for d in distances for _, shard in query_pieces[d]]
        return run(
            functools.partial(query_kernel, pieces, g, bool(before)),
            [((2 * rows, GROUP_WIDTH), jnp.float32)] * 2, scalars,
            [own_rows, other_rows] + shards + list(before), waits=waits,
        )

    near = [0, 1, chips - 1, 2, chips - 2]
    far = [d for d in range(chips) if d not in near]
    sums = [query_sums(near, g, [parcel]) for g in range(2)]
    sums = [query_sums(far, g, [keys_t], sums[g]) for g in range(2)]
    arrived = []
    for g in range(2):
        same, cross = attention(
            scalars, lowest, sums[g][0], swap_cores(sums[g][1]), keys_t[g], values[g]
        )
        arrived += [to_next_section(same), to_next_section(cross, other_core=True)]
    return projected_out(scalars, arrived, out_full, to_next_section(hidden))[None]


def solution(mesh):
    return jax.shard_map(
        body,
        mesh=mesh,
        in_specs=(
            P("section", "fsdp", None),
            P("section", "fsdp"),
            P("section", "fsdp", None),
            P("section", "fsdp", None),
            P("section", None, "fsdp"),
        ),
        out_specs=P("section", "fsdp", None),
        check_vma=False,
    )
```

```python
import functools

import jax
import jax.numpy as jnp
from jax import lax
from jax.experimental import pallas as pl
from jax.experimental.pallas import tpu as pltpu
from jax.sharding import PartitionSpec as P

QUERY_HEADS = 32
KEY_HEADS = 4
HEAD_SIZE = 64
LOOKBACK_SPAN = 2048
GROUP = QUERY_HEADS // KEY_HEADS
GROUP_WIDTH = GROUP * HEAD_SIZE
TILE = 256
MASKED = -1e30
MARK_ROWS = 16


def ring_order(chips):
    return list(range(0, chips, 2)) + list(range(chips - 1, 0, -2))


def swap_cores(value):
    count = lax.axis_size("fsdp")
    return lax.ppermute(value, "fsdp", [(i, i ^ 1) for i in range(count)])


def swap_chips(value):
    count = lax.axis_size("fsdp")
    return lax.ppermute(value, "fsdp", [(i, i ^ 2) for i in range(count)])


def two_chips_on(value):
    count = lax.axis_size("fsdp")
    return lax.ppermute(value, "fsdp", [(i, i + 4) for i in range(count - 4)])


def to_next_section(value):
    count = lax.axis_size("section")
    return lax.ppermute(value, "section", [(i, (i + 1) % count) for i in range(count)])


def along_ring(value, step):
    chips = lax.axis_size("fsdp") // 2
    order = ring_order(chips)
    pairs = []
    for place in range(chips):
        target = order[(place + step) % chips]
        pairs += [(2 * order[place] + core, 2 * target + core) for core in range(2)]
    return lax.ppermute(value, "fsdp", pairs)


def run(kernel, outs, scalars, arrays, waits=(), aliases=None, scratch=()):
    whole = pl.BlockSpec(memory_space=pltpu.VMEM)
    taken = 1 + len(arrays)

    def only(*refs):
        kernel(*refs[:taken], *refs[taken + len(waits):])

    return pl.pallas_call(
        only,
        in_specs=[pl.BlockSpec(memory_space=pltpu.SMEM)] + [whole] * len(arrays)
        + [pl.BlockSpec(memory_space=pl.ANY)] * len(waits),
        out_specs=[whole] * len(outs),
        out_shape=[jax.ShapeDtypeStruct(shape, dtype) for shape, dtype in outs],
        scratch_shapes=list(scratch),
        input_output_aliases=aliases or {},
        compiler_params=pltpu.CompilerParams(vmem_limit_bytes=40 * 1024 * 1024),
        cost_estimate=pl.CostEstimate(flops=1000000, bytes_accessed=100000, transcendentals=0),
    )(scalars, *arrays, *waits)


def tied_kernel(*refs):
    pass


def after(value, *others):
    anywhere = pl.BlockSpec(memory_space=pl.ANY)
    return pl.pallas_call(
        tied_kernel,
        in_specs=[anywhere] * (1 + len(others)),
        out_specs=anywhere,
        out_shape=jax.ShapeDtypeStruct(value.shape, value.dtype),
        input_output_aliases={0: 0},
        cost_estimate=pl.CostEstimate(flops=0, bytes_accessed=0, transcendentals=0),
    )(value, *others)


def around(shard):
    chips = lax.axis_size("fsdp") // 2
    found, moving = {0: [(0, shard)]}, {1: shard, -1: shard}
    for step in range(1, (chips - 1) // 2 + 1):
        for way in (1, -1):
            moving[way] = along_ring(moving[way], way)
            found[-way * step % chips] = [(0, moving[way])]
    if chips % 2 == 0:
        half = shard.shape[0] // 2
        found[chips // 2] = [
            (0, along_ring(moving[1][:half], 1)), (half, along_ring(moving[-1][half:], -1))
        ]
    return found


def block(index, size):
    return pl.ds(pl.multiple_of(index * size, size), size)


def split_kernel(norm, scal_ref, rows_ref, kept_ref, sent_ref):
    core = scal_ref[0]
    count, width = rows_ref.shape
    size, some = 256, 64
    for first in range(0, count, some):
        at = slice(first, first + some)
        if norm:
            values = rows_ref[at, :].astype(jnp.float32)
            scale = lax.rsqrt(jnp.mean(values * values, axis=1, keepdims=True) + 1e-05)
        for j in range(width // (2 * size)):
            for out_ref, which in ((kept_ref, core), (sent_ref, 1 - core)):
                part = rows_ref[at, block(2 * j + which, size)]
                if norm:
                    part = (part.astype(jnp.float32) * scale).astype(jnp.bfloat16)
                out_ref[at, j * size:(j + 1) * size] = part


def keyval_kernel(scal_ref, segs_ref, own_ref, other_ref, weight_ref, kept_ref, sent_ref):
    core = scal_ref[0]
    rows = own_ref.shape[0]
    size = 256
    total = None
    for j in range(own_ref.shape[1] // size):
        for ref, which in ((own_ref, core), (other_ref, 1 - core)):
            found = jnp.dot(
                ref[:, j * size:(j + 1) * size], weight_ref[0, block(2 * j + which, size), :],
                preferred_element_type=jnp.float32,
            )
            total = found if total is None else total + found
    lane = lax.broadcasted_iota(jnp.int32, (rows, 128), 1)
    for part in range(2):
        low = total[:, part * 256:part * 256 + 128]
        high = total[:, part * 256 + 128:part * 256 + 256]
        zero = jnp.where(lane < HEAD_SIZE, low, pltpu.roll(high, HEAD_SIZE, 1))
        one = jnp.where(lane < HEAD_SIZE, pltpu.roll(low, HEAD_SIZE, 1), high)
        at = slice(part * 128, part * 128 + 128)
        kept_ref[:, at] = jnp.where(core == 0, zero, one).astype(kept_ref.dtype)
        sent_ref[:rows, at] = jnp.where(core == 0, one, zero).astype(sent_ref.dtype)
    marks = (segs_ref[...] + 1).astype(jnp.float32)
    sent_ref[rows:, :] = jnp.broadcast_to(marks, (MARK_ROWS, rows)).astype(sent_ref.dtype)


def parcel_kernel(scal_ref, segs_ref, kept_ref, received_ref, out_ref):
    core = scal_ref[0]
    rows = kept_ref.shape[0]
    out_ref[block(core, rows), :] = kept_ref[...]
    out_ref[block(1 - core, rows), :] = received_ref[:rows, :]
    own = (segs_ref[...] + 1).astype(jnp.float32)
    other = received_ref[rows:, :].astype(jnp.float32)[0:1, :]
    first, second = jnp.where(core == 0, own, other), jnp.where(core == 0, other, own)
    row = lax.broadcasted_iota(jnp.int32, (MARK_ROWS, rows), 0)
    marks = jnp.where(row == 0, first, jnp.where(row == 1, second, 0.0))
    out_ref[2 * rows:, :] = marks.astype(out_ref.dtype)


def window_kernel(scal_ref, four_ref, two_ref, own_ref, crossed_ref, kt_ref, v_ref, lo_ref):
    odd = scal_ref[1]
    length = own_ref.shape[0]
    count = length - MARK_ROWS
    half = count // 2
    second = pl.multiple_of(odd * length, MARK_ROWS)
    fourth = pl.multiple_of((1 - odd) * length, MARK_ROWS)
    places = [(four_ref, 0), (crossed_ref, second), (two_ref, 0), (crossed_ref, fourth), (own_ref, 0)]
    lane = lax.broadcasted_iota(jnp.int32, (count, 128), 1)
    blank = jnp.zeros((HEAD_SIZE, count), jnp.bfloat16)
    marks = []
    for i, (ref, first) in enumerate(places):
        at = slice(i * count, (i + 1) * count)
        keys = ref[pl.ds(first, count), 0:128].astype(jnp.float32).T.astype(jnp.bfloat16)
        values = ref[pl.ds(first, count), 128:256].astype(jnp.float32)
        turned = pltpu.roll(values, HEAD_SIZE, 1)
        for g in range(2):
            head = keys[g * HEAD_SIZE:(g + 1) * HEAD_SIZE]
            kt_ref[g, 0, :HEAD_SIZE, at] = head
            kt_ref[g, 0, HEAD_SIZE:, at] = blank
            kt_ref[g, 1, :HEAD_SIZE, at] = blank
            kt_ref[g, 1, HEAD_SIZE:, at] = head
            low, high = (values, turned) if g == 0 else (turned, values)
            v_ref[g, 0, at, :] = jnp.where(lane < HEAD_SIZE, low, 0.0).astype(jnp.bfloat16)
            v_ref[g, 1, at, :] = jnp.where(lane < HEAD_SIZE, 0.0, high).astype(jnp.bfloat16)
        found = ref[pl.ds(first + count, MARK_ROWS), :].astype(jnp.float32)
        marks += [found[0:1, :], found[1:2, :]]
    across = lax.broadcasted_iota(jnp.int32, (half, half), 1)
    down = lax.broadcasted_iota(jnp.int32, (half, half), 0)
    for part in range(2):
        mine = jnp.sum(jnp.where(across == down, marks[-2 + part], 0.0), axis=1, keepdims=True)
        earlier = jnp.zeros((half, half), jnp.float32)
        for row in marks:
            earlier = earlier + jnp.where(row < mine, 1.0, 0.0)
        earlier = jnp.sum(earlier, axis=1, keepdims=True).astype(jnp.int32)
        place = lax.broadcasted_iota(jnp.int32, (half, 128), 0) + (part * half + 1)
        lo_ref[part * half:(part + 1) * half, :] = jnp.maximum(earlier, place)


def query_kernel(pieces, g, more, scal_ref, own_ref, other_ref, *refs):
    weights, refs = refs[: len(pieces)], refs[len(pieces):]
    core = scal_ref[0]
    rows = own_ref.shape[0]
    outs = refs[-2:]
    for rows_ref, which in ((own_ref, core), (other_ref, 1 - core)):
        at = block(which, rows)
        for i, column in enumerate((core, 1 - core)):
            total = refs[i][at, :] if more else None
            for (distance, first), weight_ref in zip(pieces, weights):
                depth = weight_ref.shape[0]
                start = pl.multiple_of(scal_ref[2 + distance] * rows + first, depth)
                found = jnp.dot(
                    rows_ref[:, pl.ds(start, depth)], weight_ref[:, block(2 * g + column, GROUP_WIDTH)],
                    preferred_element_type=jnp.float32,
                )
                total = found if total is None else total + found
            outs[i][at, :] = total


def attention_kernel(lo_ref, kept_ref, received_ref, kt_ref, v_ref, out_ref, query_ref, score_ref):
    tile = pl.program_id(0)
    start = pl.multiple_of(tile * TILE, TILE)
    span = LOOKBACK_SPAN + TILE
    lo = lo_ref[...] - start
    lane = lax.broadcasted_iota(jnp.int32, (TILE, 128), 1)
    row = lax.broadcasted_iota(jnp.int32, (TILE, 128), 0)
    blocks = span // TILE
    queries = (kept_ref[...] + received_ref[...]).astype(jnp.bfloat16)
    query_ref[...] = queries * jnp.bfloat16(HEAD_SIZE ** -0.5)

    def scores_of(pair, parity):
        q = query_ref[:, pair * 128:(pair + 1) * 128]
        peak = jnp.full((TILE, 128), MASKED, jnp.float32)
        for i in range(blocks):
            first = pl.multiple_of(start + i * TILE, TILE)
            found = jnp.dot(q, kt_ref[parity, :, pl.ds(first, TILE)], preferred_element_type=jnp.float32)
            for part in range(TILE // 128):
                at = i * TILE + part * 128
                visible = lane + at >= lo
                if at >= LOOKBACK_SPAN:
                    visible = visible & (lane + (at - LOOKBACK_SPAN) <= row)
                kept = jnp.where(visible, found[:, part * 128:(part + 1) * 128], MASKED)
                peak = jnp.maximum(peak, kept)
                score_ref[parity, :, at:at + 128] = kept
        return jnp.max(peak, axis=1, keepdims=True)

    def mixed_of(parity, peak):
        total = jnp.zeros((TILE, 128), jnp.float32)
        mixed = jnp.zeros((TILE, 128), jnp.float32)
        for i in range(blocks):
            first = pl.multiple_of(start + i * TILE, TILE)
            weights = jnp.exp(score_ref[parity, :, i * TILE:(i + 1) * TILE] - peak)
            for part in range(TILE // 128):
                total = total + weights[:, part * 128:(part + 1) * 128]
            mixed = mixed + jnp.dot(
                weights.astype(jnp.bfloat16), v_ref[parity, pl.ds(first, TILE), :],
                preferred_element_type=jnp.float32,
            )
        return mixed * (1.0 / jnp.sum(total, axis=1, keepdims=True))

    for pair in range(GROUP // 2):
        peaks = [scores_of(pair, parity) for parity in range(2)]
        parts = [mixed_of(parity, peaks[parity]) for parity in range(2)]
        out_ref[:, pair * 128:(pair + 1) * 128] = (parts[0] + parts[1]).astype(out_ref.dtype)


def attention(lo, kept, received, keys_t, values, waits):
    rows = kept.shape[0]
    window = keys_t.shape[2]
    span = LOOKBACK_SPAN + TILE

    def only(*refs):
        attention_kernel(*refs[:5], *refs[5 + len(waits):])

    return pl.pallas_call(
        only,
        grid=(rows // TILE,),
        in_specs=[
            pl.BlockSpec((TILE, 128), lambda t: (t, 0)),
            pl.BlockSpec((TILE, GROUP_WIDTH), lambda t: (t, 0)),
            pl.BlockSpec((TILE, GROUP_WIDTH), lambda t: (t, 0)),
            pl.BlockSpec((2, 128, window), lambda t: (0, 0, 0)),
            pl.BlockSpec((2, window, 128), lambda t: (0, 0, 0)),
        ] + [pl.BlockSpec(memory_space=pl.ANY)] * len(waits),
        out_specs=pl.BlockSpec((TILE, GROUP_WIDTH), lambda t: (t, 0)),
        out_shape=jax.ShapeDtypeStruct((rows, GROUP_WIDTH), jnp.bfloat16),
        scratch_shapes=[
            pltpu.VMEM((TILE, GROUP_WIDTH), jnp.bfloat16), pltpu.VMEM((2, TILE, span), jnp.float32)
        ],
        compiler_params=pltpu.CompilerParams(vmem_limit_bytes=40 * 1024 * 1024),
        cost_estimate=pl.CostEstimate(flops=1000000, bytes_accessed=100000, transcendentals=0),
    )(lo, kept, received, keys_t, values, *waits)


def out_kernel(distances, mode, scal_ref, *refs):
    attended, refs = refs[:4], refs[4:]
    adds, refs = refs[:2], refs[2:]
    count = sum(len(pieces) for _, pieces in distances)
    weights, refs = refs[:count], refs[count:]
    outs = refs[-2:]
    core = scal_ref[0]
    rows = adds[0].shape[0]
    depth = attended[0].shape[1]
    if mode != "alone":
        for i in range(2):
            outs[i][...] = refs[i][...] if mode == "more" else jnp.zeros_like(outs[i])
    for i, which in enumerate((core, 1 - core)):
        taken = 0
        for distance, pieces in distances:
            shard = weights[taken:taken + len(pieces)]
            taken += len(pieces)
            columns = shard[0].shape[1]
            at = block(scal_ref[2 + distance], columns)
            total = adds[i][:, at].astype(jnp.float32)
            for g in range(2):
                ref, first = shard[g * len(shard) // 2], 2 * g if len(shard) == 1 else 0
                for side, column in enumerate((core, 1 - core)):
                    total = total + jnp.dot(
                        attended[2 * g + side][block(which, rows), :],
                        ref[block(first + column, depth), :],
                        preferred_element_type=jnp.float32,
                    )
            if mode == "alone":
                outs[i][...] = total.astype(outs[i].dtype)
            else:
                outs[i][:, at] = total.astype(outs[i].dtype)


def join_kernel(last, scal_ref, own_ref, other_ref, own_last_ref, other_last_ref, out_ref):
    core = scal_ref[0]
    size = own_last_ref.shape[1]
    for j in range(own_ref.shape[1] // size):
        at = slice(j * size, (j + 1) * size)
        out_ref[:, block(2 * j + core, size)] = own_ref[:, at]
        out_ref[:, block(2 * j + 1 - core, size)] = other_ref[:, at]
    j = scal_ref[2 + last]
    out_ref[:, block(2 * j + core, size)] = own_last_ref[...]
    out_ref[:, block(2 * j + 1 - core, size)] = other_last_ref[...]


def body(section_input, segment_ids, query_weight, keyval_weight, out_weight):
    hidden = section_input[0]
    rows, width = hidden.shape
    device = lax.axis_index("fsdp")
    chips = lax.axis_size("fsdp") // 2
    chip, core = device // 2, device % 2
    order = jnp.array(ring_order(chips), jnp.int32)
    place = jnp.argmax(order == chip).astype(jnp.int32)
    sources = order[(place + jnp.arange(chips, dtype=jnp.int32)) % chips]
    scalars = jnp.concatenate([jnp.stack([core, chip % 2]).astype(jnp.int32), sources])

    query_pieces = around(query_weight[0])
    keyval_full = lax.all_gather(keyval_weight, "fsdp", axis=1, tiled=True)

    half = ((rows, width // 2), jnp.bfloat16)
    own_rows, sent_rows = run(functools.partial(split_kernel, True), [half, half], scalars, [hidden])
    other_rows = swap_cores(sent_rows)
    out_shard = to_next_section(after(out_weight[0], own_rows))

    kept, sent = run(
        keyval_kernel, [((rows, 256), jnp.bfloat16), ((rows + MARK_ROWS, 256), jnp.bfloat16)],
        scalars, [segment_ids, own_rows, sent_rows, keyval_full],
    )
    parcel, = run(
        parcel_kernel, [((2 * rows + MARK_ROWS, 256), jnp.bfloat16)], scalars,
        [segment_ids, kept, swap_cores(sent)],
    )
    back_two = two_chips_on(parcel)
    back_four = two_chips_on(back_two)
    even = chip % 2 == 0
    crossed = swap_chips(jnp.concatenate([jnp.where(even, parcel, back_four), back_two], axis=0))
    window = 5 * 2 * rows
    keys_t, values, lowest = run(
        window_kernel,
        [((2, 2, 128, window), jnp.bfloat16), ((2, 2, window, 128), jnp.bfloat16), ((2 * rows, 128), jnp.int32)],
        scalars, [back_four, back_two, parcel, crossed],
    )

    def query_sums(distances, g, waits, before=()):
        pieces = [(d, first) for d in distances for first, _ in query_pieces[d]]
        shards = [shard for d in distances for _, shard in query_pieces[d]]
        return run(
            functools.partial(query_kernel, pieces, g, bool(before)),
            [((2 * rows, GROUP_WIDTH), jnp.float32)] * 2, scalars,
            [own_rows, other_rows] + shards + list(before), waits=waits,
        )

    near = [0, 1, chips - 1, 2, chips - 2]
    next_far = [3, chips - 3]
    far = [chips // 2]
    out_shard = after(out_shard, query_pieces[3][0][1], query_pieces[chips - 3][0][1])
    out_pieces = around(out_shard)
    sums = [query_sums(near, g, [parcel]) for g in range(2)]
    sums = [query_sums(next_far + far, g, [keys_t, out_shard], sums[g]) for g in range(2)]
    attended = []
    for g in range(2):
        waits = [out_pieces[d][0][1] for d in (1, chips - 1)] if g else []
        attended.append(attention(lowest, sums[g][0], swap_cores(sums[g][1]), keys_t[g], values[g], waits))
    attended[1] = after(attended[1], *[out_pieces[d][0][1] for d in (2, chips - 2)])
    kept, sent = run(
        functools.partial(split_kernel, False), [half, half], scalars, [to_next_section(hidden)]
    )
    adds = [kept, swap_cores(sent)]
    arrived = []
    for g in range(2):
        mine = to_next_section(attended[g])
        arrived += [mine, swap_cores(mine)]

    def made(some, mode, before=()):
        distances = [(d, [first for first, _ in out_pieces[d]]) for d in some]
        shards = [shard for d in some for _, shard in out_pieces[d]]
        outs = [((rows, out_shard.shape[1]), jnp.bfloat16)] * 2 if mode == "alone" else [half, half]
        taken = arrived + adds + shards
        aliases = {1 + len(taken) + i: i for i in range(2)} if before else {}
        return run(
            functools.partial(out_kernel, distances, mode), outs, scalars, taken + list(before), aliases=aliases
        )

    most = made(near, "first")
    most = made(next_far, "more", most)
    other_most = swap_cores(most[1])
    last = made(far, "alone")
    joined, = run(
        functools.partial(join_kernel, chips // 2), [((rows, width), jnp.bfloat16)], scalars,
        [most[0], other_most, last[0], swap_cores(last[1])],
    )
    return joined[None]


def solution(mesh):
    return jax.shard_map(
        body,
        mesh=mesh,
        in_specs=(
            P("section", "fsdp", None),
            P("section", "fsdp"),
            P("section", "fsdp", None),
            P("section", "fsdp", None),
            P("section", None, "fsdp"),
        ),
        out_specs=P("section", "fsdp", None),
        check_vma=False,
    )
```

```python
import functools

import jax
import jax.numpy as jnp
from jax import lax
from jax.experimental import pallas as pl
from jax.experimental.pallas import tpu as pltpu
from jax.sharding import PartitionSpec as P

QUERY_HEADS = 32
KEY_HEADS = 4
HEAD_SIZE = 64
LOOKBACK_SPAN = 2048
GROUP = QUERY_HEADS // KEY_HEADS
GROUP_WIDTH = GROUP * HEAD_SIZE
TILE = 256
MASKED = -1e30
MARK_ROWS = 16


def ring_order(chips):
    return list(range(0, chips, 2)) + list(range(chips - 1, 0, -2))


def swap_cores(value):
    count = lax.axis_size("fsdp")
    return lax.ppermute(value, "fsdp", [(i, i ^ 1) for i in range(count)])


def swap_chips(value):
    count = lax.axis_size("fsdp")
    return lax.ppermute(value, "fsdp", [(i, i ^ 2) for i in range(count)])


def two_chips_on(value):
    count = lax.axis_size("fsdp")
    return lax.ppermute(value, "fsdp", [(i, i + 4) for i in range(count - 4)])


def to_next_section(value):
    count = lax.axis_size("section")
    return lax.ppermute(value, "section", [(i, (i + 1) % count) for i in range(count)])


def along_ring(value, step):
    chips = lax.axis_size("fsdp") // 2
    order = ring_order(chips)
    pairs = []
    for place in range(chips):
        target = order[(place + step) % chips]
        pairs += [(2 * order[place] + core, 2 * target + core) for core in range(2)]
    return lax.ppermute(value, "fsdp", pairs)


def run(kernel, outs, scalars, arrays, waits=(), aliases=None, scratch=()):
    whole = pl.BlockSpec(memory_space=pltpu.VMEM)
    taken = 1 + len(arrays)

    def only(*refs):
        kernel(*refs[:taken], *refs[taken + len(waits):])

    return pl.pallas_call(
        only,
        in_specs=[pl.BlockSpec(memory_space=pltpu.SMEM)] + [whole] * len(arrays)
        + [pl.BlockSpec(memory_space=pl.ANY)] * len(waits),
        out_specs=[whole] * len(outs),
        out_shape=[jax.ShapeDtypeStruct(shape, dtype) for shape, dtype in outs],
        scratch_shapes=list(scratch),
        input_output_aliases=aliases or {},
        compiler_params=pltpu.CompilerParams(vmem_limit_bytes=40 * 1024 * 1024),
        cost_estimate=pl.CostEstimate(flops=1000000, bytes_accessed=100000, transcendentals=0),
    )(scalars, *arrays, *waits)


def tied_kernel(*refs):
    pass


def after(value, *others):
    anywhere = pl.BlockSpec(memory_space=pl.ANY)
    return pl.pallas_call(
        tied_kernel,
        in_specs=[anywhere] * (1 + len(others)),
        out_specs=anywhere,
        out_shape=jax.ShapeDtypeStruct(value.shape, value.dtype),
        input_output_aliases={0: 0},
        cost_estimate=pl.CostEstimate(flops=0, bytes_accessed=0, transcendentals=0),
    )(value, *others)


def around(shard, halved=True):
    chips = lax.axis_size("fsdp") // 2
    found, moving = {0: [(0, shard)]}, {1: shard, -1: shard}
    for step in range(1, (chips - 1) // 2 + 1):
        for way in (1, -1):
            moving[way] = along_ring(moving[way], way)
            found[-way * step % chips] = [(0, moving[way])]
    if chips % 2 == 0 and halved:
        half = shard.shape[0] // 2
        found[chips // 2] = [
            (0, along_ring(moving[1][:half], 1)), (half, along_ring(moving[-1][half:], -1))
        ]
    elif chips % 2 == 0:
        found[chips // 2] = [(0, along_ring(moving[1], 1))]
    return found


def block(index, size):
    return pl.ds(pl.multiple_of(index * size, size), size)


def split_kernel(norm, scal_ref, rows_ref, kept_ref, sent_ref):
    core = scal_ref[0]
    count, width = rows_ref.shape
    size, some = 256, 64
    for first in range(0, count, some):
        at = slice(first, first + some)
        if norm:
            values = rows_ref[at, :].astype(jnp.float32)
            scale = lax.rsqrt(jnp.mean(values * values, axis=1, keepdims=True) + 1e-05)
        for j in range(width // (2 * size)):
            for out_ref, which in ((kept_ref, core), (sent_ref, 1 - core)):
                part = rows_ref[at, block(2 * j + which, size)]
                if norm:
                    part = (part.astype(jnp.float32) * scale).astype(jnp.bfloat16)
                out_ref[at, j * size:(j + 1) * size] = part


def keyval_kernel(distances, scal_ref, segs_ref, own_ref, other_ref, *refs):
    weights, (kept_ref, sent_ref) = refs[: len(distances)], refs[len(distances):]
    core = scal_ref[0]
    rows = own_ref.shape[0]
    lane = lax.broadcasted_iota(jnp.int32, (rows, 128), 1)
    for rows_ref, which in ((own_ref, core), (other_ref, 1 - core)):
        total = None
        for distance, weight_ref in zip(distances, weights):
            found = jnp.dot(
                rows_ref[:, block(scal_ref[2 + distance], weight_ref.shape[0])], weight_ref[...],
                preferred_element_type=jnp.float32,
            )
            total = found if total is None else total + found
        for part in range(2):
            low = total[:, part * 256:part * 256 + 128]
            high = total[:, part * 256 + 128:part * 256 + 256]
            zero = jnp.where(lane < HEAD_SIZE, low, pltpu.roll(high, HEAD_SIZE, 1))
            one = jnp.where(lane < HEAD_SIZE, pltpu.roll(low, HEAD_SIZE, 1), high)
            at = slice(part * 128, part * 128 + 128)
            kept_ref[block(which, rows), at] = jnp.where(core == 0, zero, one)
            sent_ref[block(which, rows), at] = jnp.where(core == 0, one, zero)
    marks = (segs_ref[...] + 1).astype(jnp.float32)
    sent_ref[2 * rows:, :] = jnp.broadcast_to(marks, (8, marks.shape[1]))


def parcel_kernel(scal_ref, segs_ref, kept_ref, received_ref, out_ref):
    core = scal_ref[0]
    count = kept_ref.shape[0]
    out_ref[:count, :] = (kept_ref[...] + received_ref[:count, :]).astype(out_ref.dtype)
    own = (segs_ref[...] + 1).astype(jnp.float32)
    other = received_ref[count:count + 1, :]
    first, second = jnp.where(core == 0, own, other), jnp.where(core == 0, other, own)
    row = lax.broadcasted_iota(jnp.int32, (MARK_ROWS, own.shape[1]), 0)
    marks = jnp.where(row == 0, first, jnp.where(row == 1, second, 0.0))
    out_ref[count:, :] = marks.astype(out_ref.dtype)


def window_kernel(scal_ref, four_ref, two_ref, own_ref, crossed_ref, kt_ref, v_ref, lo_ref):
    odd = scal_ref[1]
    length = own_ref.shape[0]
    count = length - MARK_ROWS
    half = count // 2
    second = pl.multiple_of(odd * length, MARK_ROWS)
    fourth = pl.multiple_of((1 - odd) * length, MARK_ROWS)
    places = [(four_ref, 0), (crossed_ref, second), (two_ref, 0), (crossed_ref, fourth), (own_ref, 0)]
    lane = lax.broadcasted_iota(jnp.int32, (count, 128), 1)
    blank = jnp.zeros((HEAD_SIZE, count), jnp.bfloat16)
    marks = []
    for i, (ref, first) in enumerate(places):
        at = slice(i * count, (i + 1) * count)
        keys = ref[pl.ds(first, count), 0:128].astype(jnp.float32).T.astype(jnp.bfloat16)
        values = ref[pl.ds(first, count), 128:256].astype(jnp.float32)
        turned = pltpu.roll(values, HEAD_SIZE, 1)
        for g in range(2):
            head = keys[g * HEAD_SIZE:(g + 1) * HEAD_SIZE]
            kt_ref[g, 0, :HEAD_SIZE, at] = head
            kt_ref[g, 0, HEAD_SIZE:, at] = blank
            kt_ref[g, 1, :HEAD_SIZE, at] = blank
            kt_ref[g, 1, HEAD_SIZE:, at] = head
            low, high = (values, turned) if g == 0 else (turned, values)
            v_ref[g, 0, at, :] = jnp.where(lane < HEAD_SIZE, low, 0.0).astype(jnp.bfloat16)
            v_ref[g, 1, at, :] = jnp.where(lane < HEAD_SIZE, 0.0, high).astype(jnp.bfloat16)
        found = ref[pl.ds(first + count, MARK_ROWS), :].astype(jnp.float32)
        marks += [found[0:1, :], found[1:2, :]]
    across = lax.broadcasted_iota(jnp.int32, (half, half), 1)
    down = lax.broadcasted_iota(jnp.int32, (half, half), 0)
    for part in range(2):
        mine = jnp.sum(jnp.where(across == down, marks[-2 + part], 0.0), axis=1, keepdims=True)
        earlier = jnp.zeros((half, half), jnp.float32)
        for row in marks:
            earlier = earlier + jnp.where(row < mine, 1.0, 0.0)
        earlier = jnp.sum(earlier, axis=1, keepdims=True).astype(jnp.int32)
        place = lax.broadcasted_iota(jnp.int32, (half, 128), 0) + (part * half + 1)
        lo_ref[part * half:(part + 1) * half, :] = jnp.maximum(earlier, place)


def query_kernel(pieces, g, more, scal_ref, own_ref, other_ref, *refs):
    weights, refs = refs[: len(pieces)], refs[len(pieces):]
    core = scal_ref[0]
    rows = own_ref.shape[0]
    outs = refs[-2:]
    for rows_ref, which in ((own_ref, core), (other_ref, 1 - core)):
        at = block(which, rows)
        for i, column in enumerate((core, 1 - core)):
            total = refs[i][at, :] if more else None
            for (distance, first), weight_ref in zip(pieces, weights):
                depth = weight_ref.shape[0]
                start = pl.multiple_of(scal_ref[2 + distance] * rows + first, depth)
                found = jnp.dot(
                    rows_ref[:, pl.ds(start, depth)], weight_ref[:, block(2 * g + column, GROUP_WIDTH)],
                    preferred_element_type=jnp.float32,
                )
                total = found if total is None else total + found
            outs[i][at, :] = total


def attention_kernel(lo_ref, kept_ref, received_ref, kt_ref, v_ref, out_ref, query_ref, score_ref):
    tile = pl.program_id(0)
    start = pl.multiple_of(tile * TILE, TILE)
    span = LOOKBACK_SPAN + TILE
    lo = lo_ref[...] - start
    lane = lax.broadcasted_iota(jnp.int32, (TILE, 128), 1)
    row = lax.broadcasted_iota(jnp.int32, (TILE, 128), 0)
    blocks = span // TILE
    queries = (kept_ref[...] + received_ref[...]).astype(jnp.bfloat16)
    query_ref[...] = queries * jnp.bfloat16(HEAD_SIZE ** -0.5)

    def scores_of(pair, parity):
        q = query_ref[:, pair * 128:(pair + 1) * 128]
        peak = jnp.full((TILE, 128), MASKED, jnp.float32)
        for i in range(blocks):
            first = pl.multiple_of(start + i * TILE, TILE)
            found = jnp.dot(q, kt_ref[parity, :, pl.ds(first, TILE)], preferred_element_type=jnp.float32)
            for part in range(TILE // 128):
                at = i * TILE + part * 128
                visible = lane + at >= lo
                if at >= LOOKBACK_SPAN:
                    visible = visible & (lane + (at - LOOKBACK_SPAN) <= row)
                kept = jnp.where(visible, found[:, part * 128:(part + 1) * 128], MASKED)
                peak = jnp.maximum(peak, kept)
                score_ref[parity, :, at:at + 128] = kept
        return jnp.max(peak, axis=1, keepdims=True)

    def mixed_of(parity, peak):
        total = jnp.zeros((TILE, 128), jnp.float32)
        mixed = jnp.zeros((TILE, 128), jnp.float32)
        for i in range(blocks):
            first = pl.multiple_of(start + i * TILE, TILE)
            weights = jnp.exp(score_ref[parity, :, i * TILE:(i + 1) * TILE] - peak)
            for part in range(TILE // 128):
                total = total + weights[:, part * 128:(part + 1) * 128]
            mixed = mixed + jnp.dot(
                weights.astype(jnp.bfloat16), v_ref[parity, pl.ds(first, TILE), :],
                preferred_element_type=jnp.float32,
            )
        return mixed * (1.0 / jnp.sum(total, axis=1, keepdims=True))

    for pair in range(GROUP // 2):
        peaks = [scores_of(pair, parity) for parity in range(2)]
        parts = [mixed_of(parity, peaks[parity]) for parity in range(2)]
        out_ref[:, pair * 128:(pair + 1) * 128] = (parts[0] + parts[1]).astype(out_ref.dtype)


def attention(lo, kept, received, keys_t, values, waits):
    rows = kept.shape[0]
    window = keys_t.shape[2]
    span = LOOKBACK_SPAN + TILE

    def only(*refs):
        attention_kernel(*refs[:5], *refs[5 + len(waits):])

    return pl.pallas_call(
        only,
        grid=(rows // TILE,),
        in_specs=[
            pl.BlockSpec((TILE, 128), lambda t: (t, 0)),
            pl.BlockSpec((TILE, GROUP_WIDTH), lambda t: (t, 0)),
            pl.BlockSpec((TILE, GROUP_WIDTH), lambda t: (t, 0)),
            pl.BlockSpec((2, 128, window), lambda t: (0, 0, 0)),
            pl.BlockSpec((2, window, 128), lambda t: (0, 0, 0)),
        ] + [pl.BlockSpec(memory_space=pl.ANY)] * len(waits),
        out_specs=pl.BlockSpec((TILE, GROUP_WIDTH), lambda t: (t, 0)),
        out_shape=jax.ShapeDtypeStruct((rows, GROUP_WIDTH), jnp.bfloat16),
        scratch_shapes=[
            pltpu.VMEM((TILE, GROUP_WIDTH), jnp.bfloat16), pltpu.VMEM((2, TILE, span), jnp.float32)
        ],
        compiler_params=pltpu.CompilerParams(vmem_limit_bytes=40 * 1024 * 1024),
        cost_estimate=pl.CostEstimate(flops=1000000, bytes_accessed=100000, transcendentals=0),
    )(lo, kept, received, keys_t, values, *waits)


def out_kernel(distances, mode, scal_ref, *refs):
    attended, refs = refs[:4], refs[4:]
    adds, refs = refs[:2], refs[2:]
    count = sum(len(pieces) for _, pieces in distances)
    weights, refs = refs[:count], refs[count:]
    outs = refs[-2:]
    core = scal_ref[0]
    rows = adds[0].shape[0]
    depth = attended[0].shape[1]
    if mode != "alone":
        for i in range(2):
            outs[i][...] = refs[i][...] if mode == "more" else jnp.zeros_like(outs[i])
    for i, which in enumerate((core, 1 - core)):
        taken = 0
        for distance, pieces in distances:
            shard = weights[taken:taken + len(pieces)]
            taken += len(pieces)
            columns = shard[0].shape[1]
            at = block(scal_ref[2 + distance], columns)
            total = adds[i][:, at].astype(jnp.float32)
            for g in range(2):
                ref, first = shard[g * len(shard) // 2], 2 * g if len(shard) == 1 else 0
                for side, column in enumerate((core, 1 - core)):
                    total = total + jnp.dot(
                        attended[2 * g + side][block(which, rows), :],
                        ref[block(first + column, depth), :],
                        preferred_element_type=jnp.float32,
                    )
            if mode == "alone":
                outs[i][...] = total.astype(outs[i].dtype)
            else:
                outs[i][:, at] = total.astype(outs[i].dtype)


def join_kernel(last, scal_ref, own_ref, other_ref, own_last_ref, other_last_ref, out_ref):
    core = scal_ref[0]
    size = own_last_ref.shape[1]
    for j in range(own_ref.shape[1] // size):
        at = slice(j * size, (j + 1) * size)
        out_ref[:, block(2 * j + core, size)] = own_ref[:, at]
        out_ref[:, block(2 * j + 1 - core, size)] = other_ref[:, at]
    j = scal_ref[2 + last]
    out_ref[:, block(2 * j + core, size)] = own_last_ref[...]
    out_ref[:, block(2 * j + 1 - core, size)] = other_last_ref[...]


def body(section_input, segment_ids, query_weight, keyval_weight, out_weight):
    hidden = section_input[0]
    rows, width = hidden.shape
    device = lax.axis_index("fsdp")
    chips = lax.axis_size("fsdp") // 2
    chip, core = device // 2, device % 2
    order = jnp.array(ring_order(chips), jnp.int32)
    place = jnp.argmax(order == chip).astype(jnp.int32)
    sources = order[(place + jnp.arange(chips, dtype=jnp.int32)) % chips]
    scalars = jnp.concatenate([jnp.stack([core, chip % 2]).astype(jnp.int32), sources])

    keyval_pieces = around(keyval_weight[0], halved=False)
    query_pieces = around(query_weight[0])

    half = ((rows, width // 2), jnp.bfloat16)
    own_rows, sent_rows = run(functools.partial(split_kernel, True), [half, half], scalars, [hidden])
    other_rows = swap_cores(sent_rows)
    out_shard = to_next_section(out_weight[0])

    kept, sent = run(
        functools.partial(keyval_kernel, list(range(chips))),
        [((2 * rows, 256), jnp.float32), ((2 * rows + 8, 256), jnp.float32)],
        scalars, [segment_ids, own_rows, other_rows] + [keyval_pieces[d][0][1] for d in range(chips)],
    )
    parcel, = run(
        parcel_kernel, [((2 * rows + MARK_ROWS, 256), jnp.bfloat16)], scalars,
        [segment_ids, kept, swap_cores(sent)],
    )
    back_two = two_chips_on(parcel)
    back_four = two_chips_on(back_two)
    even = chip % 2 == 0
    crossed = swap_chips(jnp.concatenate([jnp.where(even, parcel, back_four), back_two], axis=0))
    window = 5 * 2 * rows
    keys_t, values, lowest = run(
        window_kernel,
        [((2, 2, 128, window), jnp.bfloat16), ((2, 2, window, 128), jnp.bfloat16), ((2 * rows, 128), jnp.int32)],
        scalars, [back_four, back_two, parcel, crossed],
    )

    def query_sums(distances, g, waits, before=()):
        pieces = [(d, first) for d in distances for first, _ in query_pieces[d]]
        shards = [shard for d in distances for _, shard in query_pieces[d]]
        return run(
            functools.partial(query_kernel, pieces, g, bool(before)),
            [((2 * rows, GROUP_WIDTH), jnp.float32)] * 2, scalars,
            [own_rows, other_rows] + shards + list(before), waits=waits,
        )

    near = [0, 1, chips - 1, 2, chips - 2]
    next_far = [3, chips - 3]
    far = [chips // 2]
    out_shard = after(out_shard, *[piece for _, piece in query_pieces[chips // 2]])
    out_pieces = around(out_shard)
    sums = [query_sums(near, g, [parcel]) for g in range(2)]
    sums = [query_sums(next_far + far, g, [keys_t, out_shard], sums[g]) for g in range(2)]
    attended = []
    for g in range(2):
        waits = [out_pieces[d][0][1] for d in (1, chips - 1)] if g else []
        attended.append(attention(lowest, sums[g][0], swap_cores(sums[g][1]), keys_t[g], values[g], waits))
    attended[1] = after(attended[1], *[out_pieces[d][0][1] for d in (2, chips - 2)])
    kept, sent = run(
        functools.partial(split_kernel, False), [half, half], scalars, [to_next_section(hidden)], waits=attended[:1]
    )
    adds = [kept, swap_cores(sent)]
    arrived = []
    for g in range(2):
        mine = to_next_section(attended[g])
        arrived += [mine, swap_cores(mine)]

    def made(some, mode, before=()):
        distances = [(d, [first for first, _ in out_pieces[d]]) for d in some]
        shards = [shard for d in some for _, shard in out_pieces[d]]
        outs = [((rows, out_shard.shape[1]), jnp.bfloat16)] * 2 if mode == "alone" else [half, half]
        taken = arrived + adds + shards
        aliases = {1 + len(taken) + i: i for i in range(2)} if before else {}
        return run(
            functools.partial(out_kernel, distances, mode), outs, scalars, taken + list(before), aliases=aliases
        )

    most = made(near, "first")
    most = made(next_far, "more", most)
    other_most = swap_cores(most[1])
    last = made(far, "alone")
    joined, = run(
        functools.partial(join_kernel, chips // 2), [((rows, width), jnp.bfloat16)], scalars,
        [most[0], other_most, last[0], swap_cores(last[1])],
    )
    return joined[None]


def solution(mesh):
    return jax.shard_map(
        body,
        mesh=mesh,
        in_specs=(
            P("section", "fsdp", None),
            P("section", "fsdp"),
            P("section", "fsdp", None),
            P("section", "fsdp", None),
            P("section", None, "fsdp"),
        ),
        out_specs=P("section", "fsdp", None),
        check_vma=False,
    )
```

```python
import functools

import jax
import jax.numpy as jnp
from jax import lax
from jax.experimental import pallas as pl
from jax.experimental.pallas import tpu as pltpu
from jax.sharding import PartitionSpec as P

QUERY_HEADS = 32
KEY_HEADS = 4
HEAD_SIZE = 64
LOOKBACK_SPAN = 2048
GROUP = QUERY_HEADS // KEY_HEADS
GROUP_WIDTH = GROUP * HEAD_SIZE
TILE = 256
MASKED = -1e30
MARK_ROWS = 16


def ring_order(chips):
    return list(range(0, chips, 2)) + list(range(chips - 1, 0, -2))


def swap_cores(value):
    count = lax.axis_size("fsdp")
    return lax.ppermute(value, "fsdp", [(i, i ^ 1) for i in range(count)])


def swap_chips(value):
    count = lax.axis_size("fsdp")
    return lax.ppermute(value, "fsdp", [(i, i ^ 2) for i in range(count)])


def two_chips_on(value):
    count = lax.axis_size("fsdp")
    return lax.ppermute(value, "fsdp", [(i, i + 4) for i in range(count - 4)])


def to_next_section(value):
    count = lax.axis_size("section")
    return lax.ppermute(value, "section", [(i, (i + 1) % count) for i in range(count)])


def from_section_before(value):
    if lax.axis_size("section") != 2:
        return to_next_section(value)
    both = lax.all_gather(value, "section", axis=0, tiled=False)
    return lax.dynamic_index_in_dim(both, 1 - lax.axis_index("section"), 0, keepdims=False)


def along_ring(value, step):
    chips = lax.axis_size("fsdp") // 2
    order = ring_order(chips)
    pairs = []
    for place in range(chips):
        target = order[(place + step) % chips]
        pairs += [(2 * order[place] + core, 2 * target + core) for core in range(2)]
    return lax.ppermute(value, "fsdp", pairs)


def run(kernel, outs, scalars, arrays, waits=(), aliases=None, scratch=()):
    whole = pl.BlockSpec(memory_space=pltpu.VMEM)
    taken = 1 + len(arrays)

    def only(*refs):
        kernel(*refs[:taken], *refs[taken + len(waits):])

    return pl.pallas_call(
        only,
        in_specs=[pl.BlockSpec(memory_space=pltpu.SMEM)] + [whole] * len(arrays)
        + [pl.BlockSpec(memory_space=pl.ANY)] * len(waits),
        out_specs=[whole] * len(outs),
        out_shape=[jax.ShapeDtypeStruct(shape, dtype) for shape, dtype in outs],
        scratch_shapes=list(scratch),
        input_output_aliases=aliases or {},
        compiler_params=pltpu.CompilerParams(vmem_limit_bytes=40 * 1024 * 1024),
        cost_estimate=pl.CostEstimate(flops=1000000, bytes_accessed=100000, transcendentals=0),
    )(scalars, *arrays, *waits)


def tied_kernel(*refs):
    pass


def after(value, *others):
    anywhere = pl.BlockSpec(memory_space=pl.ANY)
    return pl.pallas_call(
        tied_kernel,
        in_specs=[anywhere] * (1 + len(others)),
        out_specs=anywhere,
        out_shape=jax.ShapeDtypeStruct(value.shape, value.dtype),
        input_output_aliases={0: 0},
        cost_estimate=pl.CostEstimate(flops=0, bytes_accessed=0, transcendentals=0),
    )(value, *others)


def around(shard, halved=True):
    chips = lax.axis_size("fsdp") // 2
    found, moving = {0: [(0, shard)]}, {1: shard, -1: shard}
    for step in range(1, (chips - 1) // 2 + 1):
        for way in (1, -1):
            moving[way] = along_ring(moving[way], way)
            found[-way * step % chips] = [(0, moving[way])]
    if chips % 2 == 0 and halved:
        half = shard.shape[0] // 2
        found[chips // 2] = [
            (0, along_ring(moving[1][:half], 1)), (half, along_ring(moving[-1][half:], -1))
        ]
    elif chips % 2 == 0:
        found[chips // 2] = [(0, along_ring(moving[1], 1))]
    return found


def block(index, size):
    return pl.ds(pl.multiple_of(index * size, size), size)


def split_kernel(norm, scal_ref, rows_ref, kept_ref, sent_ref):
    core = scal_ref[0]
    count, width = rows_ref.shape
    size, some = 256, 64
    for first in range(0, count, some):
        at = slice(first, first + some)
        if norm:
            values = rows_ref[at, :].astype(jnp.float32)
            scale = lax.rsqrt(jnp.mean(values * values, axis=1, keepdims=True) + 1e-05)
        for j in range(width // (2 * size)):
            for out_ref, which in ((kept_ref, core), (sent_ref, 1 - core)):
                part = rows_ref[at, block(2 * j + which, size)]
                if norm:
                    part = (part.astype(jnp.float32) * scale).astype(jnp.bfloat16)
                out_ref[at, j * size:(j + 1) * size] = part


def keyval_kernel(distances, scal_ref, segs_ref, own_ref, other_ref, *refs):
    weights, (kept_ref, sent_ref) = refs[: len(distances)], refs[len(distances):]
    core = scal_ref[0]
    rows = own_ref.shape[0]
    lane = lax.broadcasted_iota(jnp.int32, (rows, 128), 1)
    for rows_ref, which in ((own_ref, core), (other_ref, 1 - core)):
        total = None
        for distance, weight_ref in zip(distances, weights):
            found = jnp.dot(
                rows_ref[:, block(scal_ref[2 + distance], weight_ref.shape[0])], weight_ref[...],
                preferred_element_type=jnp.float32,
            )
            total = found if total is None else total + found
        for part in range(2):
            low = total[:, part * 256:part * 256 + 128]
            high = total[:, part * 256 + 128:part * 256 + 256]
            zero = jnp.where(lane < HEAD_SIZE, low, pltpu.roll(high, HEAD_SIZE, 1))
            one = jnp.where(lane < HEAD_SIZE, pltpu.roll(low, HEAD_SIZE, 1), high)
            at = slice(part * 128, part * 128 + 128)
            kept_ref[block(which, rows), at] = jnp.where(core == 0, zero, one)
            sent_ref[block(which, rows), at] = jnp.where(core == 0, one, zero)
    marks = (segs_ref[...] + 1).astype(jnp.float32)
    sent_ref[2 * rows:, :] = jnp.broadcast_to(marks, (8, marks.shape[1]))


def parcel_kernel(scal_ref, segs_ref, kept_ref, received_ref, out_ref):
    core = scal_ref[0]
    count = kept_ref.shape[0]
    out_ref[:count, :] = (kept_ref[...] + received_ref[:count, :]).astype(out_ref.dtype)
    own = (segs_ref[...] + 1).astype(jnp.float32)
    other = received_ref[count:count + 1, :]
    first, second = jnp.where(core == 0, own, other), jnp.where(core == 0, other, own)
    row = lax.broadcasted_iota(jnp.int32, (MARK_ROWS, own.shape[1]), 0)
    marks = jnp.where(row == 0, first, jnp.where(row == 1, second, 0.0))
    out_ref[count:, :] = marks.astype(out_ref.dtype)


def window_kernel(scal_ref, four_ref, two_ref, own_ref, crossed_ref, kt_ref, v_ref, lo_ref):
    odd = scal_ref[1]
    length = own_ref.shape[0]
    count = length - MARK_ROWS
    half = count // 2
    second = pl.multiple_of(odd * length, MARK_ROWS)
    fourth = pl.multiple_of((1 - odd) * length, MARK_ROWS)
    places = [(four_ref, 0), (crossed_ref, second), (two_ref, 0), (crossed_ref, fourth), (own_ref, 0)]
    lane = lax.broadcasted_iota(jnp.int32, (count, 128), 1)
    blank = jnp.zeros((HEAD_SIZE, count), jnp.bfloat16)
    marks = []
    for i, (ref, first) in enumerate(places):
        at = slice(i * count, (i + 1) * count)
        keys = ref[pl.ds(first, count), 0:128].astype(jnp.float32).T.astype(jnp.bfloat16)
        values = ref[pl.ds(first, count), 128:256].astype(jnp.float32)
        turned = pltpu.roll(values, HEAD_SIZE, 1)
        for g in range(2):
            head = keys[g * HEAD_SIZE:(g + 1) * HEAD_SIZE]
            kt_ref[g, 0, :HEAD_SIZE, at] = head
            kt_ref[g, 0, HEAD_SIZE:, at] = blank
            kt_ref[g, 1, :HEAD_SIZE, at] = blank
            kt_ref[g, 1, HEAD_SIZE:, at] = head
            low, high = (values, turned) if g == 0 else (turned, values)
            v_ref[g, 0, at, :] = jnp.where(lane < HEAD_SIZE, low, 0.0).astype(jnp.bfloat16)
            v_ref[g, 1, at, :] = jnp.where(lane < HEAD_SIZE, 0.0, high).astype(jnp.bfloat16)
        found = ref[pl.ds(first + count, MARK_ROWS), :].astype(jnp.float32)
        marks += [found[0:1, :], found[1:2, :]]
    across = lax.broadcasted_iota(jnp.int32, (half, half), 1)
    down = lax.broadcasted_iota(jnp.int32, (half, half), 0)
    for part in range(2):
        mine = jnp.sum(jnp.where(across == down, marks[-2 + part], 0.0), axis=1, keepdims=True)
        earlier = jnp.zeros((half, half), jnp.float32)
        for row in marks:
            earlier = earlier + jnp.where(row < mine, 1.0, 0.0)
        earlier = jnp.sum(earlier, axis=1, keepdims=True).astype(jnp.int32)
        place = lax.broadcasted_iota(jnp.int32, (half, 128), 0) + (part * half + 1)
        lo_ref[part * half:(part + 1) * half, :] = jnp.maximum(earlier, place)


def query_kernel(pieces, g, more, scal_ref, own_ref, other_ref, *refs):
    weights, refs = refs[: len(pieces)], refs[len(pieces):]
    core = scal_ref[0]
    rows = own_ref.shape[0]
    outs = refs[-2:]
    for rows_ref, which in ((own_ref, core), (other_ref, 1 - core)):
        at = block(which, rows)
        for i, column in enumerate((core, 1 - core)):
            total = refs[i][at, :] if more else None
            for (distance, first), weight_ref in zip(pieces, weights):
                depth = weight_ref.shape[0]
                start = pl.multiple_of(scal_ref[2 + distance] * rows + first, depth)
                found = jnp.dot(
                    rows_ref[:, pl.ds(start, depth)], weight_ref[:, block(2 * g + column, GROUP_WIDTH)],
                    preferred_element_type=jnp.float32,
                )
                total = found if total is None else total + found
            outs[i][at, :] = total


def attention_kernel(lo_ref, kept_ref, received_ref, kt_ref, v_ref, out_ref, query_ref, score_ref):
    tile = pl.program_id(0)
    start = pl.multiple_of(tile * TILE, TILE)
    span = LOOKBACK_SPAN + TILE
    lo = lo_ref[...] - start
    lane = lax.broadcasted_iota(jnp.int32, (TILE, 128), 1)
    row = lax.broadcasted_iota(jnp.int32, (TILE, 128), 0)
    blocks = span // TILE
    queries = (kept_ref[...] + received_ref[...]).astype(jnp.bfloat16)
    query_ref[...] = queries * jnp.bfloat16(HEAD_SIZE ** -0.5)

    def scores_of(pair, parity):
        q = query_ref[:, pair * 128:(pair + 1) * 128]
        peak = jnp.full((TILE, 128), MASKED, jnp.float32)
        for i in range(blocks):
            first = pl.multiple_of(start + i * TILE, TILE)
            found = jnp.dot(q, kt_ref[parity, :, pl.ds(first, TILE)], preferred_element_type=jnp.float32)
            for part in range(TILE // 128):
                at = i * TILE + part * 128
                visible = lane + at >= lo
                if at >= LOOKBACK_SPAN:
                    visible = visible & (lane + (at - LOOKBACK_SPAN) <= row)
                kept = jnp.where(visible, found[:, part * 128:(part + 1) * 128], MASKED)
                peak = jnp.maximum(peak, kept)
                score_ref[parity, :, at:at + 128] = kept
        return jnp.max(peak, axis=1, keepdims=True)

    def mixed_of(parity, peak):
        total = jnp.zeros((TILE, 128), jnp.float32)
        mixed = jnp.zeros((TILE, 128), jnp.float32)
        for i in range(blocks):
            first = pl.multiple_of(start + i * TILE, TILE)
            weights = jnp.exp(score_ref[parity, :, i * TILE:(i + 1) * TILE] - peak)
            for part in range(TILE // 128):
                total = total + weights[:, part * 128:(part + 1) * 128]
            mixed = mixed + jnp.dot(
                weights.astype(jnp.bfloat16), v_ref[parity, pl.ds(first, TILE), :],
                preferred_element_type=jnp.float32,
            )
        return mixed * (1.0 / jnp.sum(total, axis=1, keepdims=True))

    for pair in range(GROUP // 2):
        peaks = [scores_of(pair, parity) for parity in range(2)]
        parts = [mixed_of(parity, peaks[parity]) for parity in range(2)]
        out_ref[:, pair * 128:(pair + 1) * 128] = (parts[0] + parts[1]).astype(out_ref.dtype)


def attention(lo, kept, received, keys_t, values, waits):
    rows = kept.shape[0]
    window = keys_t.shape[2]
    span = LOOKBACK_SPAN + TILE

    def only(*refs):
        attention_kernel(*refs[:5], *refs[5 + len(waits):])

    return pl.pallas_call(
        only,
        grid=(rows // TILE,),
        in_specs=[
            pl.BlockSpec((TILE, 128), lambda t: (t, 0)),
            pl.BlockSpec((TILE, GROUP_WIDTH), lambda t: (t, 0)),
            pl.BlockSpec((TILE, GROUP_WIDTH), lambda t: (t, 0)),
            pl.BlockSpec((2, 128, window), lambda t: (0, 0, 0)),
            pl.BlockSpec((2, window, 128), lambda t: (0, 0, 0)),
        ] + [pl.BlockSpec(memory_space=pl.ANY)] * len(waits),
        out_specs=pl.BlockSpec((TILE, GROUP_WIDTH), lambda t: (t, 0)),
        out_shape=jax.ShapeDtypeStruct((rows, GROUP_WIDTH), jnp.bfloat16),
        scratch_shapes=[
            pltpu.VMEM((TILE, GROUP_WIDTH), jnp.bfloat16), pltpu.VMEM((2, TILE, span), jnp.float32)
        ],
        compiler_params=pltpu.CompilerParams(vmem_limit_bytes=40 * 1024 * 1024),
        cost_estimate=pl.CostEstimate(flops=1000000, bytes_accessed=100000, transcendentals=0),
    )(lo, kept, received, keys_t, values, *waits)


def out_kernel(distances, mode, scal_ref, *refs):
    attended, refs = refs[:4], refs[4:]
    adds, refs = refs[:2], refs[2:]
    count = sum(len(pieces) for _, pieces in distances)
    weights, refs = refs[:count], refs[count:]
    outs = refs[-2:]
    core = scal_ref[0]
    rows = adds[0].shape[0]
    depth = attended[0].shape[1]
    if mode != "alone":
        for i in range(2):
            outs[i][...] = refs[i][...] if mode == "more" else jnp.zeros_like(outs[i])
    for i, which in enumerate((core, 1 - core)):
        taken = 0
        for distance, pieces in distances:
            shard = weights[taken:taken + len(pieces)]
            taken += len(pieces)
            columns = shard[0].shape[1]
            at = block(scal_ref[2 + distance], columns)
            total = adds[i][:, at].astype(jnp.float32)
            for g in range(2):
                ref, first = shard[g * len(shard) // 2], 2 * g if len(shard) == 1 else 0
                for side, column in enumerate((core, 1 - core)):
                    total = total + jnp.dot(
                        attended[2 * g + side][block(which, rows), :],
                        ref[block(first + column, depth), :],
                        preferred_element_type=jnp.float32,
                    )
            if mode == "alone":
                outs[i][...] = total.astype(outs[i].dtype)
            else:
                outs[i][:, at] = total.astype(outs[i].dtype)


def join_kernel(last, scal_ref, own_ref, other_ref, own_last_ref, other_last_ref, out_ref):
    core = scal_ref[0]
    size = own_last_ref.shape[1]
    for j in range(own_ref.shape[1] // size):
        at = slice(j * size, (j + 1) * size)
        out_ref[:, block(2 * j + core, size)] = own_ref[:, at]
        out_ref[:, block(2 * j + 1 - core, size)] = other_ref[:, at]
    j = scal_ref[2 + last]
    out_ref[:, block(2 * j + core, size)] = own_last_ref[...]
    out_ref[:, block(2 * j + 1 - core, size)] = other_last_ref[...]


def body(section_input, segment_ids, query_weight, keyval_weight, out_weight):
    hidden = section_input[0]
    rows, width = hidden.shape
    device = lax.axis_index("fsdp")
    chips = lax.axis_size("fsdp") // 2
    chip, core = device // 2, device % 2
    order = jnp.array(ring_order(chips), jnp.int32)
    place = jnp.argmax(order == chip).astype(jnp.int32)
    sources = order[(place + jnp.arange(chips, dtype=jnp.int32)) % chips]
    scalars = jnp.concatenate([jnp.stack([core, chip % 2]).astype(jnp.int32), sources])

    keyval_pieces = around(keyval_weight[0], halved=False)
    query_pieces = around(after(query_weight[0], keyval_pieces[chips // 2][0][1]))

    half = ((rows, width // 2), jnp.bfloat16)
    own_rows, sent_rows = run(functools.partial(split_kernel, True), [half, half], scalars, [hidden])
    other_rows = swap_cores(sent_rows)
    out_shard = from_section_before(out_weight[0])

    kept, sent = run(
        functools.partial(keyval_kernel, list(range(chips))),
        [((2 * rows, 256), jnp.float32), ((2 * rows + 8, 256), jnp.float32)],
        scalars, [segment_ids, own_rows, other_rows] + [keyval_pieces[d][0][1] for d in range(chips)],
    )
    parcel, = run(
        parcel_kernel, [((2 * rows + MARK_ROWS, 256), jnp.bfloat16)], scalars,
        [segment_ids, kept, swap_cores(sent)],
    )
    steps = [[query_pieces[d][0][1] for d in (step, chips - step)] for step in range(1, 4)]
    back_two = after(two_chips_on(parcel), *steps[0])
    back_four = after(two_chips_on(back_two), *steps[1])
    even = chip % 2 == 0
    crossed = swap_chips(jnp.concatenate([jnp.where(even, parcel, back_four), back_two], axis=0))
    window = 5 * 2 * rows
    keys_t, values, lowest = run(
        window_kernel,
        [((2, 2, 128, window), jnp.bfloat16), ((2, 2, window, 128), jnp.bfloat16), ((2 * rows, 128), jnp.int32)],
        scalars, [back_four, back_two, parcel, crossed], waits=steps[2],
    )

    def query_sums(distances, g, waits, before=()):
        pieces = [(d, first) for d in distances for first, _ in query_pieces[d]]
        shards = [shard for d in distances for _, shard in query_pieces[d]]
        return run(
            functools.partial(query_kernel, pieces, g, bool(before)),
            [((2 * rows, GROUP_WIDTH), jnp.float32)] * 2, scalars,
            [own_rows, other_rows] + shards + list(before), waits=waits,
        )

    near = [0, 1, chips - 1, 2, chips - 2]
    next_far = [3, chips - 3]
    far = [chips // 2]
    out_shard = after(out_shard, *[piece for _, piece in query_pieces[chips // 2]])
    out_pieces = around(out_shard)
    sums = [query_sums(near, g, [parcel]) for g in range(2)]
    sums = [query_sums(next_far + far, g, [keys_t, out_shard], sums[g]) for g in range(2)]
    attended = []
    for g in range(2):
        waits = [out_pieces[d][0][1] for d in (1, chips - 1)] if g else []
        attended.append(attention(lowest, sums[g][0], swap_cores(sums[g][1]), keys_t[g], values[g], waits))
    attended[1] = after(attended[1], *[out_pieces[d][0][1] for d in (2, chips - 2)])
    kept, sent = run(
        functools.partial(split_kernel, False), [half, half], scalars, [from_section_before(hidden)], waits=attended[:1]
    )
    adds = [kept, swap_cores(sent)]
    arrived = []
    for g in range(2):
        mine = to_next_section(attended[g])
        arrived += [mine, swap_cores(mine)]

    def made(some, mode, before=()):
        distances = [(d, [first for first, _ in out_pieces[d]]) for d in some]
        shards = [shard for d in some for _, shard in out_pieces[d]]
        outs = [((rows, out_shard.shape[1]), jnp.bfloat16)] * 2 if mode == "alone" else [half, half]
        taken = arrived + adds + shards
        aliases = {1 + len(taken) + i: i for i in range(2)} if before else {}
        return run(
            functools.partial(out_kernel, distances, mode), outs, scalars, taken + list(before), aliases=aliases
        )

    most = made(near, "first")
    most = made(next_far, "more", most)
    other_most = swap_cores(most[1])
    last = made(far, "alone")
    joined, = run(
        functools.partial(join_kernel, chips // 2), [((rows, width), jnp.bfloat16)], scalars,
        [most[0], other_most, last[0], swap_cores(last[1])],
    )
    return joined[None]


def solution(mesh):
    return jax.shard_map(
        body,
        mesh=mesh,
        in_specs=(
            P("section", "fsdp", None),
            P("section", "fsdp"),
            P("section", "fsdp", None),
            P("section", "fsdp", None),
            P("section", None, "fsdp"),
        ),
        out_specs=P("section", "fsdp", None),
        check_vma=False,
    )
```

```python
import functools

import jax
import jax.numpy as jnp
from jax import lax
from jax.experimental import pallas as pl
from jax.experimental.pallas import tpu as pltpu
from jax.sharding import PartitionSpec as P

QUERY_HEADS = 32
KEY_HEADS = 4
HEAD_SIZE = 64
LOOKBACK_SPAN = 2048
GROUP = QUERY_HEADS // KEY_HEADS
GROUP_WIDTH = GROUP * HEAD_SIZE
TILE = 256
MASKED = -1e30
MARK_ROWS = 16


def ring_order(chips):
    return list(range(0, chips, 2)) + list(range(chips - 1, 0, -2))


def swap_cores(value):
    count = lax.axis_size("fsdp")
    return lax.ppermute(value, "fsdp", [(i, i ^ 1) for i in range(count)])


def gathered(value):
    count = lax.axis_size("fsdp")
    groups = [list(range(core, count, 2)) for core in range(2)]
    return lax.all_gather(value, "fsdp", axis=0, tiled=False, axis_index_groups=groups)


def to_next_section(value):
    count = lax.axis_size("section")
    return lax.ppermute(value, "section", [(i, (i + 1) % count) for i in range(count)])


def from_section_before(value):
    if lax.axis_size("section") != 2:
        return to_next_section(value)
    both = lax.all_gather(value, "section", axis=0, tiled=False)
    return lax.dynamic_index_in_dim(both, 1 - lax.axis_index("section"), 0, keepdims=False)


def along_ring(value, step):
    chips = lax.axis_size("fsdp") // 2
    order = ring_order(chips)
    pairs = []
    for place in range(chips):
        target = order[(place + step) % chips]
        pairs += [(2 * order[place] + core, 2 * target + core) for core in range(2)]
    return lax.ppermute(value, "fsdp", pairs)


def run(kernel, outs, scalars, arrays, waits=(), aliases=None, scratch=()):
    whole = pl.BlockSpec(memory_space=pltpu.VMEM)
    taken = 1 + len(arrays)

    def only(*refs):
        kernel(*refs[:taken], *refs[taken + len(waits):])

    return pl.pallas_call(
        only,
        in_specs=[pl.BlockSpec(memory_space=pltpu.SMEM)] + [whole] * len(arrays)
        + [pl.BlockSpec(memory_space=pl.ANY)] * len(waits),
        out_specs=[whole] * len(outs),
        out_shape=[jax.ShapeDtypeStruct(shape, dtype) for shape, dtype in outs],
        scratch_shapes=list(scratch),
        input_output_aliases=aliases or {},
        compiler_params=pltpu.CompilerParams(vmem_limit_bytes=40 * 1024 * 1024),
        cost_estimate=pl.CostEstimate(flops=1000000, bytes_accessed=100000, transcendentals=0),
    )(scalars, *arrays, *waits)


def tied_kernel(*refs):
    pass


def after(value, *others):
    anywhere = pl.BlockSpec(memory_space=pl.ANY)
    return pl.pallas_call(
        tied_kernel,
        in_specs=[anywhere] * (1 + len(others)),
        out_specs=anywhere,
        out_shape=jax.ShapeDtypeStruct(value.shape, value.dtype),
        input_output_aliases={0: 0},
        cost_estimate=pl.CostEstimate(flops=0, bytes_accessed=0, transcendentals=0),
    )(value, *others)


def around(shard, halved=True):
    chips = lax.axis_size("fsdp") // 2
    found, moving = {0: [(0, shard)]}, {1: shard, -1: shard}
    for step in range(1, (chips - 1) // 2 + 1):
        for way in (1, -1):
            moving[way] = along_ring(moving[way], way)
            found[-way * step % chips] = [(0, moving[way])]
    if chips % 2 == 0 and halved:
        half = shard.shape[0] // 2
        found[chips // 2] = [
            (0, along_ring(moving[1][:half], 1)), (half, along_ring(moving[-1][half:], -1))
        ]
    elif chips % 2 == 0:
        found[chips // 2] = [(0, along_ring(moving[1], 1))]
    return found


def block(index, size):
    return pl.ds(pl.multiple_of(index * size, size), size)


def split_kernel(norm, scal_ref, rows_ref, kept_ref, sent_ref):
    core = scal_ref[0]
    count, width = rows_ref.shape
    size, some = 256, 64
    for first in range(0, count, some):
        at = slice(first, first + some)
        if norm:
            values = rows_ref[at, :].astype(jnp.float32)
            scale = lax.rsqrt(jnp.mean(values * values, axis=1, keepdims=True) + 1e-05)
        for j in range(width // (2 * size)):
            for out_ref, which in ((kept_ref, core), (sent_ref, 1 - core)):
                part = rows_ref[at, block(2 * j + which, size)]
                if norm:
                    part = (part.astype(jnp.float32) * scale).astype(jnp.bfloat16)
                out_ref[at, j * size:(j + 1) * size] = part


def keyval_kernel(distances, scal_ref, segs_ref, own_ref, other_ref, *refs):
    weights, (kept_ref, sent_ref) = refs[: len(distances)], refs[len(distances):]
    core = scal_ref[0]
    rows = own_ref.shape[0]
    lane = lax.broadcasted_iota(jnp.int32, (rows, 128), 1)
    for rows_ref, which in ((own_ref, core), (other_ref, 1 - core)):
        total = None
        for distance, weight_ref in zip(distances, weights):
            found = jnp.dot(
                rows_ref[:, block(scal_ref[2 + distance], weight_ref.shape[0])], weight_ref[...],
                preferred_element_type=jnp.float32,
            )
            total = found if total is None else total + found
        for part in range(2):
            low = total[:, part * 256:part * 256 + 128]
            high = total[:, part * 256 + 128:part * 256 + 256]
            zero = jnp.where(lane < HEAD_SIZE, low, pltpu.roll(high, HEAD_SIZE, 1))
            one = jnp.where(lane < HEAD_SIZE, pltpu.roll(low, HEAD_SIZE, 1), high)
            at = slice(part * 128, part * 128 + 128)
            kept_ref[block(which, rows), at] = jnp.where(core == 0, zero, one)
            sent_ref[block(which, rows), at] = jnp.where(core == 0, one, zero)
    marks = (segs_ref[...] + 1).astype(jnp.float32)
    sent_ref[2 * rows:, :] = jnp.broadcast_to(marks, (8, marks.shape[1]))


def parcel_kernel(scal_ref, segs_ref, kept_ref, received_ref, out_ref):
    core = scal_ref[0]
    count = kept_ref.shape[0]
    out_ref[:count, :] = (kept_ref[...] + received_ref[:count, :]).astype(out_ref.dtype)
    own = (segs_ref[...] + 1).astype(jnp.float32)
    other = received_ref[count:count + 1, :]
    first, second = jnp.where(core == 0, own, other), jnp.where(core == 0, other, own)
    row = lax.broadcasted_iota(jnp.int32, (MARK_ROWS, own.shape[1]), 0)
    marks = jnp.where(row == 0, first, jnp.where(row == 1, second, 0.0))
    out_ref[count:, :] = marks.astype(out_ref.dtype)


def copy_kernel(scal_ref, in_ref, out_ref):
    out_ref[...] = in_ref[...]


def window_kernel(back, scal_ref, parcels_ref, *refs):
    kt_refs, v_refs, lo_ref = refs[:2], refs[2:4], refs[4]
    chip = scal_ref[1]
    count = parcels_ref.shape[1] - MARK_ROWS
    half = count // 2
    lane = lax.broadcasted_iota(jnp.int32, (count, 128), 1)
    blank = jnp.zeros((HEAD_SIZE, count), jnp.bfloat16)
    marks = []
    for i in range(back + 1):
        source = chip - back + i
        ref = parcels_ref.at[jnp.maximum(source, 0)]
        at = slice(i * count, (i + 1) * count)
        keys = ref[:count, 0:128].astype(jnp.float32).T.astype(jnp.bfloat16)
        values = ref[:count, 128:256].astype(jnp.float32)
        turned = pltpu.roll(values, HEAD_SIZE, 1)
        for g in range(2):
            head = keys[g * HEAD_SIZE:(g + 1) * HEAD_SIZE]
            kt_refs[g][0, :HEAD_SIZE, at] = head
            kt_refs[g][0, HEAD_SIZE:, at] = blank
            kt_refs[g][1, :HEAD_SIZE, at] = blank
            kt_refs[g][1, HEAD_SIZE:, at] = head
            low, high = (values, turned) if g == 0 else (turned, values)
            v_refs[g][0, at, :] = jnp.where(lane < HEAD_SIZE, low, 0.0).astype(jnp.bfloat16)
            v_refs[g][1, at, :] = jnp.where(lane < HEAD_SIZE, 0.0, high).astype(jnp.bfloat16)
        found = jnp.where(source >= 0, ref[count:, :].astype(jnp.float32), 0.0)
        marks += [found[0:1, :], found[1:2, :]]
    across = lax.broadcasted_iota(jnp.int32, (half, half), 1)
    down = lax.broadcasted_iota(jnp.int32, (half, half), 0)
    for part in range(2):
        mine = jnp.sum(jnp.where(across == down, marks[-2 + part], 0.0), axis=1, keepdims=True)
        earlier = jnp.zeros((half, half), jnp.float32)
        for row in marks:
            earlier = earlier + jnp.where(row < mine, 1.0, 0.0)
        earlier = jnp.sum(earlier, axis=1, keepdims=True).astype(jnp.int32)
        place = lax.broadcasted_iota(jnp.int32, (half, 128), 0) + (part * half + 1)
        lo_ref[part * half:(part + 1) * half, :] = jnp.maximum(earlier, place)


def query_kernel(pieces, g, more, scal_ref, own_ref, other_ref, *refs):
    weights, refs = refs[: len(pieces)], refs[len(pieces):]
    core = scal_ref[0]
    rows = own_ref.shape[0]
    outs = refs[-2:]
    for rows_ref, which in ((own_ref, core), (other_ref, 1 - core)):
        at = block(which, rows)
        for i, column in enumerate((core, 1 - core)):
            total = refs[i][at, :] if more else None
            for (distance, first), weight_ref in zip(pieces, weights):
                depth = weight_ref.shape[0]
                start = pl.multiple_of(scal_ref[2 + distance] * rows + first, depth)
                found = jnp.dot(
                    rows_ref[:, pl.ds(start, depth)], weight_ref[:, block(2 * g + column, GROUP_WIDTH)],
                    preferred_element_type=jnp.float32,
                )
                total = found if total is None else total + found
            outs[i][at, :] = total


def attention_kernel(lo_ref, kept_ref, received_ref, kt_ref, v_ref, out_ref, query_ref, score_ref):
    tile = pl.program_id(0)
    start = pl.multiple_of(tile * TILE, TILE)
    span = LOOKBACK_SPAN + TILE
    lo = lo_ref[...] - start
    lane = lax.broadcasted_iota(jnp.int32, (TILE, 128), 1)
    row = lax.broadcasted_iota(jnp.int32, (TILE, 128), 0)
    blocks = span // TILE
    queries = (kept_ref[...] + received_ref[...]).astype(jnp.bfloat16)
    query_ref[...] = queries * jnp.bfloat16(HEAD_SIZE ** -0.5)

    def scores_of(pair, parity):
        q = query_ref[:, pair * 128:(pair + 1) * 128]
        peak = jnp.full((TILE, 128), MASKED, jnp.float32)
        for i in range(blocks):
            first = pl.multiple_of(start + i * TILE, TILE)
            found = jnp.dot(q, kt_ref[parity, :, pl.ds(first, TILE)], preferred_element_type=jnp.float32)
            for part in range(TILE // 128):
                at = i * TILE + part * 128
                visible = lane + at >= lo
                if at >= LOOKBACK_SPAN:
                    visible = visible & (lane + (at - LOOKBACK_SPAN) <= row)
                kept = jnp.where(visible, found[:, part * 128:(part + 1) * 128], MASKED)
                peak = jnp.maximum(peak, kept)
                score_ref[parity, :, at:at + 128] = kept
        return jnp.max(peak, axis=1, keepdims=True)

    def mixed_of(parity, peak):
        total = jnp.zeros((TILE, 128), jnp.float32)
        mixed = jnp.zeros((TILE, 128), jnp.float32)
        for i in range(blocks):
            first = pl.multiple_of(start + i * TILE, TILE)
            weights = jnp.exp(score_ref[parity, :, i * TILE:(i + 1) * TILE] - peak)
            for part in range(TILE // 128):
                total = total + weights[:, part * 128:(part + 1) * 128]
            mixed = mixed + jnp.dot(
                weights.astype(jnp.bfloat16), v_ref[parity, pl.ds(first, TILE), :],
                preferred_element_type=jnp.float32,
            )
        return mixed * (1.0 / jnp.sum(total, axis=1, keepdims=True))

    for pair in range(GROUP // 2):
        peaks = [scores_of(pair, parity) for parity in range(2)]
        parts = [mixed_of(parity, peaks[parity]) for parity in range(2)]
        out_ref[:, pair * 128:(pair + 1) * 128] = (parts[0] + parts[1]).astype(out_ref.dtype)


def attention(lo, kept, received, keys_t, values, waits):
    rows = kept.shape[0]
    window = keys_t.shape[2]
    span = LOOKBACK_SPAN + TILE

    def only(*refs):
        attention_kernel(*refs[:5], *refs[5 + len(waits):])

    return pl.pallas_call(
        only,
        grid=(rows // TILE,),
        in_specs=[
            pl.BlockSpec((TILE, 128), lambda t: (t, 0)),
            pl.BlockSpec((TILE, GROUP_WIDTH), lambda t: (t, 0)),
            pl.BlockSpec((TILE, GROUP_WIDTH), lambda t: (t, 0)),
            pl.BlockSpec((2, 128, window), lambda t: (0, 0, 0)),
            pl.BlockSpec((2, window, 128), lambda t: (0, 0, 0)),
        ] + [pl.BlockSpec(memory_space=pl.ANY)] * len(waits),
        out_specs=pl.BlockSpec((TILE, GROUP_WIDTH), lambda t: (t, 0)),
        out_shape=jax.ShapeDtypeStruct((rows, GROUP_WIDTH), jnp.bfloat16),
        scratch_shapes=[
            pltpu.VMEM((TILE, GROUP_WIDTH), jnp.bfloat16), pltpu.VMEM((2, TILE, span), jnp.float32)
        ],
        compiler_params=pltpu.CompilerParams(vmem_limit_bytes=40 * 1024 * 1024),
        cost_estimate=pl.CostEstimate(flops=1000000, bytes_accessed=100000, transcendentals=0),
    )(lo, kept, received, keys_t, values, *waits)


def out_kernel(distances, mode, scal_ref, *refs):
    attended, refs = refs[:4], refs[4:]
    adds, refs = refs[:2], refs[2:]
    count = sum(len(pieces) for _, pieces in distances)
    weights, refs = refs[:count], refs[count:]
    outs = refs[-2:]
    core = scal_ref[0]
    rows = adds[0].shape[0]
    depth = attended[0].shape[1]
    if mode != "alone":
        for i in range(2):
            outs[i][...] = refs[i][...] if mode == "more" else jnp.zeros_like(outs[i])
    for i, which in enumerate((core, 1 - core)):
        taken = 0
        for distance, pieces in distances:
            shard = weights[taken:taken + len(pieces)]
            taken += len(pieces)
            columns = shard[0].shape[1]
            at = block(scal_ref[2 + distance], columns)
            total = adds[i][:, at].astype(jnp.float32)
            for g in range(2):
                ref, first = shard[g * len(shard) // 2], 2 * g if len(shard) == 1 else 0
                for side, column in enumerate((core, 1 - core)):
                    total = total + jnp.dot(
                        attended[2 * g + side][block(which, rows), :],
                        ref[block(first + column, depth), :],
                        preferred_element_type=jnp.float32,
                    )
            if mode == "alone":
                outs[i][...] = total.astype(outs[i].dtype)
            else:
                outs[i][:, at] = total.astype(outs[i].dtype)


def join_kernel(last, scal_ref, own_ref, other_ref, own_last_ref, other_last_ref, out_ref):
    core = scal_ref[0]
    size = own_last_ref.shape[1]
    for j in range(own_ref.shape[1] // size):
        at = slice(j * size, (j + 1) * size)
        out_ref[:, block(2 * j + core, size)] = own_ref[:, at]
        out_ref[:, block(2 * j + 1 - core, size)] = other_ref[:, at]
    j = scal_ref[2 + last]
    out_ref[:, block(2 * j + core, size)] = own_last_ref[...]
    out_ref[:, block(2 * j + 1 - core, size)] = other_last_ref[...]


def body(section_input, segment_ids, query_weight, keyval_weight, out_weight):
    hidden = section_input[0]
    rows, width = hidden.shape
    device = lax.axis_index("fsdp")
    chips = lax.axis_size("fsdp") // 2
    order = ring_order(chips)
    table = []
    for i in range(2 * chips):
        place = order.index(i // 2)
        table.append([i % 2, i // 2] + [order[(place + d) % chips] for d in range(chips)])
    scalars = lax.dynamic_index_in_dim(jnp.array(table, jnp.int32), device, 0, keepdims=False)

    keyval_pieces = around(keyval_weight[0], halved=False)
    out_shard = to_next_section(out_weight[0])
    kv_steps = [keyval_pieces[d][0][1] for d in (3, chips - 3)]
    query_shard, = run(
        copy_kernel, [(query_weight.shape[1:], jnp.bfloat16)], scalars, [query_weight[0]],
        waits=kv_steps + [out_shard],
    )
    query_pieces = around(query_shard)

    half = ((rows, width // 2), jnp.bfloat16)
    own_rows, sent_rows = run(functools.partial(split_kernel, True), [half, half], scalars, [hidden])
    other_rows = swap_cores(sent_rows)

    kept, sent = run(
        functools.partial(keyval_kernel, list(range(chips))),
        [((2 * rows, 256), jnp.float32), ((2 * rows + 8, 256), jnp.float32)],
        scalars, [segment_ids, own_rows, other_rows] + [keyval_pieces[d][0][1] for d in range(chips)],
    )
    parcel, = run(
        parcel_kernel, [((2 * rows + MARK_ROWS, 256), jnp.bfloat16)], scalars,
        [segment_ids, kept, swap_cores(sent)],
    )
    back = -(-LOOKBACK_SPAN // (2 * rows))
    window = (back + 1) * 2 * rows
    *heads, lowest = run(
        functools.partial(window_kernel, back),
        [((2, 128, window), jnp.bfloat16)] * 2 + [((2, window, 128), jnp.bfloat16)] * 2
        + [((2 * rows, 128), jnp.int32)],
        scalars, [gathered(parcel)],
    )

    def query_sums(distances, g, waits, before=()):
        pieces = [(d, first) for d in distances for first, _ in query_pieces[d]]
        shards = [shard for d in distances for _, shard in query_pieces[d]]
        return run(
            functools.partial(query_kernel, pieces, g, bool(before)),
            [((2 * rows, GROUP_WIDTH), jnp.float32)] * 2, scalars,
            [own_rows, other_rows] + shards + list(before), waits=waits,
        )

    near = [0, 1, chips - 1, 2, chips - 2]
    next_far = [3, chips - 3]
    far = [chips // 2]
    sums = [query_sums(near, g, [parcel]) for g in range(2)]
    out_shard = after(out_shard, *[piece for _, piece in query_pieces[chips // 2]], sums[0][0], sums[1][0])
    out_pieces = around(out_shard)
    sums = [query_sums(next_far + far, g, [lowest, out_shard], sums[g]) for g in range(2)]
    attended = []
    for g in range(2):
        waits = [out_pieces[d][0][1] for d in (1, chips - 1)] if g else []
        attended.append(attention(lowest, sums[g][0], swap_cores(sums[g][1]), heads[g], heads[2 + g], waits))
    attended[1] = after(attended[1], *[out_pieces[d][0][1] for d in (2, chips - 2)])
    kept, sent = run(
        functools.partial(split_kernel, False), [half, half], scalars, [from_section_before(hidden)], waits=attended[:1]
    )
    adds = [kept, swap_cores(sent)]
    arrived = []
    for g in range(2):
        mine = to_next_section(attended[g])
        arrived += [mine, swap_cores(mine)]

    def made(some, mode, before=()):
        distances = [(d, [first for first, _ in out_pieces[d]]) for d in some]
        shards = [shard for d in some for _, shard in out_pieces[d]]
        outs = [((rows, out_shard.shape[1]), jnp.bfloat16)] * 2 if mode == "alone" else [half, half]
        taken = arrived + adds + shards
        aliases = {1 + len(taken) + i: i for i in range(2)} if before else {}
        return run(
            functools.partial(out_kernel, distances, mode), outs, scalars, taken + list(before), aliases=aliases
        )

    most = made(near, "first")
    most = made(next_far, "more", most)
    other_most = swap_cores(most[1])
    last = made(far, "alone")
    joined, = run(
        functools.partial(join_kernel, chips // 2), [((rows, width), jnp.bfloat16)], scalars,
        [most[0], other_most, last[0], swap_cores(last[1])],
    )
    return joined[None]


def solution(mesh):
    return jax.shard_map(
        body,
        mesh=mesh,
        in_specs=(
            P("section", "fsdp", None),
            P("section", "fsdp"),
            P("section", "fsdp", None),
            P("section", "fsdp", None),
            P("section", None, "fsdp"),
        ),
        out_specs=P("section", "fsdp", None),
        check_vma=False,
    )
```

```python
import functools

import jax
import jax.numpy as jnp
from jax import lax
from jax.experimental import pallas as pl
from jax.experimental.pallas import tpu as pltpu
from jax.sharding import PartitionSpec as P

QUERY_HEADS = 32
KEY_HEADS = 4
HEAD_SIZE = 64
LOOKBACK_SPAN = 2048
GROUP = QUERY_HEADS // KEY_HEADS
GROUP_WIDTH = GROUP * HEAD_SIZE
TILE = 256
MASKED = -1e30
MARK_ROWS = 16


def ring_order(chips):
    return list(range(0, chips, 2)) + list(range(chips - 1, 0, -2))


def swap_cores(value):
    count = lax.axis_size("fsdp")
    return lax.ppermute(value, "fsdp", [(i, i ^ 1) for i in range(count)])


def gathered(value):
    count = lax.axis_size("fsdp")
    groups = [list(range(core, count, 2)) for core in range(2)]
    return lax.all_gather(value, "fsdp", axis=0, tiled=False, axis_index_groups=groups)


def to_next_section(value):
    count = lax.axis_size("section")
    return lax.ppermute(value, "section", [(i, (i + 1) % count) for i in range(count)])


def from_section_before(value):
    if lax.axis_size("section") != 2:
        return to_next_section(value)
    both = lax.all_gather(value, "section", axis=0, tiled=False)
    return lax.dynamic_index_in_dim(both, 1 - lax.axis_index("section"), 0, keepdims=False)


def along_ring(value, step):
    chips = lax.axis_size("fsdp") // 2
    order = ring_order(chips)
    pairs = []
    for place in range(chips):
        target = order[(place + step) % chips]
        pairs += [(2 * order[place] + core, 2 * target + core) for core in range(2)]
    return lax.ppermute(value, "fsdp", pairs)


def run(kernel, outs, scalars, arrays, waits=(), aliases=None, scratch=()):
    whole = pl.BlockSpec(memory_space=pltpu.VMEM)
    taken = 1 + len(arrays)

    def only(*refs):
        kernel(*refs[:taken], *refs[taken + len(waits):])

    return pl.pallas_call(
        only,
        in_specs=[pl.BlockSpec(memory_space=pltpu.SMEM)] + [whole] * len(arrays)
        + [pl.BlockSpec(memory_space=pl.ANY)] * len(waits),
        out_specs=[whole] * len(outs),
        out_shape=[jax.ShapeDtypeStruct(shape, dtype) for shape, dtype in outs],
        scratch_shapes=list(scratch),
        input_output_aliases=aliases or {},
        compiler_params=pltpu.CompilerParams(vmem_limit_bytes=8 * 1024 * 1024),
        cost_estimate=pl.CostEstimate(flops=1000000, bytes_accessed=100000, transcendentals=0),
    )(scalars, *arrays, *waits)


def tied_kernel(*refs):
    pass


def after(value, *others):
    anywhere = pl.BlockSpec(memory_space=pl.ANY)
    return pl.pallas_call(
        tied_kernel,
        in_specs=[anywhere] * (1 + len(others)),
        out_specs=anywhere,
        out_shape=jax.ShapeDtypeStruct(value.shape, value.dtype),
        input_output_aliases={0: 0},
        cost_estimate=pl.CostEstimate(flops=0, bytes_accessed=0, transcendentals=0),
    )(value, *others)


def around(shard, halved=True):
    chips = lax.axis_size("fsdp") // 2
    found, moving = {0: [(0, shard)]}, {1: shard, -1: shard}
    for step in range(1, (chips - 1) // 2 + 1):
        for way in (1, -1):
            moving[way] = along_ring(moving[way], way)
            found[-way * step % chips] = [(0, moving[way])]
    if chips % 2 == 0 and halved:
        half = shard.shape[0] // 2
        found[chips // 2] = [
            (0, along_ring(moving[1][:half], 1)), (half, along_ring(moving[-1][half:], -1))
        ]
    elif chips % 2 == 0:
        found[chips // 2] = [(0, along_ring(moving[1], 1))]
    return found


def block(index, size):
    return pl.ds(pl.multiple_of(index * size, size), size)


def split_kernel(norm, scal_ref, rows_ref, kept_ref, sent_ref):
    core = scal_ref[0]
    count, width = rows_ref.shape
    size, some = 256, 64
    for first in range(0, count, some):
        at = slice(first, first + some)
        if norm:
            values = rows_ref[at, :].astype(jnp.float32)
            scale = lax.rsqrt(jnp.mean(values * values, axis=1, keepdims=True) + 1e-05)
        for j in range(width // (2 * size)):
            for out_ref, which in ((kept_ref, core), (sent_ref, 1 - core)):
                part = rows_ref[at, block(2 * j + which, size)]
                if norm:
                    part = (part.astype(jnp.float32) * scale).astype(jnp.bfloat16)
                out_ref[at, j * size:(j + 1) * size] = part


def keyval_kernel(distances, scal_ref, segs_ref, own_ref, other_ref, *refs):
    weights, (kept_ref, sent_ref) = refs[: len(distances)], refs[len(distances):]
    core = scal_ref[0]
    rows = own_ref.shape[0]
    lane = lax.broadcasted_iota(jnp.int32, (rows, 128), 1)
    for rows_ref, which in ((own_ref, core), (other_ref, 1 - core)):
        total = None
        for distance, weight_ref in zip(distances, weights):
            found = jnp.dot(
                rows_ref[:, block(scal_ref[2 + distance], weight_ref.shape[0])], weight_ref[...],
                preferred_element_type=jnp.float32,
            )
            total = found if total is None else total + found
        for part in range(2):
            low = total[:, part * 256:part * 256 + 128]
            high = total[:, part * 256 + 128:part * 256 + 256]
            zero = jnp.where(lane < HEAD_SIZE, low, pltpu.roll(high, HEAD_SIZE, 1))
            one = jnp.where(lane < HEAD_SIZE, pltpu.roll(low, HEAD_SIZE, 1), high)
            at = slice(part * 128, part * 128 + 128)
            kept_ref[block(which, rows), at] = jnp.where(core == 0, zero, one)
            sent_ref[block(which, rows), at] = jnp.where(core == 0, one, zero)
    marks = (segs_ref[...] + 1).astype(jnp.float32)
    sent_ref[2 * rows:, :] = jnp.broadcast_to(marks, (8, marks.shape[1]))


def parcel_kernel(scal_ref, segs_ref, kept_ref, received_ref, out_ref):
    core = scal_ref[0]
    count = kept_ref.shape[0]
    out_ref[:count, :] = (kept_ref[...] + received_ref[:count, :]).astype(out_ref.dtype)
    own = (segs_ref[...] + 1).astype(jnp.float32)
    other = received_ref[count:count + 1, :]
    first, second = jnp.where(core == 0, own, other), jnp.where(core == 0, other, own)
    row = lax.broadcasted_iota(jnp.int32, (MARK_ROWS, own.shape[1]), 0)
    marks = jnp.where(row == 0, first, jnp.where(row == 1, second, 0.0))
    out_ref[count:, :] = marks.astype(out_ref.dtype)


def copy_kernel(scal_ref, in_ref, out_ref):
    out_ref[...] = in_ref[...]


def window_kernel(back, scal_ref, parcels_ref, *refs):
    kt_refs, v_refs, lo_ref = refs[:2], refs[2:4], refs[4]
    chip = scal_ref[1]
    count = parcels_ref.shape[1] - MARK_ROWS
    half = count // 2
    lane = lax.broadcasted_iota(jnp.int32, (count, 128), 1)
    blank = jnp.zeros((HEAD_SIZE, count), jnp.bfloat16)
    marks = []
    for i in range(back + 1):
        source = chip - back + i
        ref = parcels_ref.at[jnp.maximum(source, 0)]
        at = slice(i * count, (i + 1) * count)
        keys = ref[:count, 0:128].astype(jnp.float32).T.astype(jnp.bfloat16)
        values = ref[:count, 128:256].astype(jnp.float32)
        turned = pltpu.roll(values, HEAD_SIZE, 1)
        for g in range(2):
            head = keys[g * HEAD_SIZE:(g + 1) * HEAD_SIZE]
            kt_refs[g][0, :HEAD_SIZE, at] = head
            kt_refs[g][0, HEAD_SIZE:, at] = blank
            kt_refs[g][1, :HEAD_SIZE, at] = blank
            kt_refs[g][1, HEAD_SIZE:, at] = head
            low, high = (values, turned) if g == 0 else (turned, values)
            v_refs[g][0, at, :] = jnp.where(lane < HEAD_SIZE, low, 0.0).astype(jnp.bfloat16)
            v_refs[g][1, at, :] = jnp.where(lane < HEAD_SIZE, 0.0, high).astype(jnp.bfloat16)
        found = jnp.where(source >= 0, ref[count:, :].astype(jnp.float32), 0.0)
        marks += [found[0:1, :], found[1:2, :]]
    across = lax.broadcasted_iota(jnp.int32, (half, half), 1)
    down = lax.broadcasted_iota(jnp.int32, (half, half), 0)
    for part in range(2):
        mine = jnp.sum(jnp.where(across == down, marks[-2 + part], 0.0), axis=1, keepdims=True)
        earlier = jnp.zeros((half, half), jnp.float32)
        for row in marks:
            earlier = earlier + jnp.where(row < mine, 1.0, 0.0)
        earlier = jnp.sum(earlier, axis=1, keepdims=True).astype(jnp.int32)
        place = lax.broadcasted_iota(jnp.int32, (half, 128), 0) + (part * half + 1)
        lo_ref[part * half:(part + 1) * half, :] = jnp.maximum(earlier, place)


def query_kernel(pieces, g, more, scal_ref, own_ref, other_ref, *refs):
    weights, refs = refs[: len(pieces)], refs[len(pieces):]
    core = scal_ref[0]
    rows = own_ref.shape[0]
    outs = refs[-2:]
    for rows_ref, which in ((own_ref, core), (other_ref, 1 - core)):
        at = block(which, rows)
        for i, column in enumerate((core, 1 - core)):
            total = refs[i][at, :] if more else None
            for (distance, first), weight_ref in zip(pieces, weights):
                depth = weight_ref.shape[0]
                start = pl.multiple_of(scal_ref[2 + distance] * rows + first, depth)
                found = jnp.dot(
                    rows_ref[:, pl.ds(start, depth)], weight_ref[:, block(2 * g + column, GROUP_WIDTH)],
                    preferred_element_type=jnp.float32,
                )
                total = found if total is None else total + found
            outs[i][at, :] = total


def attention_kernel(lo_ref, kept_ref, received_ref, kt_ref, v_ref, out_ref, query_ref, score_ref):
    tile = pl.program_id(0)
    start = pl.multiple_of(tile * TILE, TILE)
    span = LOOKBACK_SPAN + TILE
    lo = lo_ref[...] - start
    lane = lax.broadcasted_iota(jnp.int32, (TILE, 128), 1)
    row = lax.broadcasted_iota(jnp.int32, (TILE, 128), 0)
    blocks = span // TILE
    queries = (kept_ref[...] + received_ref[...]).astype(jnp.bfloat16)
    query_ref[...] = queries * jnp.bfloat16(HEAD_SIZE ** -0.5)

    def scores_of(pair, parity):
        q = query_ref[:, pair * 128:(pair + 1) * 128]
        peak = jnp.full((TILE, 128), MASKED, jnp.float32)
        for i in range(blocks):
            first = pl.multiple_of(start + i * TILE, TILE)
            found = jnp.dot(q, kt_ref[parity, :, pl.ds(first, TILE)], preferred_element_type=jnp.float32)
            for part in range(TILE // 128):
                at = i * TILE + part * 128
                visible = lane + at >= lo
                if at >= LOOKBACK_SPAN:
                    visible = visible & (lane + (at - LOOKBACK_SPAN) <= row)
                kept = jnp.where(visible, found[:, part * 128:(part + 1) * 128], MASKED)
                peak = jnp.maximum(peak, kept)
                score_ref[parity, :, at:at + 128] = kept
        return jnp.max(peak, axis=1, keepdims=True)

    def mixed_of(parity, peak):
        total = jnp.zeros((TILE, 128), jnp.float32)
        mixed = jnp.zeros((TILE, 128), jnp.float32)
        for i in range(blocks):
            first = pl.multiple_of(start + i * TILE, TILE)
            weights = jnp.exp(score_ref[parity, :, i * TILE:(i + 1) * TILE] - peak)
            for part in range(TILE // 128):
                total = total + weights[:, part * 128:(part + 1) * 128]
            mixed = mixed + jnp.dot(
                weights.astype(jnp.bfloat16), v_ref[parity, pl.ds(first, TILE), :],
                preferred_element_type=jnp.float32,
            )
        return mixed * (1.0 / jnp.sum(total, axis=1, keepdims=True))

    for pair in range(GROUP // 2):
        peaks = [scores_of(pair, parity) for parity in range(2)]
        parts = [mixed_of(parity, peaks[parity]) for parity in range(2)]
        out_ref[:, pair * 128:(pair + 1) * 128] = (parts[0] + parts[1]).astype(out_ref.dtype)


def attention(lo, kept, received, keys_t, values, waits):
    rows = kept.shape[0]
    window = keys_t.shape[2]
    span = LOOKBACK_SPAN + TILE

    def only(*refs):
        attention_kernel(*refs[:5], *refs[5 + len(waits):])

    return pl.pallas_call(
        only,
        grid=(rows // TILE,),
        in_specs=[
            pl.BlockSpec((TILE, 128), lambda t: (t, 0)),
            pl.BlockSpec((TILE, GROUP_WIDTH), lambda t: (t, 0)),
            pl.BlockSpec((TILE, GROUP_WIDTH), lambda t: (t, 0)),
            pl.BlockSpec((2, 128, window), lambda t: (0, 0, 0)),
            pl.BlockSpec((2, window, 128), lambda t: (0, 0, 0)),
        ] + [pl.BlockSpec(memory_space=pl.ANY)] * len(waits),
        out_specs=pl.BlockSpec((TILE, GROUP_WIDTH), lambda t: (t, 0)),
        out_shape=jax.ShapeDtypeStruct((rows, GROUP_WIDTH), jnp.bfloat16),
        scratch_shapes=[
            pltpu.VMEM((TILE, GROUP_WIDTH), jnp.bfloat16), pltpu.VMEM((2, TILE, span), jnp.float32)
        ],
        compiler_params=pltpu.CompilerParams(vmem_limit_bytes=20 * 1024 * 1024),
        cost_estimate=pl.CostEstimate(flops=1000000, bytes_accessed=100000, transcendentals=0),
    )(lo, kept, received, keys_t, values, *waits)


def out_kernel(distances, mode, scal_ref, *refs):
    attended, refs = refs[:4], refs[4:]
    adds, refs = refs[:2], refs[2:]
    count = sum(len(pieces) for _, pieces in distances)
    weights, refs = refs[:count], refs[count:]
    outs = refs[-2:]
    core = scal_ref[0]
    rows = adds[0].shape[0]
    depth = attended[0].shape[1]
    if mode != "alone":
        for i in range(2):
            outs[i][...] = refs[i][...] if mode == "more" else jnp.zeros_like(outs[i])
    for i, which in enumerate((core, 1 - core)):
        taken = 0
        for distance, pieces in distances:
            shard = weights[taken:taken + len(pieces)]
            taken += len(pieces)
            columns = shard[0].shape[1]
            at = block(scal_ref[2 + distance], columns)
            total = adds[i][:, at].astype(jnp.float32)
            for g in range(2):
                ref, first = shard[g * len(shard) // 2], 2 * g if len(shard) == 1 else 0
                for side, column in enumerate((core, 1 - core)):
                    total = total + jnp.dot(
                        attended[2 * g + side][block(which, rows), :],
                        ref[block(first + column, depth), :],
                        preferred_element_type=jnp.float32,
                    )
            if mode == "alone":
                outs[i][...] = total.astype(outs[i].dtype)
            else:
                outs[i][:, at] = total.astype(outs[i].dtype)


def join_kernel(last, scal_ref, own_ref, other_ref, own_last_ref, other_last_ref, out_ref):
    core = scal_ref[0]
    size = own_last_ref.shape[1]
    for j in range(own_ref.shape[1] // size):
        at = slice(j * size, (j + 1) * size)
        out_ref[:, block(2 * j + core, size)] = own_ref[:, at]
        out_ref[:, block(2 * j + 1 - core, size)] = other_ref[:, at]
    j = scal_ref[2 + last]
    out_ref[:, block(2 * j + core, size)] = own_last_ref[...]
    out_ref[:, block(2 * j + 1 - core, size)] = other_last_ref[...]


def body(section_input, segment_ids, query_weight, keyval_weight, out_weight):
    hidden = section_input[0]
    rows, width = hidden.shape
    device = lax.axis_index("fsdp")
    chips = lax.axis_size("fsdp") // 2
    order = ring_order(chips)
    table = []
    for i in range(2 * chips):
        place = order.index(i // 2)
        table.append([i % 2, i // 2] + [order[(place + d) % chips] for d in range(chips)])
    scalars = lax.dynamic_index_in_dim(jnp.array(table, jnp.int32), device, 0, keepdims=False)

    keyval_pieces = around(keyval_weight[0], halved=False)
    out_shard = from_section_before(out_weight[0])
    kv_steps = [keyval_pieces[d][0][1] for d in (3, chips - 3)]
    query_shard, = run(
        copy_kernel, [(query_weight.shape[1:], jnp.bfloat16)], scalars, [query_weight[0]],
        waits=kv_steps,
    )
    query_pieces = around(query_shard)

    half = ((rows, width // 2), jnp.bfloat16)
    own_rows, sent_rows = run(functools.partial(split_kernel, True), [half, half], scalars, [hidden])
    other_rows = swap_cores(sent_rows)

    kept, sent = run(
        functools.partial(keyval_kernel, list(range(chips))),
        [((2 * rows, 256), jnp.float32), ((2 * rows + 8, 256), jnp.float32)],
        scalars, [segment_ids, own_rows, other_rows] + [keyval_pieces[d][0][1] for d in range(chips)],
    )
    parcel, = run(
        parcel_kernel, [((2 * rows + MARK_ROWS, 256), jnp.bfloat16)], scalars,
        [segment_ids, kept, swap_cores(sent)],
    )
    back = -(-LOOKBACK_SPAN // (2 * rows))
    window = (back + 1) * 2 * rows
    *heads, lowest = run(
        functools.partial(window_kernel, back),
        [((2, 128, window), jnp.bfloat16)] * 2 + [((2, window, 128), jnp.bfloat16)] * 2
        + [((2 * rows, 128), jnp.int32)],
        scalars, [gathered(parcel)],
    )

    def query_sums(distances, g, waits, before=()):
        pieces = [(d, first) for d in distances for first, _ in query_pieces[d]]
        shards = [shard for d in distances for _, shard in query_pieces[d]]
        return run(
            functools.partial(query_kernel, pieces, g, bool(before)),
            [((2 * rows, GROUP_WIDTH), jnp.float32)] * 2, scalars,
            [own_rows, other_rows] + shards + list(before), waits=waits,
        )

    near = [0, 1, chips - 1, 2, chips - 2]
    next_far = [3, chips - 3]
    far = [chips // 2]
    sums = [query_sums(near, g, [parcel]) for g in range(2)]
    out_shard = after(out_shard, *[piece for _, piece in query_pieces[chips // 2]], sums[0][0], sums[1][0])
    out_pieces = around(out_shard)
    sums = [query_sums(next_far + far, g, [lowest, out_shard], sums[g]) for g in range(2)]
    attended = []
    for g in range(2):
        waits = [out_pieces[d][0][1] for d in (1, chips - 1)] if g else []
        attended.append(attention(lowest, sums[g][0], swap_cores(sums[g][1]), heads[g], heads[2 + g], waits))
    attended[1] = after(attended[1], *[out_pieces[d][0][1] for d in (2, chips - 2)])
    kept, sent = run(
        functools.partial(split_kernel, False), [half, half], scalars, [to_next_section(hidden)], waits=attended[:1]
    )
    adds = [kept, swap_cores(sent)]
    arrived = []
    for g in range(2):
        mine = to_next_section(attended[g])
        arrived += [mine, swap_cores(mine)]

    def made(some, mode, before=()):
        distances = [(d, [first for first, _ in out_pieces[d]]) for d in some]
        shards = [shard for d in some for _, shard in out_pieces[d]]
        outs = [((rows, out_shard.shape[1]), jnp.bfloat16)] * 2 if mode == "alone" else [half, half]
        taken = arrived + adds + shards
        aliases = {1 + len(taken) + i: i for i in range(2)} if before else {}
        return run(
            functools.partial(out_kernel, distances, mode), outs, scalars, taken + list(before), aliases=aliases
        )

    most = made(near, "first")
    most = made(next_far, "more", most)
    other_most = swap_cores(most[1])
    last = made(far, "alone")
    joined, = run(
        functools.partial(join_kernel, chips // 2), [((rows, width), jnp.bfloat16)], scalars,
        [most[0], other_most, last[0], swap_cores(last[1])],
    )
    return joined[None]


def solution(mesh):
    return jax.shard_map(
        body,
        mesh=mesh,
        in_specs=(
            P("section", "fsdp", None),
            P("section", "fsdp"),
            P("section", "fsdp", None),
            P("section", "fsdp", None),
            P("section", None, "fsdp"),
        ),
        out_specs=P("section", "fsdp", None),
        check_vma=False,
    )
```

```python
import functools

import jax
import jax.numpy as jnp
from jax import lax
from jax.experimental import pallas as pl
from jax.experimental.pallas import tpu as pltpu
from jax.sharding import PartitionSpec as P

QUERY_HEADS = 32
KEY_HEADS = 4
HEAD_SIZE = 64
LOOKBACK_SPAN = 2048
GROUP = QUERY_HEADS // KEY_HEADS
GROUP_WIDTH = GROUP * HEAD_SIZE
TILE = 256
MASKED = -1e30
MARK_ROWS = 16


def ring_order(chips):
    return list(range(0, chips, 2)) + list(range(chips - 1, 0, -2))


def swap_cores(value):
    count = lax.axis_size("fsdp")
    return lax.ppermute(value, "fsdp", [(i, i ^ 1) for i in range(count)])


def swap_chips(value):
    count = lax.axis_size("fsdp")
    return lax.ppermute(value, "fsdp", [(i, i ^ 2) for i in range(count)])


def two_chips_on(value):
    count = lax.axis_size("fsdp")
    return lax.ppermute(value, "fsdp", [(i, i + 4) for i in range(count - 4)])


def to_next_section(value):
    count = lax.axis_size("section")
    return lax.ppermute(value, "section", [(i, (i + 1) % count) for i in range(count)])


def from_section_before(value):
    if lax.axis_size("section") != 2:
        return to_next_section(value)
    both = lax.all_gather(value, "section", axis=0, tiled=False)
    return lax.dynamic_index_in_dim(both, 1 - lax.axis_index("section"), 0, keepdims=False)


def along_ring(value, step):
    chips = lax.axis_size("fsdp") // 2
    order = ring_order(chips)
    pairs = []
    for place in range(chips):
        target = order[(place + step) % chips]
        pairs += [(2 * order[place] + core, 2 * target + core) for core in range(2)]
    return lax.ppermute(value, "fsdp", pairs)


def run(kernel, outs, scalars, arrays, waits=(), aliases=None, scratch=()):
    whole = pl.BlockSpec(memory_space=pltpu.VMEM)
    taken = 1 + len(arrays)

    def only(*refs):
        kernel(*refs[:taken], *refs[taken + len(waits):])

    return pl.pallas_call(
        only,
        in_specs=[pl.BlockSpec(memory_space=pltpu.SMEM)] + [whole] * len(arrays)
        + [pl.BlockSpec(memory_space=pl.ANY)] * len(waits),
        out_specs=[whole] * len(outs),
        out_shape=[jax.ShapeDtypeStruct(shape, dtype) for shape, dtype in outs],
        scratch_shapes=list(scratch),
        input_output_aliases=aliases or {},
        compiler_params=pltpu.CompilerParams(vmem_limit_bytes=8 * 1024 * 1024),
        cost_estimate=pl.CostEstimate(flops=1000000, bytes_accessed=100000, transcendentals=0),
    )(scalars, *arrays, *waits)


def tied_kernel(*refs):
    pass


def after(value, *others):
    anywhere = pl.BlockSpec(memory_space=pl.ANY)
    return pl.pallas_call(
        tied_kernel,
        in_specs=[anywhere] * (1 + len(others)),
        out_specs=anywhere,
        out_shape=jax.ShapeDtypeStruct(value.shape, value.dtype),
        input_output_aliases={0: 0},
        cost_estimate=pl.CostEstimate(flops=0, bytes_accessed=0, transcendentals=0),
    )(value, *others)


def around(shard, halved=True):
    chips = lax.axis_size("fsdp") // 2
    found, moving = {0: [(0, shard)]}, {1: shard, -1: shard}
    for step in range(1, (chips - 1) // 2 + 1):
        for way in (1, -1):
            moving[way] = along_ring(moving[way], way)
            found[-way * step % chips] = [(0, moving[way])]
    if chips % 2 == 0 and halved:
        half = shard.shape[0] // 2
        found[chips // 2] = [
            (0, along_ring(moving[1][:half], 1)), (half, along_ring(moving[-1][half:], -1))
        ]
    elif chips % 2 == 0:
        found[chips // 2] = [(0, along_ring(moving[1], 1))]
    return found


def block(index, size):
    return pl.ds(pl.multiple_of(index * size, size), size)


def split_kernel(norm, scal_ref, rows_ref, kept_ref, sent_ref):
    core = scal_ref[0]
    count, width = rows_ref.shape
    size, some = 256, 64
    for first in range(0, count, some):
        at = slice(first, first + some)
        if norm:
            values = rows_ref[at, :].astype(jnp.float32)
            scale = lax.rsqrt(jnp.mean(values * values, axis=1, keepdims=True) + 1e-05)
        for j in range(width // (2 * size)):
            for out_ref, which in ((kept_ref, core), (sent_ref, 1 - core)):
                part = rows_ref[at, block(2 * j + which, size)]
                if norm:
                    part = (part.astype(jnp.float32) * scale).astype(jnp.bfloat16)
                out_ref[at, j * size:(j + 1) * size] = part


def keyval_kernel(distances, scal_ref, segs_ref, own_ref, other_ref, *refs):
    weights, (kept_ref, sent_ref) = refs[: len(distances)], refs[len(distances):]
    core = scal_ref[0]
    rows = own_ref.shape[0]
    lane = lax.broadcasted_iota(jnp.int32, (rows, 128), 1)
    for rows_ref, which in ((own_ref, core), (other_ref, 1 - core)):
        total = None
        for distance, weight_ref in zip(distances, weights):
            found = jnp.dot(
                rows_ref[:, block(scal_ref[2 + distance], weight_ref.shape[0])], weight_ref[...],
                preferred_element_type=jnp.float32,
            )
            total = found if total is None else total + found
        for part in range(2):
            low = total[:, part * 256:part * 256 + 128]
            high = total[:, part * 256 + 128:part * 256 + 256]
            zero = jnp.where(lane < HEAD_SIZE, low, pltpu.roll(high, HEAD_SIZE, 1))
            one = jnp.where(lane < HEAD_SIZE, pltpu.roll(low, HEAD_SIZE, 1), high)
            at = slice(part * 128, part * 128 + 128)
            kept_ref[block(which, rows), at] = jnp.where(core == 0, zero, one)
            sent_ref[block(which, rows), at] = jnp.where(core == 0, one, zero)
    marks = (segs_ref[...] + 1).astype(jnp.float32)
    sent_ref[2 * rows:, :] = jnp.broadcast_to(marks, (8, marks.shape[1]))


def parcel_kernel(scal_ref, segs_ref, kept_ref, received_ref, out_ref):
    core = scal_ref[0]
    count = kept_ref.shape[0]
    out_ref[:count, :] = (kept_ref[...] + received_ref[:count, :]).astype(out_ref.dtype)
    own = (segs_ref[...] + 1).astype(jnp.float32)
    other = received_ref[count:count + 1, :]
    first, second = jnp.where(core == 0, own, other), jnp.where(core == 0, other, own)
    row = lax.broadcasted_iota(jnp.int32, (MARK_ROWS, own.shape[1]), 0)
    marks = jnp.where(row == 0, first, jnp.where(row == 1, second, 0.0))
    out_ref[count:, :] = marks.astype(out_ref.dtype)


def copy_kernel(scal_ref, in_ref, out_ref):
    out_ref[...] = in_ref[...]


def window_kernel(scal_ref, four_ref, two_ref, own_ref, crossed_ref, *refs):
    kt_refs, v_refs, lo_ref = refs[:2], refs[2:4], refs[4]
    odd = scal_ref[1]
    length = own_ref.shape[0]
    count = length - MARK_ROWS
    half = count // 2
    second = pl.multiple_of(odd * length, MARK_ROWS)
    fourth = pl.multiple_of((1 - odd) * length, MARK_ROWS)
    places = [(four_ref, 0), (crossed_ref, second), (two_ref, 0), (crossed_ref, fourth), (own_ref, 0)]
    lane = lax.broadcasted_iota(jnp.int32, (count, 128), 1)
    blank = jnp.zeros((HEAD_SIZE, count), jnp.bfloat16)
    marks = []
    for i, (ref, first) in enumerate(places):
        at = slice(i * count, (i + 1) * count)
        keys = ref[pl.ds(first, count), 0:128].astype(jnp.float32).T.astype(jnp.bfloat16)
        values = ref[pl.ds(first, count), 128:256].astype(jnp.float32)
        turned = pltpu.roll(values, HEAD_SIZE, 1)
        for g in range(2):
            head = keys[g * HEAD_SIZE:(g + 1) * HEAD_SIZE]
            kt_refs[g][0, :HEAD_SIZE, at] = head
            kt_refs[g][0, HEAD_SIZE:, at] = blank
            kt_refs[g][1, :HEAD_SIZE, at] = blank
            kt_refs[g][1, HEAD_SIZE:, at] = head
            low, high = (values, turned) if g == 0 else (turned, values)
            v_refs[g][0, at, :] = jnp.where(lane < HEAD_SIZE, low, 0.0).astype(jnp.bfloat16)
            v_refs[g][1, at, :] = jnp.where(lane < HEAD_SIZE, 0.0, high).astype(jnp.bfloat16)
        found = ref[pl.ds(first + count, MARK_ROWS), :].astype(jnp.float32)
        marks += [found[0:1, :], found[1:2, :]]
    across = lax.broadcasted_iota(jnp.int32, (half, half), 1)
    down = lax.broadcasted_iota(jnp.int32, (half, half), 0)
    for part in range(2):
        mine = jnp.sum(jnp.where(across == down, marks[-2 + part], 0.0), axis=1, keepdims=True)
        earlier = jnp.zeros((half, half), jnp.float32)
        for row in marks:
            earlier = earlier + jnp.where(row < mine, 1.0, 0.0)
        earlier = jnp.sum(earlier, axis=1, keepdims=True).astype(jnp.int32)
        place = lax.broadcasted_iota(jnp.int32, (half, 128), 0) + (part * half + 1)
        lo_ref[part * half:(part + 1) * half, :] = jnp.maximum(earlier, place)


def query_kernel(pieces, g, more, scal_ref, own_ref, other_ref, *refs):
    weights, refs = refs[: len(pieces)], refs[len(pieces):]
    core = scal_ref[0]
    rows = own_ref.shape[0]
    outs = refs[-2:]
    for rows_ref, which in ((own_ref, core), (other_ref, 1 - core)):
        at = block(which, rows)
        for i, column in enumerate((core, 1 - core)):
            total = refs[i][at, :] if more else None
            for (distance, first), weight_ref in zip(pieces, weights):
                depth = weight_ref.shape[0]
                start = pl.multiple_of(scal_ref[2 + distance] * rows + first, depth)
                found = jnp.dot(
                    rows_ref[:, pl.ds(start, depth)], weight_ref[:, block(2 * g + column, GROUP_WIDTH)],
                    preferred_element_type=jnp.float32,
                )
                total = found if total is None else total + found
            outs[i][at, :] = total


def attention_kernel(lo_ref, kept_ref, received_ref, kt_ref, v_ref, out_ref, query_ref, score_ref):
    tile = pl.program_id(0)
    start = pl.multiple_of(tile * TILE, TILE)
    span = LOOKBACK_SPAN + TILE
    lo = lo_ref[...] - start
    lane = lax.broadcasted_iota(jnp.int32, (TILE, 128), 1)
    row = lax.broadcasted_iota(jnp.int32, (TILE, 128), 0)
    blocks = span // TILE
    queries = (kept_ref[...] + received_ref[...]).astype(jnp.bfloat16)
    query_ref[...] = queries * jnp.bfloat16(HEAD_SIZE ** -0.5)

    def scores_of(pair, parity):
        q = query_ref[:, pair * 128:(pair + 1) * 128]
        peak = jnp.full((TILE, 128), MASKED, jnp.float32)
        for i in range(blocks):
            first = pl.multiple_of(start + i * TILE, TILE)
            found = jnp.dot(q, kt_ref[parity, :, pl.ds(first, TILE)], preferred_element_type=jnp.float32)
            for part in range(TILE // 128):
                at = i * TILE + part * 128
                visible = lane + at >= lo
                if at >= LOOKBACK_SPAN:
                    visible = visible & (lane + (at - LOOKBACK_SPAN) <= row)
                kept = jnp.where(visible, found[:, part * 128:(part + 1) * 128], MASKED)
                peak = jnp.maximum(peak, kept)
                score_ref[parity, :, at:at + 128] = kept
        return jnp.max(peak, axis=1, keepdims=True)

    def mixed_of(parity, peak):
        total = jnp.zeros((TILE, 128), jnp.float32)
        mixed = jnp.zeros((TILE, 128), jnp.float32)
        for i in range(blocks):
            first = pl.multiple_of(start + i * TILE, TILE)
            weights = jnp.exp(score_ref[parity, :, i * TILE:(i + 1) * TILE] - peak)
            for part in range(TILE // 128):
                total = total + weights[:, part * 128:(part + 1) * 128]
            mixed = mixed + jnp.dot(
                weights.astype(jnp.bfloat16), v_ref[parity, pl.ds(first, TILE), :],
                preferred_element_type=jnp.float32,
            )
        return mixed * (1.0 / jnp.sum(total, axis=1, keepdims=True))

    for pair in range(GROUP // 2):
        peaks = [scores_of(pair, parity) for parity in range(2)]
        parts = [mixed_of(parity, peaks[parity]) for parity in range(2)]
        out_ref[:, pair * 128:(pair + 1) * 128] = (parts[0] + parts[1]).astype(out_ref.dtype)


def attention(lo, kept, received, keys_t, values, waits):
    rows = kept.shape[0]
    window = keys_t.shape[2]
    span = LOOKBACK_SPAN + TILE

    def only(*refs):
        attention_kernel(*refs[:5], *refs[5 + len(waits):])

    return pl.pallas_call(
        only,
        grid=(rows // TILE,),
        in_specs=[
            pl.BlockSpec((TILE, 128), lambda t: (t, 0)),
            pl.BlockSpec((TILE, GROUP_WIDTH), lambda t: (t, 0)),
            pl.BlockSpec((TILE, GROUP_WIDTH), lambda t: (t, 0)),
            pl.BlockSpec((2, 128, window), lambda t: (0, 0, 0)),
            pl.BlockSpec((2, window, 128), lambda t: (0, 0, 0)),
        ] + [pl.BlockSpec(memory_space=pl.ANY)] * len(waits),
        out_specs=pl.BlockSpec((TILE, GROUP_WIDTH), lambda t: (t, 0)),
        out_shape=jax.ShapeDtypeStruct((rows, GROUP_WIDTH), jnp.bfloat16),
        scratch_shapes=[
            pltpu.VMEM((TILE, GROUP_WIDTH), jnp.bfloat16), pltpu.VMEM((2, TILE, span), jnp.float32)
        ],
        compiler_params=pltpu.CompilerParams(vmem_limit_bytes=20 * 1024 * 1024),
        cost_estimate=pl.CostEstimate(flops=1000000, bytes_accessed=100000, transcendentals=0),
    )(lo, kept, received, keys_t, values, *waits)


def out_kernel(distances, mode, scal_ref, *refs):
    attended, refs = refs[:4], refs[4:]
    adds, refs = refs[:2], refs[2:]
    count = sum(len(pieces) for _, pieces in distances)
    weights, refs = refs[:count], refs[count:]
    outs = refs[-2:]
    core = scal_ref[0]
    rows = adds[0].shape[0]
    depth = attended[0].shape[1]
    if mode != "alone":
        for i in range(2):
            outs[i][...] = refs[i][...] if mode == "more" else jnp.zeros_like(outs[i])
    for i, which in enumerate((core, 1 - core)):
        taken = 0
        for distance, pieces in distances:
            shard = weights[taken:taken + len(pieces)]
            taken += len(pieces)
            columns = shard[0].shape[1]
            at = block(scal_ref[2 + distance], columns)
            total = adds[i][:, at].astype(jnp.float32)
            for g in range(2):
                ref, first = shard[g * len(shard) // 2], 2 * g if len(shard) == 1 else 0
                for side, column in enumerate((core, 1 - core)):
                    total = total + jnp.dot(
                        attended[2 * g + side][block(which, rows), :],
                        ref[block(first + column, depth), :],
                        preferred_element_type=jnp.float32,
                    )
            if mode == "alone":
                outs[i][...] = total.astype(outs[i].dtype)
            else:
                outs[i][:, at] = total.astype(outs[i].dtype)


def join_kernel(last, scal_ref, own_ref, other_ref, own_last_ref, other_last_ref, out_ref):
    core = scal_ref[0]
    size = own_last_ref.shape[1]
    for j in range(own_ref.shape[1] // size):
        at = slice(j * size, (j + 1) * size)
        out_ref[:, block(2 * j + core, size)] = own_ref[:, at]
        out_ref[:, block(2 * j + 1 - core, size)] = other_ref[:, at]
    j = scal_ref[2 + last]
    out_ref[:, block(2 * j + core, size)] = own_last_ref[...]
    out_ref[:, block(2 * j + 1 - core, size)] = other_last_ref[...]


def body(section_input, segment_ids, query_weight, keyval_weight, out_weight):
    hidden = section_input[0]
    rows, width = hidden.shape
    device = lax.axis_index("fsdp")
    chips = lax.axis_size("fsdp") // 2
    order = ring_order(chips)
    table = []
    for i in range(2 * chips):
        place = order.index(i // 2)
        table.append([i % 2, i // 2 % 2] + [order[(place + d) % chips] for d in range(chips)])
    scalars = lax.dynamic_index_in_dim(jnp.array(table, jnp.int32), device, 0, keepdims=False)

    keyval_pieces = around(keyval_weight[0], halved=False)
    out_shard = from_section_before(out_weight[0])
    kv_steps = [keyval_pieces[d][0][1] for d in (3, chips - 3, chips // 2)]
    query_shard, = run(
        copy_kernel, [(query_weight.shape[1:], jnp.bfloat16)], scalars, [query_weight[0]],
        waits=kv_steps,
    )
    query_pieces = around(query_shard)

    half = ((rows, width // 2), jnp.bfloat16)
    own_rows, sent_rows = run(functools.partial(split_kernel, True), [half, half], scalars, [hidden])
    other_rows = swap_cores(sent_rows)

    kept, sent = run(
        functools.partial(keyval_kernel, list(range(chips))),
        [((2 * rows, 256), jnp.float32), ((2 * rows + 8, 256), jnp.float32)],
        scalars, [segment_ids, own_rows, other_rows] + [keyval_pieces[d][0][1] for d in range(chips)],
    )
    parcel, = run(
        parcel_kernel, [((2 * rows + MARK_ROWS, 256), jnp.bfloat16)], scalars,
        [segment_ids, kept, swap_cores(sent)],
    )
    steps = [[query_pieces[d][0][1] for d in (step, chips - step)] for step in range(1, 4)]
    back_two = after(two_chips_on(parcel), *steps[0])
    back_four = after(two_chips_on(back_two), *steps[1])
    even = device // 2 % 2 == 0
    crossed = swap_chips(jnp.concatenate([jnp.where(even, parcel, back_four), back_two], axis=0))
    window = 5 * 2 * rows
    *heads, lowest = run(
        window_kernel,
        [((2, 128, window), jnp.bfloat16)] * 2 + [((2, window, 128), jnp.bfloat16)] * 2
        + [((2 * rows, 128), jnp.int32)],
        scalars, [back_four, back_two, parcel, crossed], waits=steps[2],
    )

    def query_sums(distances, g, waits, before=()):
        pieces = [(d, first) for d in distances for first, _ in query_pieces[d]]
        shards = [shard for d in distances for _, shard in query_pieces[d]]
        return run(
            functools.partial(query_kernel, pieces, g, bool(before)),
            [((2 * rows, GROUP_WIDTH), jnp.float32)] * 2, scalars,
            [own_rows, other_rows] + shards + list(before), waits=waits,
        )

    near = [0, 1, chips - 1, 2, chips - 2]
    next_far = [3, chips - 3]
    far = [chips // 2]
    sums = [query_sums(near, g, [parcel]) for g in range(2)]
    out_shard = after(out_shard, *[piece for _, piece in query_pieces[chips // 2]], sums[0][0], sums[1][0])
    out_pieces = around(out_shard)
    sums = [query_sums(next_far + far, g, [lowest, out_shard], sums[g]) for g in range(2)]
    attended = []
    for g in range(2):
        waits = [out_pieces[d][0][1] for d in (1, chips - 1)] if g else []
        attended.append(attention(lowest, sums[g][0], swap_cores(sums[g][1]), heads[g], heads[2 + g], waits))
    attended[1] = after(attended[1], *[out_pieces[d][0][1] for d in (2, chips - 2)])
    kept, sent = run(
        functools.partial(split_kernel, False), [half, half], scalars, [to_next_section(hidden)], waits=attended[:1]
    )
    adds = [kept, swap_cores(sent)]
    arrived = []
    for g in range(2):
        mine = to_next_section(attended[g])
        arrived += [mine, swap_cores(mine)]

    def made(some, mode, before=()):
        distances = [(d, [first for first, _ in out_pieces[d]]) for d in some]
        shards = [shard for d in some for _, shard in out_pieces[d]]
        outs = [((rows, out_shard.shape[1]), jnp.bfloat16)] * 2 if mode == "alone" else [half, half]
        taken = arrived + adds + shards
        aliases = {1 + len(taken) + i: i for i in range(2)} if before else {}
        return run(
            functools.partial(out_kernel, distances, mode), outs, scalars, taken + list(before), aliases=aliases
        )

    most = made(near, "first")
    most = made(next_far, "more", most)
    other_most = swap_cores(most[1])
    last = made(far, "alone")
    joined, = run(
        functools.partial(join_kernel, chips // 2), [((rows, width), jnp.bfloat16)], scalars,
        [most[0], other_most, last[0], swap_cores(last[1])],
    )
    return joined[None]


def solution(mesh):
    return jax.shard_map(
        body,
        mesh=mesh,
        in_specs=(
            P("section", "fsdp", None),
            P("section", "fsdp"),
            P("section", "fsdp", None),
            P("section", "fsdp", None),
            P("section", None, "fsdp"),
        ),
        out_specs=P("section", "fsdp", None),
        check_vma=False,
    )
```

```python
import functools

import jax
import jax.numpy as jnp
from jax import lax
from jax.experimental import pallas as pl
from jax.experimental.pallas import tpu as pltpu
from jax.sharding import PartitionSpec as P

QUERY_HEADS = 32
KEY_HEADS = 4
HEAD_SIZE = 64
LOOKBACK_SPAN = 2048
GROUP = QUERY_HEADS // KEY_HEADS
GROUP_WIDTH = GROUP * HEAD_SIZE
TILE = 256
MASKED = -1e30
MARK_ROWS = 16


def ring_order(chips):
    return list(range(0, chips, 2)) + list(range(chips - 1, 0, -2))


def swap_cores(value):
    count = lax.axis_size("fsdp")
    return lax.ppermute(value, "fsdp", [(i, i ^ 1) for i in range(count)])


def swap_chips(value):
    count = lax.axis_size("fsdp")
    return lax.ppermute(value, "fsdp", [(i, i ^ 2) for i in range(count)])


def two_chips_on(value):
    count = lax.axis_size("fsdp")
    return lax.ppermute(value, "fsdp", [(i, i + 4) for i in range(count - 4)])


def to_next_section(value):
    count = lax.axis_size("section")
    return lax.ppermute(value, "section", [(i, (i + 1) % count) for i in range(count)])


def along_ring(value, step):
    chips = lax.axis_size("fsdp") // 2
    order = ring_order(chips)
    pairs = []
    for place in range(chips):
        target = order[(place + step) % chips]
        pairs += [(2 * order[place] + core, 2 * target + core) for core in range(2)]
    return lax.ppermute(value, "fsdp", pairs)


def run(kernel, outs, scalars, arrays, waits=(), aliases=None, scratch=()):
    whole = pl.BlockSpec(memory_space=pltpu.VMEM)
    taken = 1 + len(arrays)

    def only(*refs):
        kernel(*refs[:taken], *refs[taken + len(waits):])

    return pl.pallas_call(
        only,
        in_specs=[pl.BlockSpec(memory_space=pltpu.SMEM)] + [whole] * len(arrays)
        + [pl.BlockSpec(memory_space=pl.ANY)] * len(waits),
        out_specs=[whole] * len(outs),
        out_shape=[jax.ShapeDtypeStruct(shape, dtype) for shape, dtype in outs],
        scratch_shapes=list(scratch),
        input_output_aliases=aliases or {},
        compiler_params=pltpu.CompilerParams(vmem_limit_bytes=8 * 1024 * 1024),
        cost_estimate=pl.CostEstimate(flops=1000000, bytes_accessed=100000, transcendentals=0),
    )(scalars, *arrays, *waits)


def tied_kernel(*refs):
    pass


def after(value, *others):
    anywhere = pl.BlockSpec(memory_space=pl.ANY)
    return pl.pallas_call(
        tied_kernel,
        in_specs=[anywhere] * (1 + len(others)),
        out_specs=anywhere,
        out_shape=jax.ShapeDtypeStruct(value.shape, value.dtype),
        input_output_aliases={0: 0},
        cost_estimate=pl.CostEstimate(flops=0, bytes_accessed=0, transcendentals=0),
    )(value, *others)


class Ring:
    def __init__(self, shard):
        self.chips, self.step = lax.axis_size("fsdp") // 2, 0
        self.moving, self.found = {1: shard, -1: shard}, {0: [(0, shard)]}

    def advance(self, *others):
        self.step += 1
        for way in (1, -1):
            value = along_ring(self.moving[way], way)
            self.moving[way] = after(value, *others) if others else value
            self.found[-way * self.step % self.chips] = [(0, self.moving[way])]

    def finish(self, halved):
        if halved:
            half = self.moving[1].shape[0] // 2
            last = [(0, along_ring(self.moving[1][:half], 1)), (half, along_ring(self.moving[-1][half:], -1))]
        else:
            last = [(0, along_ring(self.moving[1], 1))]
        self.found[self.chips // 2] = last

    def get(self, *distances):
        return [piece for d in distances for _, piece in self.found[d]]


def block(index, size):
    return pl.ds(pl.multiple_of(index * size, size), size)


def split_kernel(norm, scal_ref, rows_ref, kept_ref, sent_ref):
    core = scal_ref[0]
    count, width = rows_ref.shape
    size, some = 256, 64
    for first in range(0, count, some):
        at = slice(first, first + some)
        if norm:
            values = rows_ref[at, :].astype(jnp.float32)
            scale = lax.rsqrt(jnp.mean(values * values, axis=1, keepdims=True) + 1e-05)
        for j in range(width // (2 * size)):
            for out_ref, which in ((kept_ref, core), (sent_ref, 1 - core)):
                part = rows_ref[at, block(2 * j + which, size)]
                if norm:
                    part = (part.astype(jnp.float32) * scale).astype(jnp.bfloat16)
                out_ref[at, j * size:(j + 1) * size] = part


def keyval_kernel(distances, scal_ref, segs_ref, own_ref, other_ref, *refs):
    weights, (kept_ref, sent_ref) = refs[: len(distances)], refs[len(distances):]
    core = scal_ref[0]
    rows = own_ref.shape[0]
    lane = lax.broadcasted_iota(jnp.int32, (rows, 128), 1)
    for rows_ref, which in ((own_ref, core), (other_ref, 1 - core)):
        total = None
        for distance, weight_ref in zip(distances, weights):
            found = jnp.dot(
                rows_ref[:, block(scal_ref[2 + distance], weight_ref.shape[0])], weight_ref[...],
                preferred_element_type=jnp.float32,
            )
            total = found if total is None else total + found
        for part in range(2):
            low = total[:, part * 256:part * 256 + 128]
            high = total[:, part * 256 + 128:part * 256 + 256]
            zero = jnp.where(lane < HEAD_SIZE, low, pltpu.roll(high, HEAD_SIZE, 1))
            one = jnp.where(lane < HEAD_SIZE, pltpu.roll(low, HEAD_SIZE, 1), high)
            at = slice(part * 128, part * 128 + 128)
            kept_ref[block(which, rows), at] = jnp.where(core == 0, zero, one)
            sent_ref[block(which, rows), at] = jnp.where(core == 0, one, zero)
    marks = (segs_ref[...] + 1).astype(jnp.float32)
    sent_ref[2 * rows:, :] = jnp.broadcast_to(marks, (8, marks.shape[1]))


def parcel_kernel(scal_ref, segs_ref, kept_ref, received_ref, out_ref):
    core = scal_ref[0]
    count = kept_ref.shape[0]
    out_ref[:count, :] = (kept_ref[...] + received_ref[:count, :]).astype(out_ref.dtype)
    own = (segs_ref[...] + 1).astype(jnp.float32)
    other = received_ref[count:count + 1, :]
    first, second = jnp.where(core == 0, own, other), jnp.where(core == 0, other, own)
    row = lax.broadcasted_iota(jnp.int32, (MARK_ROWS, own.shape[1]), 0)
    marks = jnp.where(row == 0, first, jnp.where(row == 1, second, 0.0))
    out_ref[count:, :] = marks.astype(out_ref.dtype)


def copy_kernel(scal_ref, in_ref, out_ref):
    out_ref[...] = in_ref[...]


def window_kernel(scal_ref, four_ref, two_ref, own_ref, crossed_ref, *refs):
    kt_refs, v_refs, lo_ref = refs[:2], refs[2:4], refs[4]
    odd = scal_ref[1]
    length = own_ref.shape[0]
    count = length - MARK_ROWS
    half = count // 2
    second = pl.multiple_of(odd * length, MARK_ROWS)
    fourth = pl.multiple_of((1 - odd) * length, MARK_ROWS)
    places = [(four_ref, 0), (crossed_ref, second), (two_ref, 0), (crossed_ref, fourth), (own_ref, 0)]
    lane = lax.broadcasted_iota(jnp.int32, (count, 128), 1)
    blank = jnp.zeros((HEAD_SIZE, count), jnp.bfloat16)
    marks = []
    for i, (ref, first) in enumerate(places):
        at = slice(i * count, (i + 1) * count)
        keys = ref[pl.ds(first, count), 0:128].astype(jnp.float32).T.astype(jnp.bfloat16)
        values = ref[pl.ds(first, count), 128:256].astype(jnp.float32)
        turned = pltpu.roll(values, HEAD_SIZE, 1)
        for g in range(2):
            head = keys[g * HEAD_SIZE:(g + 1) * HEAD_SIZE]
            kt_refs[g][0, :HEAD_SIZE, at] = head
            kt_refs[g][0, HEAD_SIZE:, at] = blank
            kt_refs[g][1, :HEAD_SIZE, at] = blank
            kt_refs[g][1, HEAD_SIZE:, at] = head
            low, high = (values, turned) if g == 0 else (turned, values)
            v_refs[g][0, at, :] = jnp.where(lane < HEAD_SIZE, low, 0.0).astype(jnp.bfloat16)
            v_refs[g][1, at, :] = jnp.where(lane < HEAD_SIZE, 0.0, high).astype(jnp.bfloat16)
        found = ref[pl.ds(first + count, MARK_ROWS), :].astype(jnp.float32)
        marks += [found[0:1, :], found[1:2, :]]
    across = lax.broadcasted_iota(jnp.int32, (half, half), 1)
    down = lax.broadcasted_iota(jnp.int32, (half, half), 0)
    for part in range(2):
        mine = jnp.sum(jnp.where(across == down, marks[-2 + part], 0.0), axis=1, keepdims=True)
        earlier = jnp.zeros((half, half), jnp.float32)
        for row in marks:
            earlier = earlier + jnp.where(row < mine, 1.0, 0.0)
        earlier = jnp.sum(earlier, axis=1, keepdims=True).astype(jnp.int32)
        place = lax.broadcasted_iota(jnp.int32, (half, 128), 0) + (part * half + 1)
        lo_ref[part * half:(part + 1) * half, :] = jnp.maximum(earlier, place)


def query_kernel(pieces, g, more, scal_ref, own_ref, other_ref, *refs):
    weights, refs = refs[: len(pieces)], refs[len(pieces):]
    core = scal_ref[0]
    rows = own_ref.shape[0]
    outs = refs[-2:]
    for rows_ref, which in ((own_ref, core), (other_ref, 1 - core)):
        at = block(which, rows)
        for i, column in enumerate((core, 1 - core)):
            total = refs[i][at, :] if more else None
            for (distance, first), weight_ref in zip(pieces, weights):
                depth = weight_ref.shape[0]
                start = pl.multiple_of(scal_ref[2 + distance] * rows + first, depth)
                found = jnp.dot(
                    rows_ref[:, pl.ds(start, depth)], weight_ref[:, block(2 * g + column, GROUP_WIDTH)],
                    preferred_element_type=jnp.float32,
                )
                total = found if total is None else total + found
            outs[i][at, :] = total


def attention_kernel(tile, lo_ref, kept_ref, received_ref, kt_ref, v_ref, *refs):
    out_ref, query_ref, score_ref = refs[-3:]
    start = tile * TILE
    mine = slice(start, start + TILE)
    span = LOOKBACK_SPAN + TILE
    lo = lo_ref[mine, :] - start
    lane = lax.broadcasted_iota(jnp.int32, (TILE, 128), 1)
    row = lax.broadcasted_iota(jnp.int32, (TILE, 128), 0)
    blocks = span // TILE
    queries = (kept_ref[mine, :] + received_ref[mine, :]).astype(jnp.bfloat16)
    query_ref[...] = queries * jnp.bfloat16(HEAD_SIZE ** -0.5)

    def scores_of(pair, parity):
        q = query_ref[:, pair * 128:(pair + 1) * 128]
        peak = jnp.full((TILE, 128), MASKED, jnp.float32)
        for i in range(blocks):
            first = start + i * TILE
            found = jnp.dot(q, kt_ref[parity, :, pl.ds(first, TILE)], preferred_element_type=jnp.float32)
            for part in range(TILE // 128):
                at = i * TILE + part * 128
                visible = lane + at >= lo
                if at >= LOOKBACK_SPAN:
                    visible = visible & (lane + (at - LOOKBACK_SPAN) <= row)
                kept = jnp.where(visible, found[:, part * 128:(part + 1) * 128], MASKED)
                peak = jnp.maximum(peak, kept)
                score_ref[parity, :, at:at + 128] = kept
        return jnp.max(peak, axis=1, keepdims=True)

    def mixed_of(parity, peak):
        total = jnp.zeros((TILE, 128), jnp.float32)
        mixed = jnp.zeros((TILE, 128), jnp.float32)
        for i in range(blocks):
            first = start + i * TILE
            weights = jnp.exp(score_ref[parity, :, i * TILE:(i + 1) * TILE] - peak)
            for part in range(TILE // 128):
                total = total + weights[:, part * 128:(part + 1) * 128]
            mixed = mixed + jnp.dot(
                weights.astype(jnp.bfloat16), v_ref[parity, pl.ds(first, TILE), :],
                preferred_element_type=jnp.float32,
            )
        return mixed * (1.0 / jnp.sum(total, axis=1, keepdims=True))

    if tile:
        out_ref[:start, :] = refs[0][:start, :]
    for pair in range(GROUP // 2):
        peaks = [scores_of(pair, parity) for parity in range(2)]
        parts = [mixed_of(parity, peaks[parity]) for parity in range(2)]
        out_ref[mine, pair * 128:(pair + 1) * 128] = (parts[0] + parts[1]).astype(out_ref.dtype)


def attention(tile, arrays, before, waits):
    rows = arrays[1].shape[0]
    arrays = list(arrays) + list(before)
    span = LOOKBACK_SPAN + TILE

    def only(*refs):
        attention_kernel(tile, *refs[:len(arrays)], *refs[len(arrays) + len(waits):])

    whole = pl.BlockSpec(memory_space=pltpu.VMEM)
    return pl.pallas_call(
        only,
        in_specs=[whole] * len(arrays) + [pl.BlockSpec(memory_space=pl.ANY)] * len(waits),
        out_specs=whole,
        out_shape=jax.ShapeDtypeStruct((rows, GROUP_WIDTH), jnp.bfloat16),
        scratch_shapes=[
            pltpu.VMEM((TILE, GROUP_WIDTH), jnp.bfloat16), pltpu.VMEM((2, TILE, span), jnp.float32)
        ],
        compiler_params=pltpu.CompilerParams(vmem_limit_bytes=16 * 1024 * 1024),
        cost_estimate=pl.CostEstimate(flops=1000000, bytes_accessed=100000, transcendentals=0),
    )(*arrays, *waits)


def out_kernel(distances, mode, scal_ref, *refs):
    attended, refs = refs[:4], refs[4:]
    adds, refs = refs[:2], refs[2:]
    count = sum(len(pieces) for _, pieces in distances)
    weights, refs = refs[:count], refs[count:]
    outs = refs[-2:]
    core = scal_ref[0]
    rows = adds[0].shape[0]
    depth = attended[0].shape[1]
    if mode != "alone":
        for i in range(2):
            outs[i][...] = jnp.zeros_like(outs[i])
    for i, which in enumerate((core, 1 - core)):
        taken = 0
        for distance, pieces in distances:
            shard = weights[taken:taken + len(pieces)]
            taken += len(pieces)
            columns = shard[0].shape[1]
            at = block(scal_ref[2 + distance], columns)
            total = adds[i][:, at].astype(jnp.float32)
            for g in range(2):
                ref, first = shard[g * len(shard) // 2], 2 * g if len(shard) == 1 else 0
                for side, column in enumerate((core, 1 - core)):
                    total = total + jnp.dot(
                        attended[2 * g + side][block(which, rows), :],
                        ref[block(first + column, depth), :],
                        preferred_element_type=jnp.float32,
                    )
            if mode == "alone":
                outs[i][...] = total.astype(outs[i].dtype)
            else:
                outs[i][:, at] = total.astype(outs[i].dtype)


def join_kernel(last, scal_ref, own_ref, other_ref, own_last_ref, other_last_ref, out_ref):
    core = scal_ref[0]
    size = own_last_ref.shape[1]
    for j in range(own_ref.shape[1] // size):
        at = slice(j * size, (j + 1) * size)
        out_ref[:, block(2 * j + core, size)] = own_ref[:, at]
        out_ref[:, block(2 * j + 1 - core, size)] = other_ref[:, at]
    j = scal_ref[2 + last]
    out_ref[:, block(2 * j + core, size)] = own_last_ref[...]
    out_ref[:, block(2 * j + 1 - core, size)] = other_last_ref[...]


def body(section_input, segment_ids, query_weight, keyval_weight, out_weight):
    hidden = section_input[0]
    rows, width = hidden.shape
    device = lax.axis_index("fsdp")
    chips = lax.axis_size("fsdp") // 2
    order = ring_order(chips)
    table = []
    for i in range(2 * chips):
        place = order.index(i // 2)
        table.append([i % 2, i // 2 % 2] + [order[(place + d) % chips] for d in range(chips)])
    scalars = lax.dynamic_index_in_dim(jnp.array(table, jnp.int32), device, 0, keepdims=False)

    keyval = Ring(keyval_weight[0])
    keyval.advance()
    keyval.advance()
    keyval.advance()
    keyval.finish(halved=False)

    half = ((rows, width // 2), jnp.bfloat16)
    own_rows, sent_rows = run(functools.partial(split_kernel, True), [half, half], scalars, [hidden])
    other_rows = swap_cores(sent_rows)

    query_shard, = run(
        copy_kernel, [(query_weight.shape[1:], jnp.bfloat16)], scalars, [query_weight[0]],
        waits=keyval.get(3, chips - 3, chips // 2) + [other_rows],
    )
    kept, sent = run(
        functools.partial(keyval_kernel, list(range(chips))),
        [((2 * rows, 256), jnp.float32), ((2 * rows + 8, 256), jnp.float32)],
        scalars, [segment_ids, own_rows, other_rows] + keyval.get(*range(chips)),
    )
    parcel, = run(
        parcel_kernel, [((2 * rows + MARK_ROWS, 256), jnp.bfloat16)], scalars,
        [segment_ids, kept, swap_cores(sent)],
    )
    def query_sums(distances, g, waits, before=()):
        pieces = [(d, first) for d in distances for first, _ in query.found[d]]
        return run(
            functools.partial(query_kernel, pieces, g, bool(before)),
            [((2 * rows, GROUP_WIDTH), jnp.float32)] * 2, scalars,
            [own_rows, other_rows] + query.get(*distances) + list(before), waits=waits,
        )

    near = [0, 1, chips - 1, 2, chips - 2]
    next_far = [3, chips - 3]
    far = [chips // 2]
    query = Ring(query_shard)
    query.advance(parcel)
    back_two = two_chips_on(parcel)
    out_shard = to_next_section(out_weight[0])
    query.advance(back_two, out_shard)
    sums = [query_sums(near, g, [parcel]) for g in range(2)]
    back_four = two_chips_on(back_two)
    query.advance(back_four, sums[0][0], sums[1][0])
    even = device // 2 % 2 == 0
    crossed = swap_chips(jnp.concatenate([jnp.where(even, parcel, back_four), back_two], axis=0))
    query.finish(halved=True)
    out = Ring(after(out_shard, crossed, *query.get(*far)))
    window = 5 * 2 * rows
    *heads, lowest = run(
        window_kernel,
        [((2, 128, window), jnp.bfloat16)] * 2 + [((2, window, 128), jnp.bfloat16)] * 2
        + [((2 * rows, 128), jnp.int32)],
        scalars, [back_four, back_two, parcel, crossed],
    )
    sums = [query_sums(next_far + far, g, [lowest] + out.get(0), sums[g]) for g in range(2)]
    given = [(lowest, sums[g][0], swap_cores(sums[g][1]), heads[g], heads[2 + g]) for g in range(2)]
    out.advance()
    attended = [attention(0, given[0], [], [])]
    attended[0] = attention(1, given[0], attended[:1], out.get(1, chips - 1))
    out.advance()
    attended.append(attention(0, given[1], [], attended[:1]))
    attended[1] = attention(1, given[1], attended[1:], out.get(2, chips - 2))
    out.advance()
    out.finish(halved=True)
    kept, sent = run(
        functools.partial(split_kernel, False), [half, half], scalars, [to_next_section(hidden)], waits=attended[:1]
    )
    adds = [kept, swap_cores(sent)]
    arrived = []
    for g in range(2):
        mine = to_next_section(attended[g])
        arrived += [mine, swap_cores(mine)]

    def made(some, mode):
        distances = [(d, [first for first, _ in out.found[d]]) for d in some]
        outs = [((rows, out_shard.shape[1]), jnp.bfloat16)] * 2 if mode == "alone" else [half, half]
        return run(
            functools.partial(out_kernel, distances, mode), outs, scalars, arrived + adds + out.get(*some)
        )

    most = made(near + next_far, "first")
    other_most = swap_cores(most[1])
    last = made(far, "alone")
    joined, = run(
        functools.partial(join_kernel, chips // 2), [((rows, width), jnp.bfloat16)], scalars,
        [most[0], other_most, last[0], swap_cores(last[1])],
    )
    return joined[None]


def solution(mesh):
    return jax.shard_map(
        body,
        mesh=mesh,
        in_specs=(
            P("section", "fsdp", None),
            P("section", "fsdp"),
            P("section", "fsdp", None),
            P("section", "fsdp", None),
            P("section", None, "fsdp"),
        ),
        out_specs=P("section", "fsdp", None),
        check_vma=False,
    )
```

```python
import functools

import jax
import jax.numpy as jnp
from jax import lax
from jax.experimental import pallas as pl
from jax.experimental.pallas import tpu as pltpu
from jax.sharding import PartitionSpec as P

QUERY_HEADS = 32
KEY_HEADS = 4
HEAD_SIZE = 64
LOOKBACK_SPAN = 2048
GROUP = QUERY_HEADS // KEY_HEADS
GROUP_WIDTH = GROUP * HEAD_SIZE
TILE = 256
MASKED = -1e30
MARK_ROWS = 16


def ring_order(chips):
    return list(range(0, chips, 2)) + list(range(chips - 1, 0, -2))


def swap_cores(value):
    count = lax.axis_size("fsdp")
    return lax.ppermute(value, "fsdp", [(i, i ^ 1) for i in range(count)])


def swap_chips(value):
    count = lax.axis_size("fsdp")
    return lax.ppermute(value, "fsdp", [(i, i ^ 2) for i in range(count)])


def two_chips_on(value):
    count = lax.axis_size("fsdp")
    return lax.ppermute(value, "fsdp", [(i, i + 4) for i in range(count - 4)])


def to_next_section(value):
    count = lax.axis_size("section")
    return lax.ppermute(value, "section", [(i, (i + 1) % count) for i in range(count)])


def along_ring(value, step):
    chips = lax.axis_size("fsdp") // 2
    order = ring_order(chips)
    pairs = []
    for place in range(chips):
        target = order[(place + step) % chips]
        pairs += [(2 * order[place] + core, 2 * target + core) for core in range(2)]
    return lax.ppermute(value, "fsdp", pairs)


def run(kernel, outs, scalars, arrays, waits=(), aliases=None, scratch=()):
    whole = pl.BlockSpec(memory_space=pltpu.VMEM)
    taken = 1 + len(arrays)

    def only(*refs):
        kernel(*refs[:taken], *refs[taken + len(waits):])

    return pl.pallas_call(
        only,
        in_specs=[pl.BlockSpec(memory_space=pltpu.SMEM)] + [whole] * len(arrays)
        + [pl.BlockSpec(memory_space=pl.ANY)] * len(waits),
        out_specs=[whole] * len(outs),
        out_shape=[jax.ShapeDtypeStruct(shape, dtype) for shape, dtype in outs],
        scratch_shapes=list(scratch),
        input_output_aliases=aliases or {},
        compiler_params=pltpu.CompilerParams(vmem_limit_bytes=8 * 1024 * 1024),
        cost_estimate=pl.CostEstimate(flops=1000000, bytes_accessed=100000, transcendentals=0),
    )(scalars, *arrays, *waits)


def tied_kernel(*refs):
    pass


def after(value, *others):
    anywhere = pl.BlockSpec(memory_space=pl.ANY)
    return pl.pallas_call(
        tied_kernel,
        in_specs=[anywhere] * (1 + len(others)),
        out_specs=anywhere,
        out_shape=jax.ShapeDtypeStruct(value.shape, value.dtype),
        input_output_aliases={0: 0},
        cost_estimate=pl.CostEstimate(flops=0, bytes_accessed=0, transcendentals=0),
    )(value, *others)


class Ring:
    def __init__(self, shard):
        self.chips, self.step = lax.axis_size("fsdp") // 2, 0
        self.moving, self.found = {1: shard, -1: shard}, {0: [(0, shard)]}

    def advance(self, *others):
        self.step += 1
        for way in (1, -1):
            value = along_ring(self.moving[way], way)
            self.moving[way] = after(value, *others) if others else value
            self.found[-way * self.step % self.chips] = [(0, self.moving[way])]

    def finish(self, halved):
        if halved:
            half = self.moving[1].shape[0] // 2
            last = [(0, along_ring(self.moving[1][:half], 1)), (half, along_ring(self.moving[-1][half:], -1))]
        else:
            last = [(0, along_ring(self.moving[1], 1))]
        self.found[self.chips // 2] = last

    def get(self, *distances):
        return [piece for d in distances for _, piece in self.found[d]]


def block(index, size):
    return pl.ds(pl.multiple_of(index * size, size), size)


def split_kernel(norm, scal_ref, rows_ref, kept_ref, sent_ref):
    core = scal_ref[0]
    count, width = rows_ref.shape
    size, some = 256, 64
    for first in range(0, count, some):
        at = slice(first, first + some)
        if norm:
            values = rows_ref[at, :].astype(jnp.float32)
            scale = lax.rsqrt(jnp.mean(values * values, axis=1, keepdims=True) + 1e-05)
        for j in range(width // (2 * size)):
            for out_ref, which in ((kept_ref, core), (sent_ref, 1 - core)):
                part = rows_ref[at, block(2 * j + which, size)]
                if norm:
                    part = (part.astype(jnp.float32) * scale).astype(jnp.bfloat16)
                out_ref[at, j * size:(j + 1) * size] = part


def keyval_kernel(distances, scal_ref, segs_ref, own_ref, other_ref, *refs):
    weights, (kept_ref, sent_ref) = refs[: len(distances)], refs[len(distances):]
    core = scal_ref[0]
    rows = own_ref.shape[0]
    lane = lax.broadcasted_iota(jnp.int32, (rows, 128), 1)
    for rows_ref, which in ((own_ref, core), (other_ref, 1 - core)):
        total = None
        for distance, weight_ref in zip(distances, weights):
            found = jnp.dot(
                rows_ref[:, block(scal_ref[2 + distance], weight_ref.shape[0])], weight_ref[...],
                preferred_element_type=jnp.float32,
            )
            total = found if total is None else total + found
        for part in range(2):
            low = total[:, part * 256:part * 256 + 128]
            high = total[:, part * 256 + 128:part * 256 + 256]
            zero = jnp.where(lane < HEAD_SIZE, low, pltpu.roll(high, HEAD_SIZE, 1))
            one = jnp.where(lane < HEAD_SIZE, pltpu.roll(low, HEAD_SIZE, 1), high)
            at = slice(part * 128, part * 128 + 128)
            kept_ref[block(which, rows), at] = jnp.where(core == 0, zero, one)
            sent_ref[block(which, rows), at] = jnp.where(core == 0, one, zero)
    marks = (segs_ref[...] + 1).astype(jnp.float32)
    sent_ref[2 * rows:, :] = jnp.broadcast_to(marks, (8, marks.shape[1]))


def parcel_kernel(scal_ref, segs_ref, kept_ref, received_ref, out_ref):
    core = scal_ref[0]
    count = kept_ref.shape[0]
    out_ref[:count, :] = (kept_ref[...] + received_ref[:count, :]).astype(out_ref.dtype)
    own = (segs_ref[...] + 1).astype(jnp.float32)
    other = received_ref[count:count + 1, :]
    first, second = jnp.where(core == 0, own, other), jnp.where(core == 0, other, own)
    row = lax.broadcasted_iota(jnp.int32, (MARK_ROWS, own.shape[1]), 0)
    marks = jnp.where(row == 0, first, jnp.where(row == 1, second, 0.0))
    out_ref[count:, :] = marks.astype(out_ref.dtype)


def copy_kernel(scal_ref, in_ref, out_ref):
    out_ref[...] = in_ref[...]


def window_kernel(scal_ref, four_ref, two_ref, own_ref, crossed_ref, *refs):
    kt_refs, v_refs, lo_ref = refs[:2], refs[2:4], refs[4]
    odd = scal_ref[1]
    length = own_ref.shape[0]
    count = length - MARK_ROWS
    half = count // 2
    second = pl.multiple_of(odd * length, MARK_ROWS)
    fourth = pl.multiple_of((1 - odd) * length, MARK_ROWS)
    places = [(four_ref, 0), (crossed_ref, second), (two_ref, 0), (crossed_ref, fourth), (own_ref, 0)]
    lane = lax.broadcasted_iota(jnp.int32, (count, 128), 1)
    blank = jnp.zeros((HEAD_SIZE, count), jnp.bfloat16)
    marks = []
    for i, (ref, first) in enumerate(places):
        at = slice(i * count, (i + 1) * count)
        keys = ref[pl.ds(first, count), 0:128].astype(jnp.float32).T.astype(jnp.bfloat16)
        values = ref[pl.ds(first, count), 128:256].astype(jnp.float32)
        turned = pltpu.roll(values, HEAD_SIZE, 1)
        for g in range(2):
            head = keys[g * HEAD_SIZE:(g + 1) * HEAD_SIZE]
            kt_refs[g][0, :HEAD_SIZE, at] = head
            kt_refs[g][0, HEAD_SIZE:, at] = blank
            kt_refs[g][1, :HEAD_SIZE, at] = blank
            kt_refs[g][1, HEAD_SIZE:, at] = head
            low, high = (values, turned) if g == 0 else (turned, values)
            v_refs[g][0, at, :] = jnp.where(lane < HEAD_SIZE, low, 0.0).astype(jnp.bfloat16)
            v_refs[g][1, at, :] = jnp.where(lane < HEAD_SIZE, 0.0, high).astype(jnp.bfloat16)
        found = ref[pl.ds(first + count, MARK_ROWS), :].astype(jnp.float32)
        marks += [found[0:1, :], found[1:2, :]]
    across = lax.broadcasted_iota(jnp.int32, (half, half), 1)
    down = lax.broadcasted_iota(jnp.int32, (half, half), 0)
    for part in range(2):
        mine = jnp.sum(jnp.where(across == down, marks[-2 + part], 0.0), axis=1, keepdims=True)
        earlier = jnp.zeros((half, half), jnp.float32)
        for row in marks:
            earlier = earlier + jnp.where(row < mine, 1.0, 0.0)
        earlier = jnp.sum(earlier, axis=1, keepdims=True).astype(jnp.int32)
        place = lax.broadcasted_iota(jnp.int32, (half, 128), 0) + (part * half + 1)
        lo_ref[part * half:(part + 1) * half, :] = jnp.maximum(earlier, place)


def query_kernel(pieces, g, more, scal_ref, own_ref, other_ref, *refs):
    weights, refs = refs[: len(pieces)], refs[len(pieces):]
    core = scal_ref[0]
    rows = own_ref.shape[0]
    outs = refs[-2:]
    for rows_ref, which in ((own_ref, core), (other_ref, 1 - core)):
        at = block(which, rows)
        for i, column in enumerate((core, 1 - core)):
            total = refs[i][at, :] if more else None
            for (distance, first), weight_ref in zip(pieces, weights):
                depth = weight_ref.shape[0]
                start = pl.multiple_of(scal_ref[2 + distance] * rows + first, depth)
                found = jnp.dot(
                    rows_ref[:, pl.ds(start, depth)], weight_ref[:, block(2 * g + column, GROUP_WIDTH)],
                    preferred_element_type=jnp.float32,
                )
                total = found if total is None else total + found
            outs[i][at, :] = total


def attention_kernel(tile, lo_ref, kept_ref, received_ref, kt_ref, v_ref, *refs):
    out_ref, query_ref, score_ref = refs[-3:]
    start = tile * TILE
    mine = slice(start, start + TILE)
    span = LOOKBACK_SPAN + TILE
    lo = lo_ref[mine, :] - start
    lane = lax.broadcasted_iota(jnp.int32, (TILE, 128), 1)
    row = lax.broadcasted_iota(jnp.int32, (TILE, 128), 0)
    blocks = span // TILE
    queries = (kept_ref[mine, :] + received_ref[mine, :]).astype(jnp.bfloat16)
    query_ref[...] = queries * jnp.bfloat16(HEAD_SIZE ** -0.5)

    def scores_of(pair, parity):
        q = query_ref[:, pair * 128:(pair + 1) * 128]
        peak = jnp.full((TILE, 128), MASKED, jnp.float32)
        for i in range(blocks):
            first = start + i * TILE
            found = jnp.dot(q, kt_ref[parity, :, pl.ds(first, TILE)], preferred_element_type=jnp.float32)
            for part in range(TILE // 128):
                at = i * TILE + part * 128
                visible = lane + at >= lo
                if at >= LOOKBACK_SPAN:
                    visible = visible & (lane + (at - LOOKBACK_SPAN) <= row)
                kept = jnp.where(visible, found[:, part * 128:(part + 1) * 128], MASKED)
                peak = jnp.maximum(peak, kept)
                score_ref[parity, :, at:at + 128] = kept
        return jnp.max(peak, axis=1, keepdims=True)

    def mixed_of(parity, peak):
        total = jnp.zeros((TILE, 128), jnp.float32)
        mixed = jnp.zeros((TILE, 128), jnp.float32)
        for i in range(blocks):
            first = start + i * TILE
            weights = jnp.exp(score_ref[parity, :, i * TILE:(i + 1) * TILE] - peak)
            for part in range(TILE // 128):
                total = total + weights[:, part * 128:(part + 1) * 128]
            mixed = mixed + jnp.dot(
                weights.astype(jnp.bfloat16), v_ref[parity, pl.ds(first, TILE), :],
                preferred_element_type=jnp.float32,
            )
        return mixed * (1.0 / jnp.sum(total, axis=1, keepdims=True))

    if tile:
        out_ref[:start, :] = refs[0][:start, :]
    for pair in range(GROUP // 2):
        peaks = [scores_of(pair, parity) for parity in range(2)]
        parts = [mixed_of(parity, peaks[parity]) for parity in range(2)]
        out_ref[mine, pair * 128:(pair + 1) * 128] = (parts[0] + parts[1]).astype(out_ref.dtype)


def attention(tile, arrays, before, waits):
    rows = arrays[1].shape[0]
    arrays = list(arrays) + list(before)
    span = LOOKBACK_SPAN + TILE

    def only(*refs):
        attention_kernel(tile, *refs[:len(arrays)], *refs[len(arrays) + len(waits):])

    whole = pl.BlockSpec(memory_space=pltpu.VMEM)
    return pl.pallas_call(
        only,
        in_specs=[whole] * len(arrays) + [pl.BlockSpec(memory_space=pl.ANY)] * len(waits),
        out_specs=whole,
        out_shape=jax.ShapeDtypeStruct((rows, GROUP_WIDTH), jnp.bfloat16),
        scratch_shapes=[
            pltpu.VMEM((TILE, GROUP_WIDTH), jnp.bfloat16), pltpu.VMEM((2, TILE, span), jnp.float32)
        ],
        compiler_params=pltpu.CompilerParams(vmem_limit_bytes=16 * 1024 * 1024),
        cost_estimate=pl.CostEstimate(flops=1000000, bytes_accessed=100000, transcendentals=0),
    )(*arrays, *waits)


def out_kernel(distances, mode, scal_ref, *refs):
    attended, refs = refs[:4], refs[4:]
    adds, refs = refs[:2], refs[2:]
    count = sum(len(pieces) for _, pieces in distances)
    weights, refs = refs[:count], refs[count:]
    outs = refs[-2:]
    core = scal_ref[0]
    rows = adds[0].shape[0]
    depth = attended[0].shape[1]
    if mode != "alone":
        for i in range(2):
            outs[i][...] = jnp.zeros_like(outs[i])
    for i, which in enumerate((core, 1 - core)):
        taken = 0
        for j, (distance, pieces) in enumerate(distances):
            shard = weights[taken:taken + len(pieces)]
            taken += len(pieces)
            columns = shard[0].shape[1]
            at = block(scal_ref[2 + distance], columns)
            total = adds[i][:, at].astype(jnp.float32)
            for g in range(2):
                ref, first = shard[g * len(shard) // 2], 2 * g if len(shard) == 1 else 0
                for side, column in enumerate((core, 1 - core)):
                    total = total + jnp.dot(
                        attended[2 * g + side][block(which, rows), :],
                        ref[block(first + column, depth), :],
                        preferred_element_type=jnp.float32,
                    )
            if mode == "alone":
                outs[i][:, j * columns:(j + 1) * columns] = total.astype(outs[i].dtype)
            else:
                outs[i][:, at] = total.astype(outs[i].dtype)


def join_kernel(last, scal_ref, own_ref, other_ref, own_last_ref, other_last_ref, out_ref):
    core = scal_ref[0]
    size = 256
    for j in range(own_ref.shape[1] // size):
        at = slice(j * size, (j + 1) * size)
        out_ref[:, block(2 * j + core, size)] = own_ref[:, at]
        out_ref[:, block(2 * j + 1 - core, size)] = other_ref[:, at]
    for i, distance in enumerate(last):
        at = slice(i * size, (i + 1) * size)
        j = scal_ref[2 + distance]
        out_ref[:, block(2 * j + core, size)] = own_last_ref[:, at]
        out_ref[:, block(2 * j + 1 - core, size)] = other_last_ref[:, at]


def body(section_input, segment_ids, query_weight, keyval_weight, out_weight):
    hidden = section_input[0]
    rows, width = hidden.shape
    device = lax.axis_index("fsdp")
    chips = lax.axis_size("fsdp") // 2
    order = ring_order(chips)
    table = []
    for i in range(2 * chips):
        place = order.index(i // 2)
        table.append([i % 2, i // 2 % 2] + [order[(place + d) % chips] for d in range(chips)])
    scalars = lax.dynamic_index_in_dim(jnp.array(table, jnp.int32), device, 0, keepdims=False)

    keyval = Ring(keyval_weight[0])
    keyval.advance()
    keyval.advance()
    keyval.advance()
    keyval.finish(halved=False)

    half = ((rows, width // 2), jnp.bfloat16)
    own_rows, sent_rows = run(functools.partial(split_kernel, True), [half, half], scalars, [hidden])
    other_rows = swap_cores(sent_rows)

    query_shard, = run(
        copy_kernel, [(query_weight.shape[1:], jnp.bfloat16)], scalars, [query_weight[0]],
        waits=keyval.get(3, chips - 3, chips // 2) + [other_rows],
    )
    kept, sent = run(
        functools.partial(keyval_kernel, list(range(chips))),
        [((2 * rows, 256), jnp.float32), ((2 * rows + 8, 256), jnp.float32)],
        scalars, [segment_ids, own_rows, other_rows] + keyval.get(*range(chips)),
    )
    parcel, = run(
        parcel_kernel, [((2 * rows + MARK_ROWS, 256), jnp.bfloat16)], scalars,
        [segment_ids, kept, swap_cores(sent)],
    )
    def query_sums(distances, g, waits, before=()):
        pieces = [(d, first) for d in distances for first, _ in query.found[d]]
        return run(
            functools.partial(query_kernel, pieces, g, bool(before)),
            [((2 * rows, GROUP_WIDTH), jnp.float32)] * 2, scalars,
            [own_rows, other_rows] + query.get(*distances) + list(before), waits=waits,
        )

    near = [0, 1, chips - 1, 2, chips - 2]
    next_far = [3, chips - 3]
    far = [chips // 2]
    query = Ring(query_shard)
    query.advance(parcel)
    back_two = two_chips_on(parcel)
    out_shard = to_next_section(out_weight[0])
    query.advance(back_two, out_shard)
    sums = [query_sums(near, g, [parcel]) for g in range(2)]
    back_four = two_chips_on(after(back_two, sums[0][0], sums[1][0]))
    query.advance(back_four)
    even = device // 2 % 2 == 0
    crossed = swap_chips(jnp.concatenate([jnp.where(even, parcel, back_four), back_two], axis=0))
    query.finish(halved=True)
    out = Ring(after(out_shard, crossed, *query.get(*far)))
    window = 5 * 2 * rows
    *heads, lowest = run(
        window_kernel,
        [((2, 128, window), jnp.bfloat16)] * 2 + [((2, window, 128), jnp.bfloat16)] * 2
        + [((2 * rows, 128), jnp.int32)],
        scalars, [back_four, back_two, parcel, crossed],
    )
    sums = [query_sums(next_far + far, g, [lowest] + out.get(0), sums[g]) for g in range(2)]
    given = [(lowest, sums[g][0], swap_cores(sums[g][1]), heads[g], heads[2 + g]) for g in range(2)]
    out.advance()
    attended = [attention(0, given[0], [], [])]
    attended[0] = attention(1, given[0], attended[:1], out.get(1, chips - 1))
    out.advance()
    attended.append(attention(0, given[1], [], attended[:1]))
    attended[1] = attention(1, given[1], attended[1:], out.get(2, chips - 2))
    out.advance()
    out.finish(halved=True)
    kept, sent = run(
        functools.partial(split_kernel, False), [half, half], scalars, [to_next_section(hidden)], waits=attended[:1]
    )
    adds = [kept, swap_cores(sent)]
    arrived = []
    for g in range(2):
        mine = to_next_section(attended[g])
        if g:
            mine = after(mine, *out.get(*next_far))
        arrived += [mine, swap_cores(mine)]

    def made(some, mode):
        distances = [(d, [first for first, _ in out.found[d]]) for d in some]
        outs = [((rows, len(some) * out_shard.shape[1]), jnp.bfloat16)] * 2 if mode == "alone" else [half, half]
        return run(
            functools.partial(out_kernel, distances, mode), outs, scalars, arrived + adds + out.get(*some)
        )

    most = made(near, "first")
    other_most = swap_cores(most[1])
    last = made(next_far + far, "alone")
    joined, = run(
        functools.partial(join_kernel, next_far + far), [((rows, width), jnp.bfloat16)], scalars,
        [most[0], other_most, last[0], swap_cores(last[1])],
    )
    return joined[None]


def solution(mesh):
    return jax.shard_map(
        body,
        mesh=mesh,
        in_specs=(
            P("section", "fsdp", None),
            P("section", "fsdp"),
            P("section", "fsdp", None),
            P("section", "fsdp", None),
            P("section", None, "fsdp"),
        ),
        out_specs=P("section", "fsdp", None),
        check_vma=False,
    )
```

```python
import functools

import jax
import jax.numpy as jnp
from jax import lax
from jax.experimental import pallas as pl
from jax.experimental.pallas import tpu as pltpu
from jax.sharding import PartitionSpec as P

QUERY_HEADS = 32
KEY_HEADS = 4
HEAD_SIZE = 64
LOOKBACK_SPAN = 2048
GROUP = QUERY_HEADS // KEY_HEADS
GROUP_WIDTH = GROUP * HEAD_SIZE
TILE = 256
MASKED = -1e30
MARK_ROWS = 16


def ring_order(chips):
    return list(range(0, chips, 2)) + list(range(chips - 1, 0, -2))


def swap_cores(value):
    count = lax.axis_size("fsdp")
    return lax.ppermute(value, "fsdp", [(i, i ^ 1) for i in range(count)])


def swap_chips(value):
    count = lax.axis_size("fsdp")
    return lax.ppermute(value, "fsdp", [(i, i ^ 2) for i in range(count)])


def two_chips_on(value):
    count = lax.axis_size("fsdp")
    return lax.ppermute(value, "fsdp", [(i, i + 4) for i in range(count - 4)])


def to_next_section(value):
    count = lax.axis_size("section")
    return lax.ppermute(value, "section", [(i, (i + 1) % count) for i in range(count)])


def along_ring(value, step):
    chips = lax.axis_size("fsdp") // 2
    order = ring_order(chips)
    pairs = []
    for place in range(chips):
        target = order[(place + step) % chips]
        pairs += [(2 * order[place] + core, 2 * target + core) for core in range(2)]
    return lax.ppermute(value, "fsdp", pairs)


def run(kernel, outs, scalars, arrays, waits=(), mebibytes=8):
    whole = pl.BlockSpec(memory_space=pltpu.VMEM)
    taken = 1 + len(arrays)

    def only(*refs):
        kernel(*refs[:taken], *refs[taken + len(waits):])

    return pl.pallas_call(
        only,
        in_specs=[pl.BlockSpec(memory_space=pltpu.SMEM)] + [whole] * len(arrays)
        + [pl.BlockSpec(memory_space=pl.ANY)] * len(waits),
        out_specs=[whole] * len(outs),
        out_shape=[jax.ShapeDtypeStruct(shape, dtype) for shape, dtype in outs],
        compiler_params=pltpu.CompilerParams(vmem_limit_bytes=mebibytes * 1024 * 1024),
        cost_estimate=pl.CostEstimate(flops=1000000, bytes_accessed=100000, transcendentals=0),
    )(scalars, *arrays, *waits)


def tied_kernel(*refs):
    pass


def after(value, *others):
    anywhere = pl.BlockSpec(memory_space=pl.ANY)
    return pl.pallas_call(
        tied_kernel,
        in_specs=[anywhere] * (1 + len(others)),
        out_specs=anywhere,
        out_shape=jax.ShapeDtypeStruct(value.shape, value.dtype),
        input_output_aliases={0: 0},
        cost_estimate=pl.CostEstimate(flops=0, bytes_accessed=0, transcendentals=0),
    )(value, *others)


class Ring:
    def __init__(self, shard):
        self.chips, self.step = lax.axis_size("fsdp") // 2, 0
        self.moving, self.found = {1: shard, -1: shard}, {0: [(0, shard)]}

    def advance(self, *others):
        self.step += 1
        for way in (1, -1):
            value = along_ring(self.moving[way], way)
            self.moving[way] = after(value, *others) if others else value
            self.found[-way * self.step % self.chips] = [(0, self.moving[way])]

    def finish(self, halved):
        if halved:
            half = self.moving[1].shape[0] // 2
            last = [(0, along_ring(self.moving[1][:half], 1)), (half, along_ring(self.moving[-1][half:], -1))]
        else:
            last = [(0, along_ring(self.moving[1], 1))]
        self.found[self.chips // 2] = last

    def get(self, *distances):
        return [piece for d in distances for _, piece in self.found[d]]


def block(index, size):
    return pl.ds(pl.multiple_of(index * size, size), size)


def split_kernel(norm, scal_ref, rows_ref, kept_ref, sent_ref):
    core = scal_ref[0]
    count, width = rows_ref.shape
    size, some = 256, 64
    for first in range(0, count, some):
        at = slice(first, first + some)
        if norm:
            values = rows_ref[at, :].astype(jnp.float32)
            scale = lax.rsqrt(jnp.mean(values * values, axis=1, keepdims=True) + 1e-05)
        for j in range(width // (2 * size)):
            for out_ref, which in ((kept_ref, core), (sent_ref, 1 - core)):
                part = rows_ref[at, block(2 * j + which, size)]
                if norm:
                    part = (part.astype(jnp.float32) * scale).astype(jnp.bfloat16)
                out_ref[at, j * size:(j + 1) * size] = part


def keyval_kernel(distances, scal_ref, segs_ref, own_ref, other_ref, *refs):
    weights, (kept_ref, sent_ref) = refs[: len(distances)], refs[len(distances):]
    core = scal_ref[0]
    rows = own_ref.shape[0]
    lane = lax.broadcasted_iota(jnp.int32, (rows, 128), 1)
    for rows_ref, which in ((own_ref, core), (other_ref, 1 - core)):
        total = None
        for distance, weight_ref in zip(distances, weights):
            found = jnp.dot(
                rows_ref[:, block(scal_ref[2 + distance], weight_ref.shape[0])], weight_ref[...],
                preferred_element_type=jnp.float32,
            )
            total = found if total is None else total + found
        for part in range(2):
            low = total[:, part * 256:part * 256 + 128]
            high = total[:, part * 256 + 128:part * 256 + 256]
            zero = jnp.where(lane < HEAD_SIZE, low, pltpu.roll(high, HEAD_SIZE, 1))
            one = jnp.where(lane < HEAD_SIZE, pltpu.roll(low, HEAD_SIZE, 1), high)
            at = slice(part * 128, part * 128 + 128)
            kept_ref[block(which, rows), at] = jnp.where(core == 0, zero, one)
            sent_ref[block(which, rows), at] = jnp.where(core == 0, one, zero)
    marks = (segs_ref[...] + 1).astype(jnp.float32)
    sent_ref[2 * rows:, :] = jnp.broadcast_to(marks, (8, marks.shape[1]))


def parcel_kernel(scal_ref, segs_ref, kept_ref, received_ref, out_ref):
    core = scal_ref[0]
    count = kept_ref.shape[0]
    out_ref[:count, :] = (kept_ref[...] + received_ref[:count, :]).astype(out_ref.dtype)
    own = (segs_ref[...] + 1).astype(jnp.float32)
    other = received_ref[count:count + 1, :]
    first, second = jnp.where(core == 0, own, other), jnp.where(core == 0, other, own)
    row = lax.broadcasted_iota(jnp.int32, (MARK_ROWS, own.shape[1]), 0)
    marks = jnp.where(row == 0, first, jnp.where(row == 1, second, 0.0))
    out_ref[count:, :] = marks.astype(out_ref.dtype)


def copy_kernel(scal_ref, in_ref, out_ref):
    out_ref[...] = in_ref[...]


def window_kernel(scal_ref, four_ref, two_ref, own_ref, crossed_ref, *refs):
    kt_refs, v_refs, lo_ref = refs[:2], refs[2:4], refs[4]
    odd = scal_ref[1]
    length = own_ref.shape[0]
    count = length - MARK_ROWS
    half = count // 2
    second = pl.multiple_of(odd * length, MARK_ROWS)
    fourth = pl.multiple_of((1 - odd) * length, MARK_ROWS)
    places = [(four_ref, 0), (crossed_ref, second), (two_ref, 0), (crossed_ref, fourth), (own_ref, 0)]
    lane = lax.broadcasted_iota(jnp.int32, (count, 128), 1)
    blank = jnp.zeros((HEAD_SIZE, count), jnp.bfloat16)
    marks = []
    for i, (ref, first) in enumerate(places):
        at = slice(i * count, (i + 1) * count)
        keys = ref[pl.ds(first, count), 0:128].astype(jnp.float32).T.astype(jnp.bfloat16)
        values = ref[pl.ds(first, count), 128:256].astype(jnp.float32)
        turned = pltpu.roll(values, HEAD_SIZE, 1)
        for g in range(2):
            head = keys[g * HEAD_SIZE:(g + 1) * HEAD_SIZE]
            kt_refs[g][0, :HEAD_SIZE, at] = head
            kt_refs[g][0, HEAD_SIZE:, at] = blank
            kt_refs[g][1, :HEAD_SIZE, at] = blank
            kt_refs[g][1, HEAD_SIZE:, at] = head
            low, high = (values, turned) if g == 0 else (turned, values)
            v_refs[g][0, at, :] = jnp.where(lane < HEAD_SIZE, low, 0.0).astype(jnp.bfloat16)
            v_refs[g][1, at, :] = jnp.where(lane < HEAD_SIZE, 0.0, high).astype(jnp.bfloat16)
        found = ref[pl.ds(first + count, MARK_ROWS), :].astype(jnp.float32)
        marks += [found[0:1, :], found[1:2, :]]
    across = lax.broadcasted_iota(jnp.int32, (half, half), 1)
    down = lax.broadcasted_iota(jnp.int32, (half, half), 0)
    for part in range(2):
        mine = jnp.sum(jnp.where(across == down, marks[-2 + part], 0.0), axis=1, keepdims=True)
        earlier = jnp.zeros((half, half), jnp.float32)
        for row in marks:
            earlier = earlier + jnp.where(row < mine, 1.0, 0.0)
        earlier = jnp.sum(earlier, axis=1, keepdims=True).astype(jnp.int32)
        place = lax.broadcasted_iota(jnp.int32, (half, 128), 0) + (part * half + 1)
        lo_ref[part * half:(part + 1) * half, :] = jnp.maximum(earlier, place)


def query_kernel(pieces, g, more, scal_ref, own_ref, other_ref, *refs):
    weights, refs = refs[: len(pieces)], refs[len(pieces):]
    core = scal_ref[0]
    rows = own_ref.shape[0]
    outs = refs[-2:]
    for rows_ref, which in ((own_ref, core), (other_ref, 1 - core)):
        at = block(which, rows)
        for i, column in enumerate((core, 1 - core)):
            total = refs[i][at, :] if more else None
            for (distance, first), weight_ref in zip(pieces, weights):
                depth = weight_ref.shape[0]
                start = pl.multiple_of(scal_ref[2 + distance] * rows + first, depth)
                found = jnp.dot(
                    rows_ref[:, pl.ds(start, depth)], weight_ref[:, block(2 * g + column, GROUP_WIDTH)],
                    preferred_element_type=jnp.float32,
                )
                total = found if total is None else total + found
            outs[i][at, :] = total


def attention_kernel(tile, lo_ref, kept_ref, received_ref, kt_ref, v_ref, *refs):
    out_ref, query_ref, score_ref = refs[-3:]
    start = tile * TILE
    mine = slice(start, start + TILE)
    span = LOOKBACK_SPAN + TILE
    lo = lo_ref[mine, :] - start
    lane = lax.broadcasted_iota(jnp.int32, (TILE, 128), 1)
    row = lax.broadcasted_iota(jnp.int32, (TILE, 128), 0)
    blocks = span // TILE
    queries = (kept_ref[mine, :] + received_ref[mine, :]).astype(jnp.bfloat16)
    query_ref[...] = queries * jnp.bfloat16(HEAD_SIZE ** -0.5)

    def scores_of(pair, parity):
        q = query_ref[:, pair * 128:(pair + 1) * 128]
        peak = jnp.full((TILE, 128), MASKED, jnp.float32)
        for i in range(blocks):
            first = start + i * TILE
            found = jnp.dot(q, kt_ref[parity, :, pl.ds(first, TILE)], preferred_element_type=jnp.float32)
            for part in range(TILE // 128):
                at = i * TILE + part * 128
                visible = lane + at >= lo
                if at >= LOOKBACK_SPAN:
                    visible = visible & (lane + (at - LOOKBACK_SPAN) <= row)
                kept = jnp.where(visible, found[:, part * 128:(part + 1) * 128], MASKED)
                peak = jnp.maximum(peak, kept)
                score_ref[parity, :, at:at + 128] = kept
        return jnp.max(peak, axis=1, keepdims=True)

    def mixed_of(parity, peak):
        total = jnp.zeros((TILE, 128), jnp.float32)
        mixed = jnp.zeros((TILE, 128), jnp.float32)
        for i in range(blocks):
            first = start + i * TILE
            weights = jnp.exp(score_ref[parity, :, i * TILE:(i + 1) * TILE] - peak)
            for part in range(TILE // 128):
                total = total + weights[:, part * 128:(part + 1) * 128]
            mixed = mixed + jnp.dot(
                weights.astype(jnp.bfloat16), v_ref[parity, pl.ds(first, TILE), :],
                preferred_element_type=jnp.float32,
            )
        return mixed * (1.0 / jnp.sum(total, axis=1, keepdims=True))

    if tile:
        out_ref[:start, :] = refs[0][:start, :]
    for pair in range(GROUP // 2):
        peaks = [scores_of(pair, parity) for parity in range(2)]
        parts = [mixed_of(parity, peaks[parity]) for parity in range(2)]
        out_ref[mine, pair * 128:(pair + 1) * 128] = (parts[0] + parts[1]).astype(out_ref.dtype)


def attention(tile, arrays, before, waits):
    rows = arrays[1].shape[0]
    arrays = list(arrays) + list(before)
    span = LOOKBACK_SPAN + TILE

    def only(*refs):
        attention_kernel(tile, *refs[:len(arrays)], *refs[len(arrays) + len(waits):])

    whole = pl.BlockSpec(memory_space=pltpu.VMEM)
    return pl.pallas_call(
        only,
        in_specs=[whole] * len(arrays) + [pl.BlockSpec(memory_space=pl.ANY)] * len(waits),
        out_specs=whole,
        out_shape=jax.ShapeDtypeStruct((rows, GROUP_WIDTH), jnp.bfloat16),
        scratch_shapes=[
            pltpu.VMEM((TILE, GROUP_WIDTH), jnp.bfloat16), pltpu.VMEM((2, TILE, span), jnp.float32)
        ],
        compiler_params=pltpu.CompilerParams(vmem_limit_bytes=16 * 1024 * 1024),
        cost_estimate=pl.CostEstimate(flops=1000000, bytes_accessed=100000, transcendentals=0),
    )(*arrays, *waits)


def out_kernel(distances, scal_ref, *refs):
    attended, refs = refs[:4], refs[4:]
    adds, refs = refs[:2], refs[2:]
    weights, outs = refs[:-2], refs[-2:]
    core = scal_ref[0]
    rows = adds[0].shape[0]
    depth = attended[0].shape[1]
    for i, which in enumerate((core, 1 - core)):
        taken = 0
        for distance, pieces in distances:
            shard = weights[taken:taken + len(pieces)]
            taken += len(pieces)
            columns = shard[0].shape[1]
            at = block(scal_ref[2 + distance], columns)
            total = adds[i][:, at].astype(jnp.float32)
            for g in range(2):
                ref, first = shard[g * len(shard) // 2], 2 * g if len(shard) == 1 else 0
                for side, column in enumerate((core, 1 - core)):
                    total = total + jnp.dot(
                        attended[2 * g + side][block(which, rows), :],
                        ref[block(first + column, depth), :],
                        preferred_element_type=jnp.float32,
                    )
            outs[i][:, at] = total.astype(outs[i].dtype)


def join_kernel(scal_ref, own_ref, other_ref, out_ref):
    core = scal_ref[0]
    size = 256
    for j in range(own_ref.shape[1] // size):
        at = slice(j * size, (j + 1) * size)
        out_ref[:, block(2 * j + core, size)] = own_ref[:, at]
        out_ref[:, block(2 * j + 1 - core, size)] = other_ref[:, at]


def body(section_input, segment_ids, query_weight, keyval_weight, out_weight):
    hidden = section_input[0]
    rows, width = hidden.shape
    device = lax.axis_index("fsdp")
    chips = lax.axis_size("fsdp") // 2
    order = ring_order(chips)
    table = []
    for i in range(2 * chips):
        place = order.index(i // 2)
        table.append([i % 2, i // 2 % 2] + [order[(place + d) % chips] for d in range(chips)])
    scalars = lax.dynamic_index_in_dim(jnp.array(table, jnp.int32), device, 0, keepdims=False)

    keyval = Ring(keyval_weight[0])
    keyval.advance()
    keyval.advance()
    keyval.advance()
    keyval.finish(halved=False)

    half = ((rows, width // 2), jnp.bfloat16)
    own_rows, sent_rows = run(functools.partial(split_kernel, True), [half, half], scalars, [hidden])
    other_rows = swap_cores(sent_rows)

    query_shard, = run(
        copy_kernel, [(query_weight.shape[1:], jnp.bfloat16)], scalars, [query_weight[0]],
        waits=keyval.get(3, chips - 3, chips // 2) + [other_rows],
    )
    kept, sent = run(
        functools.partial(keyval_kernel, list(range(chips))),
        [((2 * rows, 256), jnp.float32), ((2 * rows + 8, 256), jnp.float32)],
        scalars, [segment_ids, own_rows, other_rows] + keyval.get(*range(chips)),
    )
    parcel, = run(
        parcel_kernel, [((2 * rows + MARK_ROWS, 256), jnp.bfloat16)], scalars,
        [segment_ids, kept, swap_cores(sent)],
    )
    def query_sums(distances, g, waits, before=()):
        pieces = [(d, first) for d in distances for first, _ in query.found[d]]
        return run(
            functools.partial(query_kernel, pieces, g, bool(before)),
            [((2 * rows, GROUP_WIDTH), jnp.float32)] * 2, scalars,
            [own_rows, other_rows] + query.get(*distances) + list(before), waits=waits,
        )

    near = [0, 1, chips - 1, 2, chips - 2]
    next_far = [3, chips - 3]
    far = [chips // 2]
    query = Ring(query_shard)
    query.advance(parcel)
    back_two = two_chips_on(parcel)
    out_shard = to_next_section(out_weight[0])
    query.advance(back_two, out_shard)
    sums = [query_sums(near, g, [parcel]) for g in range(2)]
    back_four = two_chips_on(after(back_two, sums[0][0], sums[1][0]))
    query.advance(back_four)
    even = device // 2 % 2 == 0
    crossed = swap_chips(jnp.concatenate([jnp.where(even, parcel, back_four), back_two], axis=0))
    query.finish(halved=True)
    out = Ring(after(out_shard, crossed, *query.get(*far)))
    window = 5 * 2 * rows
    *heads, lowest = run(
        window_kernel,
        [((2, 128, window), jnp.bfloat16)] * 2 + [((2, window, 128), jnp.bfloat16)] * 2
        + [((2 * rows, 128), jnp.int32)],
        scalars, [back_four, back_two, parcel, crossed],
    )
    sums = [query_sums(next_far + far, g, [lowest] + out.get(0), sums[g]) for g in range(2)]
    received = [swap_cores(sums[g][1]) for g in range(2)]
    out.advance(lowest, sums[1][0], received[0])
    attended = []
    for g in range(2):
        given = (lowest, sums[g][0], received[g], heads[g], heads[2 + g])
        part = attention(0, given, [], [])
        attended.append(attention(1, given, [part], []))
        out.advance(attended[g])
    out.finish(halved=True)
    kept, sent = run(
        functools.partial(split_kernel, False), [half, half], scalars, [to_next_section(hidden)], waits=attended[:1]
    )
    adds = [kept, swap_cores(sent)]
    arrived = []
    for g in range(2):
        mine = to_next_section(attended[g])
        if g:
            mine = after(mine, *out.get(*far))
        arrived += [mine, swap_cores(mine)]

    made = [(d, [first for first, _ in out.found[d]]) for d in range(chips)]
    own, other = run(
        functools.partial(out_kernel, made), [half, half], scalars, arrived + adds + out.get(*range(chips)),
        mebibytes=32,
    )
    joined, = run(join_kernel, [((rows, width), jnp.bfloat16)], scalars, [own, swap_cores(other)])
    return joined[None]


def solution(mesh):
    return jax.shard_map(
        body,
        mesh=mesh,
        in_specs=(
            P("section", "fsdp", None),
            P("section", "fsdp"),
            P("section", "fsdp", None),
            P("section", "fsdp", None),
            P("section", None, "fsdp"),
        ),
        out_specs=P("section", "fsdp", None),
        check_vma=False,
    )
```

```python
import functools

import jax
import jax.numpy as jnp
from jax import lax
from jax.experimental import pallas as pl
from jax.experimental.pallas import tpu as pltpu
from jax.sharding import PartitionSpec as P

QUERY_HEADS = 32
KEY_HEADS = 4
HEAD_SIZE = 64
LOOKBACK_SPAN = 2048
GROUP = QUERY_HEADS // KEY_HEADS
GROUP_WIDTH = GROUP * HEAD_SIZE
TILE = 256
MASKED = -1e30
MARK_ROWS = 16


def ring_order(chips):
    return list(range(0, chips, 2)) + list(range(chips - 1, 0, -2))


def swap_cores(value):
    count = lax.axis_size("fsdp")
    return lax.ppermute(value, "fsdp", [(i, i ^ 1) for i in range(count)])


def swap_chips(value):
    count = lax.axis_size("fsdp")
    return lax.ppermute(value, "fsdp", [(i, i ^ 2) for i in range(count)])


def two_chips_on(value):
    count = lax.axis_size("fsdp")
    return lax.ppermute(value, "fsdp", [(i, i + 4) for i in range(count - 4)])


def to_next_section(value):
    count = lax.axis_size("section")
    return lax.ppermute(value, "section", [(i, (i + 1) % count) for i in range(count)])


def along_ring(value, step):
    chips = lax.axis_size("fsdp") // 2
    order = ring_order(chips)
    pairs = []
    for place in range(chips):
        target = order[(place + step) % chips]
        pairs += [(2 * order[place] + core, 2 * target + core) for core in range(2)]
    return lax.ppermute(value, "fsdp", pairs)


def run(kernel, outs, scalars, arrays, waits=(), mebibytes=8):
    whole = pl.BlockSpec(memory_space=pltpu.VMEM)
    taken = 1 + len(arrays)

    def only(*refs):
        kernel(*refs[:taken], *refs[taken + len(waits):])

    return pl.pallas_call(
        only,
        in_specs=[pl.BlockSpec(memory_space=pltpu.SMEM)] + [whole] * len(arrays)
        + [pl.BlockSpec(memory_space=pl.ANY)] * len(waits),
        out_specs=[whole] * len(outs),
        out_shape=[jax.ShapeDtypeStruct(shape, dtype) for shape, dtype in outs],
        compiler_params=pltpu.CompilerParams(vmem_limit_bytes=mebibytes * 1024 * 1024),
        cost_estimate=pl.CostEstimate(flops=1000000, bytes_accessed=100000, transcendentals=0),
    )(scalars, *arrays, *waits)


def tied_kernel(*refs):
    pass


def after(value, *others):
    anywhere = pl.BlockSpec(memory_space=pl.ANY)
    return pl.pallas_call(
        tied_kernel,
        in_specs=[anywhere] * (1 + len(others)),
        out_specs=anywhere,
        out_shape=jax.ShapeDtypeStruct(value.shape, value.dtype),
        input_output_aliases={0: 0},
        cost_estimate=pl.CostEstimate(flops=0, bytes_accessed=0, transcendentals=0),
    )(value, *others)


def rows_kernel(first, in_ref, out_ref, sem):
    copy = pltpu.make_async_copy(in_ref.at[pl.ds(first, out_ref.shape[0])], out_ref, sem)
    copy.start()
    copy.wait()


def rows_of(value, first, count):
    anywhere = pl.BlockSpec(memory_space=pl.ANY)
    return pl.pallas_call(
        functools.partial(rows_kernel, first),
        in_specs=[anywhere],
        out_specs=anywhere,
        out_shape=jax.ShapeDtypeStruct((count,) + value.shape[1:], value.dtype),
        scratch_shapes=[pltpu.SemaphoreType.DMA],
        cost_estimate=pl.CostEstimate(flops=0, bytes_accessed=100000, transcendentals=0),
    )(value)


class Ring:
    def __init__(self, shard):
        self.chips, self.step = lax.axis_size("fsdp") // 2, 0
        self.moving, self.found = {1: shard, -1: shard}, {0: [(0, shard)]}

    def advance(self, *others):
        self.step += 1
        for way in (1, -1):
            value = along_ring(self.moving[way], way)
            self.moving[way] = after(value, *others) if others else value
            self.found[-way * self.step % self.chips] = [(0, self.moving[way])]

    def finish(self, halved):
        if halved:
            half = self.moving[1].shape[0] // 2
            last = [
                (0, along_ring(rows_of(self.moving[1], 0, half), 1)),
                (half, along_ring(rows_of(self.moving[-1], half, half), -1)),
            ]
        else:
            last = [(0, along_ring(self.moving[1], 1))]
        self.found[self.chips // 2] = last

    def get(self, *distances):
        return [piece for d in distances for _, piece in self.found[d]]


def block(index, size):
    return pl.ds(pl.multiple_of(index * size, size), size)


def split_kernel(norm, scal_ref, rows_ref, kept_ref, sent_ref):
    core = scal_ref[0]
    count, width = rows_ref.shape
    size, some = 256, 64
    for first in range(0, count, some):
        at = slice(first, first + some)
        if norm:
            values = rows_ref[at, :].astype(jnp.float32)
            scale = lax.rsqrt(jnp.mean(values * values, axis=1, keepdims=True) + 1e-05)
        for j in range(width // (2 * size)):
            for out_ref, which in ((kept_ref, core), (sent_ref, 1 - core)):
                part = rows_ref[at, block(2 * j + which, size)]
                if norm:
                    part = (part.astype(jnp.float32) * scale).astype(jnp.bfloat16)
                out_ref[at, j * size:(j + 1) * size] = part


def keyval_kernel(distances, scal_ref, segs_ref, own_ref, other_ref, *refs):
    weights, (kept_ref, sent_ref) = refs[: len(distances)], refs[len(distances):]
    core = scal_ref[0]
    rows = own_ref.shape[0]
    lane = lax.broadcasted_iota(jnp.int32, (rows, 128), 1)
    for rows_ref, which in ((own_ref, core), (other_ref, 1 - core)):
        total = None
        for distance, weight_ref in zip(distances, weights):
            found = jnp.dot(
                rows_ref[:, block(scal_ref[2 + distance], weight_ref.shape[0])], weight_ref[...],
                preferred_element_type=jnp.float32,
            )
            total = found if total is None else total + found
        for part in range(2):
            low = total[:, part * 256:part * 256 + 128]
            high = total[:, part * 256 + 128:part * 256 + 256]
            zero = jnp.where(lane < HEAD_SIZE, low, pltpu.roll(high, HEAD_SIZE, 1))
            one = jnp.where(lane < HEAD_SIZE, pltpu.roll(low, HEAD_SIZE, 1), high)
            at = slice(part * 128, part * 128 + 128)
            kept_ref[block(which, rows), at] = jnp.where(core == 0, zero, one)
            sent_ref[block(which, rows), at] = jnp.where(core == 0, one, zero)
    marks = (segs_ref[...] + 1).astype(jnp.float32)
    sent_ref[2 * rows:, :] = jnp.broadcast_to(marks, (8, marks.shape[1]))


def parcel_kernel(scal_ref, segs_ref, kept_ref, received_ref, out_ref):
    core = scal_ref[0]
    count = kept_ref.shape[0]
    out_ref[:count, :] = (kept_ref[...] + received_ref[:count, :]).astype(out_ref.dtype)
    own = (segs_ref[...] + 1).astype(jnp.float32)
    other = received_ref[count:count + 1, :]
    first, second = jnp.where(core == 0, own, other), jnp.where(core == 0, other, own)
    row = lax.broadcasted_iota(jnp.int32, (MARK_ROWS, own.shape[1]), 0)
    marks = jnp.where(row == 0, first, jnp.where(row == 1, second, 0.0))
    out_ref[count:, :] = marks.astype(out_ref.dtype)


def copy_kernel(scal_ref, in_ref, out_ref):
    out_ref[...] = in_ref[...]


def window_kernel(scal_ref, four_ref, two_ref, own_ref, crossed_ref, *refs):
    kt_refs, v_refs, lo_ref = refs[:2], refs[2:4], refs[4]
    odd = scal_ref[1]
    length = own_ref.shape[0]
    count = length - MARK_ROWS
    half = count // 2
    second = pl.multiple_of(odd * length, MARK_ROWS)
    fourth = pl.multiple_of((1 - odd) * length, MARK_ROWS)
    places = [(four_ref, 0), (crossed_ref, second), (two_ref, 0), (crossed_ref, fourth), (own_ref, 0)]
    lane = lax.broadcasted_iota(jnp.int32, (count, 128), 1)
    blank = jnp.zeros((HEAD_SIZE, count), jnp.bfloat16)
    marks = []
    for i, (ref, first) in enumerate(places):
        at = slice(i * count, (i + 1) * count)
        keys = ref[pl.ds(first, count), 0:128].astype(jnp.float32).T.astype(jnp.bfloat16)
        values = ref[pl.ds(first, count), 128:256].astype(jnp.float32)
        turned = pltpu.roll(values, HEAD_SIZE, 1)
        for g in range(2):
            head = keys[g * HEAD_SIZE:(g + 1) * HEAD_SIZE]
            kt_refs[g][0, :HEAD_SIZE, at] = head
            kt_refs[g][0, HEAD_SIZE:, at] = blank
            kt_refs[g][1, :HEAD_SIZE, at] = blank
            kt_refs[g][1, HEAD_SIZE:, at] = head
            low, high = (values, turned) if g == 0 else (turned, values)
            v_refs[g][0, at, :] = jnp.where(lane < HEAD_SIZE, low, 0.0).astype(jnp.bfloat16)
            v_refs[g][1, at, :] = jnp.where(lane < HEAD_SIZE, 0.0, high).astype(jnp.bfloat16)
        found = ref[pl.ds(first + count, MARK_ROWS), :].astype(jnp.float32)
        marks += [found[0:1, :], found[1:2, :]]
    across = lax.broadcasted_iota(jnp.int32, (half, half), 1)
    down = lax.broadcasted_iota(jnp.int32, (half, half), 0)
    for part in range(2):
        mine = jnp.sum(jnp.where(across == down, marks[-2 + part], 0.0), axis=1, keepdims=True)
        earlier = jnp.zeros((half, half), jnp.float32)
        for row in marks:
            earlier = earlier + jnp.where(row < mine, 1.0, 0.0)
        earlier = jnp.sum(earlier, axis=1, keepdims=True).astype(jnp.int32)
        place = lax.broadcasted_iota(jnp.int32, (half, 128), 0) + (part * half + 1)
        lo_ref[part * half:(part + 1) * half, :] = jnp.maximum(earlier, place)


def query_kernel(pieces, g, more, scal_ref, own_ref, other_ref, *refs):
    weights, refs = refs[: len(pieces)], refs[len(pieces):]
    core = scal_ref[0]
    rows = own_ref.shape[0]
    outs = refs[-2:]
    for rows_ref, which in ((own_ref, core), (other_ref, 1 - core)):
        at = block(which, rows)
        for i, column in enumerate((core, 1 - core)):
            total = refs[i][at, :] if more else None
            for (distance, first), weight_ref in zip(pieces, weights):
                depth = weight_ref.shape[0]
                start = pl.multiple_of(scal_ref[2 + distance] * rows + first, depth)
                found = jnp.dot(
                    rows_ref[:, pl.ds(start, depth)], weight_ref[:, block(2 * g + column, GROUP_WIDTH)],
                    preferred_element_type=jnp.float32,
                )
                total = found if total is None else total + found
            outs[i][at, :] = total


def attention_kernel(tile, lo_ref, kept_ref, received_ref, kt_ref, v_ref, *refs):
    out_ref, query_ref, score_ref = refs[-3:]
    start = tile * TILE
    mine = slice(start, start + TILE)
    span = LOOKBACK_SPAN + TILE
    lo = lo_ref[mine, :] - start
    lane = lax.broadcasted_iota(jnp.int32, (TILE, 128), 1)
    row = lax.broadcasted_iota(jnp.int32, (TILE, 128), 0)
    blocks = span // TILE
    queries = (kept_ref[mine, :] + received_ref[mine, :]).astype(jnp.bfloat16)
    query_ref[...] = queries * jnp.bfloat16(HEAD_SIZE ** -0.5)

    def scores_of(pair, parity):
        q = query_ref[:, pair * 128:(pair + 1) * 128]
        peak = jnp.full((TILE, 128), MASKED, jnp.float32)
        for i in range(blocks):
            first = start + i * TILE
            found = jnp.dot(q, kt_ref[parity, :, pl.ds(first, TILE)], preferred_element_type=jnp.float32)
            for part in range(TILE // 128):
                at = i * TILE + part * 128
                visible = lane + at >= lo
                if at >= LOOKBACK_SPAN:
                    visible = visible & (lane + (at - LOOKBACK_SPAN) <= row)
                kept = jnp.where(visible, found[:, part * 128:(part + 1) * 128], MASKED)
                peak = jnp.maximum(peak, kept)
                score_ref[parity, :, at:at + 128] = kept
        return jnp.max(peak, axis=1, keepdims=True)

    def mixed_of(parity, peak):
        total = jnp.zeros((TILE, 128), jnp.float32)
        mixed = jnp.zeros((TILE, 128), jnp.float32)
        for i in range(blocks):
            first = start + i * TILE
            weights = jnp.exp(score_ref[parity, :, i * TILE:(i + 1) * TILE] - peak)
            for part in range(TILE // 128):
                total = total + weights[:, part * 128:(part + 1) * 128]
            mixed = mixed + jnp.dot(
                weights.astype(jnp.bfloat16), v_ref[parity, pl.ds(first, TILE), :],
                preferred_element_type=jnp.float32,
            )
        return mixed * (1.0 / jnp.sum(total, axis=1, keepdims=True))

    if tile:
        out_ref[:start, :] = refs[0][:start, :]
    for pair in range(GROUP // 2):
        peaks = [scores_of(pair, parity) for parity in range(2)]
        parts = [mixed_of(parity, peaks[parity]) for parity in range(2)]
        out_ref[mine, pair * 128:(pair + 1) * 128] = (parts[0] + parts[1]).astype(out_ref.dtype)


def attention(tile, arrays, before, waits):
    rows = arrays[1].shape[0]
    arrays = list(arrays) + list(before)
    span = LOOKBACK_SPAN + TILE

    def only(*refs):
        attention_kernel(tile, *refs[:len(arrays)], *refs[len(arrays) + len(waits):])

    whole = pl.BlockSpec(memory_space=pltpu.VMEM)
    return pl.pallas_call(
        only,
        in_specs=[whole] * len(arrays) + [pl.BlockSpec(memory_space=pl.ANY)] * len(waits),
        out_specs=whole,
        out_shape=jax.ShapeDtypeStruct((rows, GROUP_WIDTH), jnp.bfloat16),
        scratch_shapes=[
            pltpu.VMEM((TILE, GROUP_WIDTH), jnp.bfloat16), pltpu.VMEM((2, TILE, span), jnp.float32)
        ],
        compiler_params=pltpu.CompilerParams(vmem_limit_bytes=16 * 1024 * 1024),
        cost_estimate=pl.CostEstimate(flops=1000000, bytes_accessed=100000, transcendentals=0),
    )(*arrays, *waits)


def out_kernel(distances, mode, scal_ref, *refs):
    attended, refs = refs[:4], refs[4:]
    adds, refs = refs[:2], refs[2:]
    count = sum(len(pieces) for _, pieces in distances)
    weights, refs = refs[:count], refs[count:]
    outs = refs[-2:]
    core = scal_ref[0]
    rows = adds[0].shape[0]
    depth = attended[0].shape[1]
    if mode != "alone":
        for i in range(2):
            outs[i][...] = jnp.zeros_like(outs[i])
    for i, which in enumerate((core, 1 - core)):
        taken = 0
        for j, (distance, pieces) in enumerate(distances):
            shard = weights[taken:taken + len(pieces)]
            taken += len(pieces)
            columns = shard[0].shape[1]
            at = block(scal_ref[2 + distance], columns)
            total = adds[i][:, at].astype(jnp.float32)
            for g in range(2):
                ref, first = shard[g * len(shard) // 2], 2 * g if len(shard) == 1 else 0
                for side, column in enumerate((core, 1 - core)):
                    total = total + jnp.dot(
                        attended[2 * g + side][block(which, rows), :],
                        ref[block(first + column, depth), :],
                        preferred_element_type=jnp.float32,
                    )
            if mode == "alone":
                outs[i][:, j * columns:(j + 1) * columns] = total.astype(outs[i].dtype)
            else:
                outs[i][:, at] = total.astype(outs[i].dtype)


def join_kernel(last, scal_ref, own_ref, other_ref, own_last_ref, other_last_ref, out_ref):
    core = scal_ref[0]
    size = 256
    for j in range(own_ref.shape[1] // size):
        at = slice(j * size, (j + 1) * size)
        out_ref[:, block(2 * j + core, size)] = own_ref[:, at]
        out_ref[:, block(2 * j + 1 - core, size)] = other_ref[:, at]
    for i, distance in enumerate(last):
        at = slice(i * size, (i + 1) * size)
        j = scal_ref[2 + distance]
        out_ref[:, block(2 * j + core, size)] = own_last_ref[:, at]
        out_ref[:, block(2 * j + 1 - core, size)] = other_last_ref[:, at]


def body(section_input, segment_ids, query_weight, keyval_weight, out_weight):
    hidden = section_input[0]
    rows, width = hidden.shape
    device = lax.axis_index("fsdp")
    chips = lax.axis_size("fsdp") // 2
    order = ring_order(chips)
    table = []
    for i in range(2 * chips):
        place = order.index(i // 2)
        table.append([i % 2, i // 2 % 2] + [order[(place + d) % chips] for d in range(chips)])
    scalars = lax.dynamic_index_in_dim(jnp.array(table, jnp.int32), device, 0, keepdims=False)

    keyval = Ring(keyval_weight[0])
    keyval.advance()
    keyval.advance()
    keyval.advance()
    keyval.finish(halved=False)

    half = ((rows, width // 2), jnp.bfloat16)
    own_rows, sent_rows = run(functools.partial(split_kernel, True), [half, half], scalars, [hidden])
    other_rows = swap_cores(sent_rows)

    query_shard, = run(
        copy_kernel, [(query_weight.shape[1:], jnp.bfloat16)], scalars, [query_weight[0]],
        waits=keyval.get(3, chips - 3, chips // 2) + [other_rows],
    )
    kept, sent = run(
        functools.partial(keyval_kernel, list(range(chips))),
        [((2 * rows, 256), jnp.float32), ((2 * rows + 8, 256), jnp.float32)],
        scalars, [segment_ids, own_rows, other_rows] + keyval.get(*range(chips)),
    )
    parcel, = run(
        parcel_kernel, [((2 * rows + MARK_ROWS, 256), jnp.bfloat16)], scalars,
        [segment_ids, kept, swap_cores(sent)],
    )
    def query_sums(distances, g, waits, before=()):
        pieces = [(d, first) for d in distances for first, _ in query.found[d]]
        return run(
            functools.partial(query_kernel, pieces, g, bool(before)),
            [((2 * rows, GROUP_WIDTH), jnp.float32)] * 2, scalars,
            [own_rows, other_rows] + query.get(*distances) + list(before), waits=waits,
        )

    near = [0, 1, chips - 1, 2, chips - 2]
    next_far = [3, chips - 3]
    far = [chips // 2]
    query = Ring(query_shard)
    query.advance(parcel)
    back_two = two_chips_on(parcel)
    out_shard = to_next_section(out_weight[0])
    query.advance(back_two, out_shard)
    sums = [query_sums(near, g, [parcel]) for g in range(2)]
    back_four = two_chips_on(after(back_two, sums[0][0], sums[1][0]))
    query.advance(back_four)
    even = device // 2 % 2 == 0
    crossed = swap_chips(jnp.concatenate([jnp.where(even, parcel, back_four), back_two], axis=0))
    query.finish(halved=True)
    out = Ring(after(out_shard, crossed, *query.get(*far)))
    window = 5 * 2 * rows
    *heads, lowest = run(
        window_kernel,
        [((2, 128, window), jnp.bfloat16)] * 2 + [((2, window, 128), jnp.bfloat16)] * 2
        + [((2 * rows, 128), jnp.int32)],
        scalars, [back_four, back_two, parcel, crossed],
    )
    sums = [query_sums(next_far + far, g, [lowest] + out.get(0), sums[g]) for g in range(2)]
    received = [swap_cores(sums[g][1]) for g in range(2)]
    out.advance(lowest, sums[0][0], sums[1][0])
    kept, sent = run(
        functools.partial(split_kernel, False), [half, half], scalars, [to_next_section(hidden)], waits=received[:1]
    )
    adds = [kept, swap_cores(sent)]
    given = [(lowest, sums[g][0], received[g], heads[g], heads[2 + g]) for g in range(2)]
    parts = [attention(0, given[g], [], []) for g in range(2)]
    attended = [attention(1, given[g], [parts[g]], []) for g in range(2)]
    out.advance(attended[0], parts[1])
    arrived = []
    for g in range(2):
        mine = to_next_section(attended[g])
        arrived += [mine, swap_cores(mine)]
    out.advance(*arrived)
    out.finish(halved=True)

    def made(some, mode):
        distances = [(d, [first for first, _ in out.found[d]]) for d in some]
        outs = [((rows, len(some) * out_shard.shape[1]), jnp.bfloat16)] * 2 if mode == "alone" else [half, half]
        return run(
            functools.partial(out_kernel, distances, mode), outs, scalars, arrived + adds + out.get(*some),
            mebibytes=32,
        )

    most = made(near + next_far, "first")
    other_most = swap_cores(most[1])
    last = made(far, "alone")
    joined, = run(
        functools.partial(join_kernel, far), [((rows, width), jnp.bfloat16)], scalars,
        [most[0], other_most, last[0], swap_cores(last[1])],
    )
    return joined[None]


def solution(mesh):
    return jax.shard_map(
        body,
        mesh=mesh,
        in_specs=(
            P("section", "fsdp", None),
            P("section", "fsdp"),
            P("section", "fsdp", None),
            P("section", "fsdp", None),
            P("section", None, "fsdp"),
        ),
        out_specs=P("section", "fsdp", None),
        check_vma=False,
    )
```

```python
import functools

import jax
import jax.numpy as jnp
from jax import lax
from jax.experimental import pallas as pl
from jax.experimental.pallas import tpu as pltpu
from jax.sharding import PartitionSpec as P

QUERY_HEADS = 32
KEY_HEADS = 4
HEAD_SIZE = 64
LOOKBACK_SPAN = 2048
GROUP = QUERY_HEADS // KEY_HEADS
GROUP_WIDTH = GROUP * HEAD_SIZE
TILE = 256
MASKED = -1e30
MARK_ROWS = 16


def ring_order(chips):
    return list(range(0, chips, 2)) + list(range(chips - 1, 0, -2))


def swap_cores(value):
    count = lax.axis_size("fsdp")
    return lax.ppermute(value, "fsdp", [(i, i ^ 1) for i in range(count)])


def swap_chips(value):
    count = lax.axis_size("fsdp")
    return lax.ppermute(value, "fsdp", [(i, i ^ 2) for i in range(count)])


def two_chips_on(value):
    count = lax.axis_size("fsdp")
    return lax.ppermute(value, "fsdp", [(i, i + 4) for i in range(count - 4)])


def to_next_section(value):
    count = lax.axis_size("section")
    return lax.ppermute(value, "section", [(i, (i + 1) % count) for i in range(count)])


def along_ring(value, step):
    chips = lax.axis_size("fsdp") // 2
    order = ring_order(chips)
    pairs = []
    for place in range(chips):
        target = order[(place + step) % chips]
        pairs += [(2 * order[place] + core, 2 * target + core) for core in range(2)]
    return lax.ppermute(value, "fsdp", pairs)


def run(kernel, outs, scalars, arrays, waits=(), aliases=None, scratch=()):
    whole = pl.BlockSpec(memory_space=pltpu.VMEM)
    taken = 1 + len(arrays)

    def only(*refs):
        kernel(*refs[:taken], *refs[taken + len(waits):])

    return pl.pallas_call(
        only,
        in_specs=[pl.BlockSpec(memory_space=pltpu.SMEM)] + [whole] * len(arrays)
        + [pl.BlockSpec(memory_space=pl.ANY)] * len(waits),
        out_specs=[whole] * len(outs),
        out_shape=[jax.ShapeDtypeStruct(shape, dtype) for shape, dtype in outs],
        scratch_shapes=list(scratch),
        input_output_aliases=aliases or {},
        compiler_params=pltpu.CompilerParams(vmem_limit_bytes=8 * 1024 * 1024),
        cost_estimate=pl.CostEstimate(flops=1000000, bytes_accessed=100000, transcendentals=0),
    )(scalars, *arrays, *waits)


def tied_kernel(*refs):
    pass


def after(value, *others):
    anywhere = pl.BlockSpec(memory_space=pl.ANY)
    return pl.pallas_call(
        tied_kernel,
        in_specs=[anywhere] * (1 + len(others)),
        out_specs=anywhere,
        out_shape=jax.ShapeDtypeStruct(value.shape, value.dtype),
        input_output_aliases={0: 0},
        cost_estimate=pl.CostEstimate(flops=0, bytes_accessed=0, transcendentals=0),
    )(value, *others)


class Ring:
    def __init__(self, shard):
        self.chips, self.step = lax.axis_size("fsdp") // 2, 0
        self.moving, self.found = {1: shard, -1: shard}, {0: [(0, shard)]}

    def advance(self, *others):
        self.step += 1
        for way in (1, -1):
            value = along_ring(self.moving[way], way)
            self.moving[way] = after(value, *others) if others else value
            self.found[-way * self.step % self.chips] = [(0, self.moving[way])]

    def finish(self, halved):
        if halved:
            half = self.moving[1].shape[0] // 2
            last = [(0, along_ring(self.moving[1][:half], 1)), (half, along_ring(self.moving[-1][half:], -1))]
        else:
            last = [(0, along_ring(self.moving[1], 1))]
        self.found[self.chips // 2] = last

    def get(self, *distances):
        return [piece for d in distances for _, piece in self.found[d]]


def block(index, size):
    return pl.ds(pl.multiple_of(index * size, size), size)


def split_kernel(norm, scal_ref, rows_ref, kept_ref, sent_ref):
    core = scal_ref[0]
    count, width = rows_ref.shape
    size, some = 256, 64
    for first in range(0, count, some):
        at = slice(first, first + some)
        if norm:
            values = rows_ref[at, :].astype(jnp.float32)
            scale = lax.rsqrt(jnp.mean(values * values, axis=1, keepdims=True) + 1e-05)
        for j in range(width // (2 * size)):
            for out_ref, which in ((kept_ref, core), (sent_ref, 1 - core)):
                part = rows_ref[at, block(2 * j + which, size)]
                if norm:
                    part = (part.astype(jnp.float32) * scale).astype(jnp.bfloat16)
                out_ref[at, j * size:(j + 1) * size] = part


def keyval_kernel(distances, scal_ref, segs_ref, own_ref, other_ref, *refs):
    weights, (kept_ref, sent_ref) = refs[: len(distances)], refs[len(distances):]
    core = scal_ref[0]
    rows = own_ref.shape[0]
    lane = lax.broadcasted_iota(jnp.int32, (rows, 128), 1)
    for rows_ref, which in ((own_ref, core), (other_ref, 1 - core)):
        total = None
        for distance, weight_ref in zip(distances, weights):
            found = jnp.dot(
                rows_ref[:, block(scal_ref[2 + distance], weight_ref.shape[0])], weight_ref[...],
                preferred_element_type=jnp.float32,
            )
            total = found if total is None else total + found
        for part in range(2):
            low = total[:, part * 256:part * 256 + 128]
            high = total[:, part * 256 + 128:part * 256 + 256]
            zero = jnp.where(lane < HEAD_SIZE, low, pltpu.roll(high, HEAD_SIZE, 1))
            one = jnp.where(lane < HEAD_SIZE, pltpu.roll(low, HEAD_SIZE, 1), high)
            at = slice(part * 128, part * 128 + 128)
            kept_ref[block(which, rows), at] = jnp.where(core == 0, zero, one)
            sent_ref[block(which, rows), at] = jnp.where(core == 0, one, zero)
    marks = (segs_ref[...] + 1).astype(jnp.float32)
    sent_ref[2 * rows:, :] = jnp.broadcast_to(marks, (8, marks.shape[1]))


def parcel_kernel(scal_ref, segs_ref, kept_ref, received_ref, out_ref):
    core = scal_ref[0]
    count = kept_ref.shape[0]
    out_ref[:count, :] = (kept_ref[...] + received_ref[:count, :]).astype(out_ref.dtype)
    own = (segs_ref[...] + 1).astype(jnp.float32)
    other = received_ref[count:count + 1, :]
    first, second = jnp.where(core == 0, own, other), jnp.where(core == 0, other, own)
    row = lax.broadcasted_iota(jnp.int32, (MARK_ROWS, own.shape[1]), 0)
    marks = jnp.where(row == 0, first, jnp.where(row == 1, second, 0.0))
    out_ref[count:, :] = marks.astype(out_ref.dtype)


def copy_kernel(scal_ref, in_ref, out_ref):
    out_ref[...] = in_ref[...]


def window_kernel(scal_ref, four_ref, two_ref, own_ref, crossed_ref, *refs):
    kt_refs, v_refs, lo_ref = refs[:2], refs[2:4], refs[4]
    odd = scal_ref[1]
    length = own_ref.shape[0]
    count = length - MARK_ROWS
    half = count // 2
    second = pl.multiple_of(odd * length, MARK_ROWS)
    fourth = pl.multiple_of((1 - odd) * length, MARK_ROWS)
    places = [(four_ref, 0), (crossed_ref, second), (two_ref, 0), (crossed_ref, fourth), (own_ref, 0)]
    lane = lax.broadcasted_iota(jnp.int32, (count, 128), 1)
    blank = jnp.zeros((HEAD_SIZE, count), jnp.bfloat16)
    marks = []
    for i, (ref, first) in enumerate(places):
        at = slice(i * count, (i + 1) * count)
        keys = ref[pl.ds(first, count), 0:128].astype(jnp.float32).T.astype(jnp.bfloat16)
        values = ref[pl.ds(first, count), 128:256].astype(jnp.float32)
        turned = pltpu.roll(values, HEAD_SIZE, 1)
        for g in range(2):
            head = keys[g * HEAD_SIZE:(g + 1) * HEAD_SIZE]
            kt_refs[g][0, :HEAD_SIZE, at] = head
            kt_refs[g][0, HEAD_SIZE:, at] = blank
            kt_refs[g][1, :HEAD_SIZE, at] = blank
            kt_refs[g][1, HEAD_SIZE:, at] = head
            low, high = (values, turned) if g == 0 else (turned, values)
            v_refs[g][0, at, :] = jnp.where(lane < HEAD_SIZE, low, 0.0).astype(jnp.bfloat16)
            v_refs[g][1, at, :] = jnp.where(lane < HEAD_SIZE, 0.0, high).astype(jnp.bfloat16)
        found = ref[pl.ds(first + count, MARK_ROWS), :].astype(jnp.float32)
        marks += [found[0:1, :], found[1:2, :]]
    across = lax.broadcasted_iota(jnp.int32, (half, half), 1)
    down = lax.broadcasted_iota(jnp.int32, (half, half), 0)
    for part in range(2):
        mine = jnp.sum(jnp.where(across == down, marks[-2 + part], 0.0), axis=1, keepdims=True)
        earlier = jnp.zeros((half, half), jnp.float32)
        for row in marks:
            earlier = earlier + jnp.where(row < mine, 1.0, 0.0)
        earlier = jnp.sum(earlier, axis=1, keepdims=True).astype(jnp.int32)
        place = lax.broadcasted_iota(jnp.int32, (half, 128), 0) + (part * half + 1)
        lo_ref[part * half:(part + 1) * half, :] = jnp.maximum(earlier, place)


def query_kernel(pieces, g, more, scal_ref, own_ref, other_ref, *refs):
    weights, refs = refs[: len(pieces)], refs[len(pieces):]
    core = scal_ref[0]
    rows = own_ref.shape[0]
    outs = refs[-2:]
    for rows_ref, which in ((own_ref, core), (other_ref, 1 - core)):
        at = block(which, rows)
        for i, column in enumerate((core, 1 - core)):
            total = refs[i][at, :] if more else None
            for (distance, first), weight_ref in zip(pieces, weights):
                depth = weight_ref.shape[0]
                start = pl.multiple_of(scal_ref[2 + distance] * rows + first, depth)
                found = jnp.dot(
                    rows_ref[:, pl.ds(start, depth)], weight_ref[:, block(2 * g + column, GROUP_WIDTH)],
                    preferred_element_type=jnp.float32,
                )
                total = found if total is None else total + found
            outs[i][at, :] = total


def attention_kernel(tile, lo_ref, kept_ref, received_ref, kt_ref, v_ref, *refs):
    out_ref, query_ref, score_ref = refs[-3:]
    start = tile * TILE
    mine = slice(start, start + TILE)
    span = LOOKBACK_SPAN + TILE
    lo = lo_ref[mine, :] - start
    lane = lax.broadcasted_iota(jnp.int32, (TILE, 128), 1)
    row = lax.broadcasted_iota(jnp.int32, (TILE, 128), 0)
    blocks = span // TILE
    queries = (kept_ref[mine, :] + received_ref[mine, :]).astype(jnp.bfloat16)
    query_ref[...] = queries * jnp.bfloat16(HEAD_SIZE ** -0.5)

    def scores_of(pair, parity):
        q = query_ref[:, pair * 128:(pair + 1) * 128]
        peak = jnp.full((TILE, 128), MASKED, jnp.float32)
        for i in range(blocks):
            first = start + i * TILE
            found = jnp.dot(q, kt_ref[parity, :, pl.ds(first, TILE)], preferred_element_type=jnp.float32)
            for part in range(TILE // 128):
                at = i * TILE + part * 128
                visible = lane + at >= lo
                if at >= LOOKBACK_SPAN:
                    visible = visible & (lane + (at - LOOKBACK_SPAN) <= row)
                kept = jnp.where(visible, found[:, part * 128:(part + 1) * 128], MASKED)
                peak = jnp.maximum(peak, kept)
                score_ref[parity, :, at:at + 128] = kept
        return jnp.max(peak, axis=1, keepdims=True)

    def mixed_of(parity, peak):
        total = jnp.zeros((TILE, 128), jnp.float32)
        mixed = jnp.zeros((TILE, 128), jnp.float32)
        for i in range(blocks):
            first = start + i * TILE
            weights = jnp.exp(score_ref[parity, :, i * TILE:(i + 1) * TILE] - peak)
            for part in range(TILE // 128):
                total = total + weights[:, part * 128:(part + 1) * 128]
            mixed = mixed + jnp.dot(
                weights.astype(jnp.bfloat16), v_ref[parity, pl.ds(first, TILE), :],
                preferred_element_type=jnp.float32,
            )
        return mixed * (1.0 / jnp.sum(total, axis=1, keepdims=True))

    if tile:
        out_ref[:start, :] = refs[0][:start, :]
    for pair in range(GROUP // 2):
        peaks = [scores_of(pair, parity) for parity in range(2)]
        parts = [mixed_of(parity, peaks[parity]) for parity in range(2)]
        out_ref[mine, pair * 128:(pair + 1) * 128] = (parts[0] + parts[1]).astype(out_ref.dtype)


def attention(tile, arrays, before, waits):
    rows = arrays[1].shape[0]
    arrays = list(arrays) + list(before)
    span = LOOKBACK_SPAN + TILE

    def only(*refs):
        attention_kernel(tile, *refs[:len(arrays)], *refs[len(arrays) + len(waits):])

    whole = pl.BlockSpec(memory_space=pltpu.VMEM)
    return pl.pallas_call(
        only,
        in_specs=[whole] * len(arrays) + [pl.BlockSpec(memory_space=pl.ANY)] * len(waits),
        out_specs=whole,
        out_shape=jax.ShapeDtypeStruct((rows, GROUP_WIDTH), jnp.bfloat16),
        scratch_shapes=[
            pltpu.VMEM((TILE, GROUP_WIDTH), jnp.bfloat16), pltpu.VMEM((2, TILE, span), jnp.float32)
        ],
        compiler_params=pltpu.CompilerParams(vmem_limit_bytes=16 * 1024 * 1024),
        cost_estimate=pl.CostEstimate(flops=1000000, bytes_accessed=100000, transcendentals=0),
    )(*arrays, *waits)


def out_kernel(distances, mode, scal_ref, *refs):
    attended, refs = refs[:4], refs[4:]
    adds, refs = refs[:2], refs[2:]
    count = sum(len(pieces) for _, pieces in distances)
    weights, refs = refs[:count], refs[count:]
    outs = refs[-2:]
    core = scal_ref[0]
    rows = adds[0].shape[0]
    depth = attended[0].shape[1]
    if mode != "alone":
        for i in range(2):
            outs[i][...] = jnp.zeros_like(outs[i])
    for i, which in enumerate((core, 1 - core)):
        taken = 0
        for distance, pieces in distances:
            shard = weights[taken:taken + len(pieces)]
            taken += len(pieces)
            columns = shard[0].shape[1]
            at = block(scal_ref[2 + distance], columns)
            total = adds[i][:, at].astype(jnp.float32)
            for g in range(2):
                ref, first = shard[g * len(shard) // 2], 2 * g if len(shard) == 1 else 0
                for side, column in enumerate((core, 1 - core)):
                    total = total + jnp.dot(
                        attended[2 * g + side][block(which, rows), :],
                        ref[block(first + column, depth), :],
                        preferred_element_type=jnp.float32,
                    )
            if mode == "alone":
                outs[i][...] = total.astype(outs[i].dtype)
            else:
                outs[i][:, at] = total.astype(outs[i].dtype)


def join_kernel(last, scal_ref, own_ref, other_ref, own_last_ref, other_last_ref, out_ref):
    core = scal_ref[0]
    size = own_last_ref.shape[1]
    for j in range(own_ref.shape[1] // size):
        at = slice(j * size, (j + 1) * size)
        out_ref[:, block(2 * j + core, size)] = own_ref[:, at]
        out_ref[:, block(2 * j + 1 - core, size)] = other_ref[:, at]
    j = scal_ref[2 + last]
    out_ref[:, block(2 * j + core, size)] = own_last_ref[...]
    out_ref[:, block(2 * j + 1 - core, size)] = other_last_ref[...]


def body(section_input, segment_ids, query_weight, keyval_weight, out_weight):
    hidden = section_input[0]
    rows, width = hidden.shape
    device = lax.axis_index("fsdp")
    chips = lax.axis_size("fsdp") // 2
    order = ring_order(chips)
    table = []
    for i in range(2 * chips):
        place = order.index(i // 2)
        table.append([i % 2, i // 2 % 2] + [order[(place + d) % chips] for d in range(chips)])
    scalars = lax.dynamic_index_in_dim(jnp.array(table, jnp.int32), device, 0, keepdims=False)

    keyval = Ring(keyval_weight[0])
    keyval.advance()
    keyval.advance()
    keyval.advance()
    keyval.finish(halved=False)

    half = ((rows, width // 2), jnp.bfloat16)
    own_rows, sent_rows = run(functools.partial(split_kernel, True), [half, half], scalars, [hidden])
    other_rows = swap_cores(sent_rows)

    query_shard, = run(
        copy_kernel, [(query_weight.shape[1:], jnp.bfloat16)], scalars, [query_weight[0]],
        waits=keyval.get(3, chips - 3, chips // 2) + [other_rows],
    )
    kept, sent = run(
        functools.partial(keyval_kernel, list(range(chips))),
        [((2 * rows, 256), jnp.float32), ((2 * rows + 8, 256), jnp.float32)],
        scalars, [segment_ids, own_rows, other_rows] + keyval.get(*range(chips)),
    )
    parcel, = run(
        parcel_kernel, [((2 * rows + MARK_ROWS, 256), jnp.bfloat16)], scalars,
        [segment_ids, kept, swap_cores(sent)],
    )
    def query_sums(distances, g, waits, before=()):
        pieces = [(d, first) for d in distances for first, _ in query.found[d]]
        return run(
            functools.partial(query_kernel, pieces, g, bool(before)),
            [((2 * rows, GROUP_WIDTH), jnp.float32)] * 2, scalars,
            [own_rows, other_rows] + query.get(*distances) + list(before), waits=waits,
        )

    near = [0, 1, chips - 1, 2, chips - 2]
    next_far = [3, chips - 3]
    far = [chips // 2]
    query = Ring(query_shard)
    query.advance(parcel)
    back_two = two_chips_on(parcel)
    out_shard = to_next_section(out_weight[0])
    query.advance(back_two, out_shard)
    sums = [query_sums(near, g, [parcel]) for g in range(2)]
    back_four = two_chips_on(after(back_two, sums[0][0], sums[1][0]))
    query.advance(back_four)
    even = device // 2 % 2 == 0
    crossed = swap_chips(jnp.concatenate([jnp.where(even, parcel, back_four), back_two], axis=0))
    query.finish(halved=True)
    out = Ring(after(out_shard, crossed, *query.get(*far)))
    window = 5 * 2 * rows
    *heads, lowest = run(
        window_kernel,
        [((2, 128, window), jnp.bfloat16)] * 2 + [((2, window, 128), jnp.bfloat16)] * 2
        + [((2 * rows, 128), jnp.int32)],
        scalars, [back_four, back_two, parcel, crossed],
    )
    sums = [query_sums(next_far + far, g, [lowest] + out.get(0), sums[g]) for g in range(2)]
    given = [(lowest, sums[g][0], swap_cores(sums[g][1]), heads[g], heads[2 + g]) for g in range(2)]
    out.advance()
    attended = [attention(0, given[0], [], [])]
    attended[0] = attention(1, given[0], attended[:1], out.get(1, chips - 1))
    out.advance()
    attended.append(attention(0, given[1], [], attended[:1] + out.get(2, chips - 2)))
    attended[1] = attention(1, given[1], attended[1:], [])
    out.advance()
    out.finish(halved=True)
    kept, sent = run(
        functools.partial(split_kernel, False), [half, half], scalars, [to_next_section(hidden)], waits=attended[:1]
    )
    adds = [kept, swap_cores(sent)]
    arrived = []
    for g in range(2):
        mine = to_next_section(attended[g])
        arrived += [mine, swap_cores(mine)]

    def made(some, mode):
        distances = [(d, [first for first, _ in out.found[d]]) for d in some]
        outs = [((rows, out_shard.shape[1]), jnp.bfloat16)] * 2 if mode == "alone" else [half, half]
        return run(
            functools.partial(out_kernel, distances, mode), outs, scalars, arrived + adds + out.get(*some)
        )

    most = made(near + next_far, "first")
    other_most = swap_cores(most[1])
    last = made(far, "alone")
    joined, = run(
        functools.partial(join_kernel, chips // 2), [((rows, width), jnp.bfloat16)], scalars,
        [most[0], other_most, last[0], swap_cores(last[1])],
    )
    return joined[None]


def solution(mesh):
    return jax.shard_map(
        body,
        mesh=mesh,
        in_specs=(
            P("section", "fsdp", None),
            P("section", "fsdp"),
            P("section", "fsdp", None),
            P("section", "fsdp", None),
            P("section", None, "fsdp"),
        ),
        out_specs=P("section", "fsdp", None),
        check_vma=False,
    )
```

```python
import functools

import jax
import jax.numpy as jnp
from jax import lax
from jax.experimental import pallas as pl
from jax.experimental.pallas import tpu as pltpu
from jax.sharding import PartitionSpec as P

QUERY_HEADS = 32
KEY_HEADS = 4
HEAD_SIZE = 64
LOOKBACK_SPAN = 2048
GROUP = QUERY_HEADS // KEY_HEADS
GROUP_WIDTH = GROUP * HEAD_SIZE
TILE = 256
MASKED = -1e30
MARK_ROWS = 16


def ring_order(chips):
    return list(range(0, chips, 2)) + list(range(chips - 1, 0, -2))


def swap_cores(value):
    count = lax.axis_size("fsdp")
    return lax.ppermute(value, "fsdp", [(i, i ^ 1) for i in range(count)])


def swap_chips(value):
    count = lax.axis_size("fsdp")
    return lax.ppermute(value, "fsdp", [(i, i ^ 2) for i in range(count)])


def two_chips_on(value):
    count = lax.axis_size("fsdp")
    return lax.ppermute(value, "fsdp", [(i, i + 4) for i in range(count - 4)])


def to_next_section(value):
    count = lax.axis_size("section")
    return lax.ppermute(value, "section", [(i, (i + 1) % count) for i in range(count)])


def along_ring(value, step):
    chips = lax.axis_size("fsdp") // 2
    order = ring_order(chips)
    pairs = []
    for place in range(chips):
        target = order[(place + step) % chips]
        pairs += [(2 * order[place] + core, 2 * target + core) for core in range(2)]
    return lax.ppermute(value, "fsdp", pairs)


def run(kernel, outs, scalars, arrays, waits=(), aliases=None, scratch=()):
    whole = pl.BlockSpec(memory_space=pltpu.VMEM)
    taken = 1 + len(arrays)

    def only(*refs):
        kernel(*refs[:taken], *refs[taken + len(waits):])

    return pl.pallas_call(
        only,
        in_specs=[pl.BlockSpec(memory_space=pltpu.SMEM)] + [whole] * len(arrays)
        + [pl.BlockSpec(memory_space=pl.ANY)] * len(waits),
        out_specs=[whole] * len(outs),
        out_shape=[jax.ShapeDtypeStruct(shape, dtype) for shape, dtype in outs],
        scratch_shapes=list(scratch),
        input_output_aliases=aliases or {},
        compiler_params=pltpu.CompilerParams(vmem_limit_bytes=8 * 1024 * 1024),
        cost_estimate=pl.CostEstimate(flops=1000000, bytes_accessed=100000, transcendentals=0),
    )(scalars, *arrays, *waits)


def tied_kernel(*refs):
    pass


def after(value, *others):
    anywhere = pl.BlockSpec(memory_space=pl.ANY)
    return pl.pallas_call(
        tied_kernel,
        in_specs=[anywhere] * (1 + len(others)),
        out_specs=anywhere,
        out_shape=jax.ShapeDtypeStruct(value.shape, value.dtype),
        input_output_aliases={0: 0},
        cost_estimate=pl.CostEstimate(flops=0, bytes_accessed=0, transcendentals=0),
    )(value, *others)


class Ring:
    def __init__(self, shard):
        self.chips, self.step = lax.axis_size("fsdp") // 2, 0
        self.moving, self.found = {1: shard, -1: shard}, {0: [(0, shard)]}

    def advance(self, *others):
        self.step += 1
        for way in (1, -1):
            value = along_ring(self.moving[way], way)
            self.moving[way] = after(value, *others) if others else value
            self.found[-way * self.step % self.chips] = [(0, self.moving[way])]

    def finish(self, halved):
        if halved:
            half = self.moving[1].shape[0] // 2
            last = [(0, along_ring(self.moving[1][:half], 1)), (half, along_ring(self.moving[-1][half:], -1))]
        else:
            last = [(0, along_ring(self.moving[1], 1))]
        self.found[self.chips // 2] = last

    def get(self, *distances):
        return [piece for d in distances for _, piece in self.found[d]]


def block(index, size):
    return pl.ds(pl.multiple_of(index * size, size), size)


def split_kernel(norm, scal_ref, rows_ref, kept_ref, sent_ref):
    core = scal_ref[0]
    count, width = rows_ref.shape
    size, some = 256, 64
    for first in range(0, count, some):
        at = slice(first, first + some)
        if norm:
            values = rows_ref[at, :].astype(jnp.float32)
            scale = lax.rsqrt(jnp.mean(values * values, axis=1, keepdims=True) + 1e-05)
        for j in range(width // (2 * size)):
            for out_ref, which in ((kept_ref, core), (sent_ref, 1 - core)):
                part = rows_ref[at, block(2 * j + which, size)]
                if norm:
                    part = (part.astype(jnp.float32) * scale).astype(jnp.bfloat16)
                out_ref[at, j * size:(j + 1) * size] = part


def keyval_kernel(distances, scal_ref, segs_ref, own_ref, other_ref, *refs):
    weights, (kept_ref, sent_ref) = refs[: len(distances)], refs[len(distances):]
    core = scal_ref[0]
    rows = own_ref.shape[0]
    lane = lax.broadcasted_iota(jnp.int32, (rows, 128), 1)
    for rows_ref, which in ((own_ref, core), (other_ref, 1 - core)):
        total = None
        for distance, weight_ref in zip(distances, weights):
            found = jnp.dot(
                rows_ref[:, block(scal_ref[2 + distance], weight_ref.shape[0])], weight_ref[...],
                preferred_element_type=jnp.float32,
            )
            total = found if total is None else total + found
        for part in range(2):
            low = total[:, part * 256:part * 256 + 128]
            high = total[:, part * 256 + 128:part * 256 + 256]
            zero = jnp.where(lane < HEAD_SIZE, low, pltpu.roll(high, HEAD_SIZE, 1))
            one = jnp.where(lane < HEAD_SIZE, pltpu.roll(low, HEAD_SIZE, 1), high)
            at = slice(part * 128, part * 128 + 128)
            kept_ref[block(which, rows), at] = jnp.where(core == 0, zero, one)
            sent_ref[block(which, rows), at] = jnp.where(core == 0, one, zero)
    marks = (segs_ref[...] + 1).astype(jnp.float32)
    sent_ref[2 * rows:, :] = jnp.broadcast_to(marks, (8, marks.shape[1]))


def parcel_kernel(scal_ref, segs_ref, kept_ref, received_ref, out_ref):
    core = scal_ref[0]
    count = kept_ref.shape[0]
    out_ref[:count, :] = (kept_ref[...] + received_ref[:count, :]).astype(out_ref.dtype)
    own = (segs_ref[...] + 1).astype(jnp.float32)
    other = received_ref[count:count + 1, :]
    first, second = jnp.where(core == 0, own, other), jnp.where(core == 0, other, own)
    row = lax.broadcasted_iota(jnp.int32, (MARK_ROWS, own.shape[1]), 0)
    marks = jnp.where(row == 0, first, jnp.where(row == 1, second, 0.0))
    out_ref[count:, :] = marks.astype(out_ref.dtype)


def copy_kernel(scal_ref, in_ref, out_ref):
    out_ref[...] = in_ref[...]


def window_kernel(scal_ref, four_ref, two_ref, own_ref, crossed_ref, *refs):
    kt_refs, v_refs, lo_ref = refs[:2], refs[2:4], refs[4]
    odd = scal_ref[1]
    length = own_ref.shape[0]
    count = length - MARK_ROWS
    half = count // 2
    second = pl.multiple_of(odd * length, MARK_ROWS)
    fourth = pl.multiple_of((1 - odd) * length, MARK_ROWS)
    places = [(four_ref, 0), (crossed_ref, second), (two_ref, 0), (crossed_ref, fourth), (own_ref, 0)]
    lane = lax.broadcasted_iota(jnp.int32, (count, 128), 1)
    blank = jnp.zeros((HEAD_SIZE, count), jnp.bfloat16)
    marks = []
    for i, (ref, first) in enumerate(places):
        at = slice(i * count, (i + 1) * count)
        keys = ref[pl.ds(first, count), 0:128].astype(jnp.float32).T.astype(jnp.bfloat16)
        values = ref[pl.ds(first, count), 128:256].astype(jnp.float32)
        turned = pltpu.roll(values, HEAD_SIZE, 1)
        for g in range(2):
            head = keys[g * HEAD_SIZE:(g + 1) * HEAD_SIZE]
            kt_refs[g][0, :HEAD_SIZE, at] = head
            kt_refs[g][0, HEAD_SIZE:, at] = blank
            kt_refs[g][1, :HEAD_SIZE, at] = blank
            kt_refs[g][1, HEAD_SIZE:, at] = head
            low, high = (values, turned) if g == 0 else (turned, values)
            v_refs[g][0, at, :] = jnp.where(lane < HEAD_SIZE, low, 0.0).astype(jnp.bfloat16)
            v_refs[g][1, at, :] = jnp.where(lane < HEAD_SIZE, 0.0, high).astype(jnp.bfloat16)
        found = ref[pl.ds(first + count, MARK_ROWS), :].astype(jnp.float32)
        marks += [found[0:1, :], found[1:2, :]]
    across = lax.broadcasted_iota(jnp.int32, (half, half), 1)
    down = lax.broadcasted_iota(jnp.int32, (half, half), 0)
    for part in range(2):
        mine = jnp.sum(jnp.where(across == down, marks[-2 + part], 0.0), axis=1, keepdims=True)
        earlier = jnp.zeros((half, half), jnp.float32)
        for row in marks:
            earlier = earlier + jnp.where(row < mine, 1.0, 0.0)
        earlier = jnp.sum(earlier, axis=1, keepdims=True).astype(jnp.int32)
        place = lax.broadcasted_iota(jnp.int32, (half, 128), 0) + (part * half + 1)
        lo_ref[part * half:(part + 1) * half, :] = jnp.maximum(earlier, place)


def query_kernel(pieces, g, more, scal_ref, own_ref, other_ref, *refs):
    weights, refs = refs[: len(pieces)], refs[len(pieces):]
    core = scal_ref[0]
    rows = own_ref.shape[0]
    outs = refs[-2:]
    for rows_ref, which in ((own_ref, core), (other_ref, 1 - core)):
        at = block(which, rows)
        for i, column in enumerate((core, 1 - core)):
            total = refs[i][at, :] if more else None
            for (distance, first), weight_ref in zip(pieces, weights):
                depth = weight_ref.shape[0]
                start = pl.multiple_of(scal_ref[2 + distance] * rows + first, depth)
                found = jnp.dot(
                    rows_ref[:, pl.ds(start, depth)], weight_ref[:, block(2 * g + column, GROUP_WIDTH)],
                    preferred_element_type=jnp.float32,
                )
                total = found if total is None else total + found
            outs[i][at, :] = total


def attention_kernel(tile, lo_ref, kept_ref, received_ref, kt_ref, v_ref, *refs):
    out_ref, query_ref, score_ref = refs[-3:]
    start = tile * TILE
    mine = slice(start, start + TILE)
    span = LOOKBACK_SPAN + TILE
    lo = lo_ref[mine, :] - start
    lane = lax.broadcasted_iota(jnp.int32, (TILE, 128), 1)
    row = lax.broadcasted_iota(jnp.int32, (TILE, 128), 0)
    blocks = span // TILE
    queries = (kept_ref[mine, :] + received_ref[mine, :]).astype(jnp.bfloat16)
    query_ref[...] = queries * jnp.bfloat16(HEAD_SIZE ** -0.5)

    def scores_of(pair, parity):
        q = query_ref[:, pair * 128:(pair + 1) * 128]
        peak = jnp.full((TILE, 128), MASKED, jnp.float32)
        for i in range(blocks):
            first = start + i * TILE
            found = jnp.dot(q, kt_ref[parity, :, pl.ds(first, TILE)], preferred_element_type=jnp.float32)
            for part in range(TILE // 128):
                at = i * TILE + part * 128
                visible = lane + at >= lo
                if at >= LOOKBACK_SPAN:
                    visible = visible & (lane + (at - LOOKBACK_SPAN) <= row)
                kept = jnp.where(visible, found[:, part * 128:(part + 1) * 128], MASKED)
                peak = jnp.maximum(peak, kept)
                score_ref[parity, :, at:at + 128] = kept
        return jnp.max(peak, axis=1, keepdims=True)

    def mixed_of(parity, peak):
        total = jnp.zeros((TILE, 128), jnp.float32)
        mixed = jnp.zeros((TILE, 128), jnp.float32)
        for i in range(blocks):
            first = start + i * TILE
            weights = jnp.exp(score_ref[parity, :, i * TILE:(i + 1) * TILE] - peak)
            for part in range(TILE // 128):
                total = total + weights[:, part * 128:(part + 1) * 128]
            mixed = mixed + jnp.dot(
                weights.astype(jnp.bfloat16), v_ref[parity, pl.ds(first, TILE), :],
                preferred_element_type=jnp.float32,
            )
        return mixed * (1.0 / jnp.sum(total, axis=1, keepdims=True))

    if tile:
        out_ref[:start, :] = refs[0][:start, :]
    for pair in range(GROUP // 2):
        peaks = [scores_of(pair, parity) for parity in range(2)]
        parts = [mixed_of(parity, peaks[parity]) for parity in range(2)]
        out_ref[mine, pair * 128:(pair + 1) * 128] = (parts[0] + parts[1]).astype(out_ref.dtype)


def attention(tile, arrays, before, waits):
    rows = arrays[1].shape[0]
    arrays = list(arrays) + list(before)
    span = LOOKBACK_SPAN + TILE

    def only(*refs):
        attention_kernel(tile, *refs[:len(arrays)], *refs[len(arrays) + len(waits):])

    whole = pl.BlockSpec(memory_space=pltpu.VMEM)
    return pl.pallas_call(
        only,
        in_specs=[whole] * len(arrays) + [pl.BlockSpec(memory_space=pl.ANY)] * len(waits),
        out_specs=whole,
        out_shape=jax.ShapeDtypeStruct((rows, GROUP_WIDTH), jnp.bfloat16),
        scratch_shapes=[
            pltpu.VMEM((TILE, GROUP_WIDTH), jnp.bfloat16), pltpu.VMEM((2, TILE, span), jnp.float32)
        ],
        compiler_params=pltpu.CompilerParams(vmem_limit_bytes=16 * 1024 * 1024),
        cost_estimate=pl.CostEstimate(flops=1000000, bytes_accessed=100000, transcendentals=0),
    )(*arrays, *waits)


def out_kernel(distances, mode, scal_ref, *refs):
    attended, refs = refs[:4], refs[4:]
    adds, refs = refs[:2], refs[2:]
    count = sum(len(pieces) for _, pieces in distances)
    weights, refs = refs[:count], refs[count:]
    outs = refs[-2:]
    core = scal_ref[0]
    rows = adds[0].shape[0]
    depth = attended[0].shape[1]
    if mode != "alone":
        for i in range(2):
            outs[i][...] = jnp.zeros_like(outs[i])
    for i, which in enumerate((core, 1 - core)):
        taken = 0
        for distance, pieces in distances:
            shard = weights[taken:taken + len(pieces)]
            taken += len(pieces)
            columns = shard[0].shape[1]
            at = block(scal_ref[2 + distance], columns)
            total = adds[i][:, at].astype(jnp.float32)
            for g in range(2):
                ref, first = shard[g * len(shard) // 2], 2 * g if len(shard) == 1 else 0
                for side, column in enumerate((core, 1 - core)):
                    total = total + jnp.dot(
                        attended[2 * g + side][block(which, rows), :],
                        ref[block(first + column, depth), :],
                        preferred_element_type=jnp.float32,
                    )
            if mode == "alone":
                outs[i][...] = total.astype(outs[i].dtype)
            else:
                outs[i][:, at] = total.astype(outs[i].dtype)


def join_kernel(last, scal_ref, own_ref, other_ref, own_last_ref, other_last_ref, out_ref):
    core = scal_ref[0]
    size = own_last_ref.shape[1]
    for j in range(own_ref.shape[1] // size):
        at = slice(j * size, (j + 1) * size)
        out_ref[:, block(2 * j + core, size)] = own_ref[:, at]
        out_ref[:, block(2 * j + 1 - core, size)] = other_ref[:, at]
    j = scal_ref[2 + last]
    out_ref[:, block(2 * j + core, size)] = own_last_ref[...]
    out_ref[:, block(2 * j + 1 - core, size)] = other_last_ref[...]


def body(section_input, segment_ids, query_weight, keyval_weight, out_weight):
    hidden = section_input[0]
    rows, width = hidden.shape
    device = lax.axis_index("fsdp")
    chips = lax.axis_size("fsdp") // 2
    order = ring_order(chips)
    table = []
    for i in range(2 * chips):
        place = order.index(i // 2)
        table.append([i % 2, i // 2 % 2] + [order[(place + d) % chips] for d in range(chips)])
    scalars = lax.dynamic_index_in_dim(jnp.array(table, jnp.int32), device, 0, keepdims=False)

    keyval = Ring(keyval_weight[0])
    keyval.advance()
    keyval.advance()
    keyval.advance()
    keyval.finish(halved=False)

    half = ((rows, width // 2), jnp.bfloat16)
    own_rows, sent_rows = run(functools.partial(split_kernel, True), [half, half], scalars, [hidden])
    other_rows = swap_cores(sent_rows)

    query_shard, = run(
        copy_kernel, [(query_weight.shape[1:], jnp.bfloat16)], scalars, [query_weight[0]],
        waits=keyval.get(3, chips - 3, chips // 2) + [other_rows],
    )
    kept, sent = run(
        functools.partial(keyval_kernel, list(range(chips))),
        [((2 * rows, 256), jnp.float32), ((2 * rows + 8, 256), jnp.float32)],
        scalars, [segment_ids, own_rows, other_rows] + keyval.get(*range(chips)),
    )
    parcel, = run(
        parcel_kernel, [((2 * rows + MARK_ROWS, 256), jnp.bfloat16)], scalars,
        [segment_ids, kept, swap_cores(sent)],
    )
    def query_sums(distances, g, waits, before=()):
        pieces = [(d, first) for d in distances for first, _ in query.found[d]]
        return run(
            functools.partial(query_kernel, pieces, g, bool(before)),
            [((2 * rows, GROUP_WIDTH), jnp.float32)] * 2, scalars,
            [own_rows, other_rows] + query.get(*distances) + list(before), waits=waits,
        )

    near = [0, 1, chips - 1, 2, chips - 2]
    next_far = [3, chips - 3]
    far = [chips // 2]
    query = Ring(query_shard)
    query.advance(parcel)
    back_two = two_chips_on(parcel)
    out_shard = to_next_section(out_weight[0])
    query.advance(back_two, out_shard)
    sums = [query_sums(near, g, [parcel]) for g in range(2)]
    back_four = two_chips_on(after(back_two, sums[0][0], sums[1][0]))
    query.advance(back_four)
    even = device // 2 % 2 == 0
    crossed = swap_chips(jnp.concatenate([jnp.where(even, parcel, back_four), back_two], axis=0))
    query.finish(halved=True)
    out = Ring(after(out_shard, crossed, *query.get(*far)))
    window = 5 * 2 * rows
    *heads, lowest = run(
        window_kernel,
        [((2, 128, window), jnp.bfloat16)] * 2 + [((2, window, 128), jnp.bfloat16)] * 2
        + [((2 * rows, 128), jnp.int32)],
        scalars, [back_four, back_two, parcel, crossed],
    )
    sums = [query_sums(next_far + far, g, [lowest] + out.get(0), sums[g]) for g in range(2)]
    given = [(lowest, sums[g][0], swap_cores(sums[g][1]), heads[g], heads[2 + g]) for g in range(2)]
    out.advance()
    attended = [attention(0, given[0], [], [])]
    attended[0] = attention(1, given[0], attended[:1], out.get(1, chips - 1))
    out.advance()
    attended.append(attention(0, given[1], [], attended[:1] + out.get(2, chips - 2)))
    attended[1] = attention(1, given[1], attended[1:], [])
    out.advance()
    out.finish(halved=True)
    kept, sent = run(
        functools.partial(split_kernel, False), [half, half], scalars, [to_next_section(hidden)], waits=attended[1:]
    )
    adds = [kept, swap_cores(sent)]
    arrived = []
    for g in range(2):
        mine = to_next_section(attended[g])
        if g:
            mine = after(mine, *out.get(*next_far))
        arrived += [mine, swap_cores(mine)]

    def made(some, mode):
        distances = [(d, [first for first, _ in out.found[d]]) for d in some]
        outs = [((rows, out_shard.shape[1]), jnp.bfloat16)] * 2 if mode == "alone" else [half, half]
        return run(
            functools.partial(out_kernel, distances, mode), outs, scalars, arrived + adds + out.get(*some)
        )

    most = made(near + next_far, "first")
    other_most = swap_cores(most[1])
    last = made(far, "alone")
    joined, = run(
        functools.partial(join_kernel, chips // 2), [((rows, width), jnp.bfloat16)], scalars,
        [most[0], other_most, last[0], swap_cores(last[1])],
    )
    return joined[None]


def solution(mesh):
    return jax.shard_map(
        body,
        mesh=mesh,
        in_specs=(
            P("section", "fsdp", None),
            P("section", "fsdp"),
            P("section", "fsdp", None),
            P("section", "fsdp", None),
            P("section", None, "fsdp"),
        ),
        out_specs=P("section", "fsdp", None),
        check_vma=False,
    )
```
